32 devices in a mesh: dp: 8 (over z, x), pipe: 4 (over y, core).
Axes of the slice: x: 2, y: 2, z: 4, core: 2. Of those that a mesh axis runs over, the one named last changes fastest.
Arguments:
- images: bfloat16 [64, 196, 768], P('dp'), may hold values from -6 to 6
- cotangent: bfloat16 [64, 196, 768], P('dp'), may hold values from -6 to 6
- valid_rows: int32 [64], P('dp'), may hold values from 0 to 1, as said below
- skip_masks: int32 [64, 2], P('dp'), may hold values 0 or 1
- norm_gain: bfloat16 [4, 768], P('pipe'), may hold values from 0.5 to 1.5
- norm_bias: bfloat16 [4, 768], P('pipe'), may hold values from -3 to 3
- token_up: bfloat16 [392, 384], P('pipe'), may hold values from -0.4375 to 0.4375
- token_up_bias: bfloat16 [768], P('pipe'), may hold values from -3 to 3
- token_down: bfloat16 [768, 196], P('pipe'), may hold values from -0.3125 to 0.3125
- token_down_bias: bfloat16 [392], P('pipe'), may hold values from -3 to 3
- chan_up: bfloat16 [1536, 3072], P('pipe'), may hold values from -0.21875 to 0.21875
- chan_up_bias: bfloat16 [6144], P('pipe'), may hold values from -3 to 3
- chan_down: bfloat16 [6144, 768], P('pipe'), may hold values from -0.109375 to 0.109375
- chan_down_bias: bfloat16 [1536], P('pipe'), may hold values from -3 to 3
Outputs:
- mixed: bfloat16 [64, 196, 768], P('dp', None, 'pipe')
- input_grad: bfloat16 [64, 196, 768], P('dp', None, 'pipe')
- norm_gain_grad: float32 [4, 768], P('pipe')
- norm_bias_grad: float32 [4, 768], P('pipe')
- token_up_grad: float32 [392, 384], P('pipe')
- token_up_bias_grad: float32 [768], P('pipe')
- token_down_grad: float32 [768, 196], P('pipe')
- token_down_bias_grad: float32 [392], P('pipe')
- chan_up_grad: float32 [1536, 3072], P('pipe', 'dp')
- chan_up_bias_grad: float32 [6144], P('pipe')
- chan_down_grad: float32 [6144, 768], P('pipe', 'dp')
- chan_down_bias_grad: float32 [1536], P('pipe')
The draws below stay inside these ranges and needn't reach their ends.
Inputs may be any that keep to these rules, and one draw needn't show every extreme that they name: `valid_rows`: each block of 8 consecutive slots (one index of dp) holds 4 or more valid images; in every draw some block has all 8 valid.
All inputs are finite; a program needn't handle non-finite values. No bound on the sum of `skip_masks` on one device may be relied on, other than what follows from the above.
Results may differ from the reference program's by a relative error of at most 0.013.
Values may be sent and summed in bfloat16 or wider, within the bound.
No kernel may reach another device: no remote copies, remote signals or barrier semaphores. Data moves between devices by JAX's collectives and lax.ppermute only.
A program may use at most 256 MiB of HBM per device.

```python
import jax
import jax.numpy as jnp
from jax import lax

D = 768
FF = 3072
TH = 384
P_SIZE = 196
SLOTS = 8
IMAGES = 64


def draw_valid_rows(key, part):
    key = jax.random.fold_in(key, 11)
    count_key, full_key, order_key = jax.random.split(key, 3)
    blocks = IMAGES // SLOTS
    counts_drawn = jax.random.randint(count_key, (blocks,), SLOTS // 2, SLOTS + 1)
    full_block = jax.random.randint(full_key, (), 0, blocks)
    counts_drawn = jnp.where(jnp.arange(blocks) == full_block, SLOTS, counts_drawn)
    order_keys = jax.random.split(order_key, blocks)
    orders = jax.vmap(lambda one_key: jax.random.permutation(one_key, SLOTS))(order_keys)
    return (orders < counts_drawn[:, None]).astype(jnp.int32).reshape(blocks * SLOTS)


def set_ends(entries, key, least, top_value):
    longest = entries.shape.index(max(entries.shape))
    spots = []
    for shift in (0, 1):
        where = [jax.random.randint(jax.random.fold_in(key, axis), (), 0, length) for axis, length in enumerate(entries.shape)]
        where[longest] = (where[longest] + shift) % entries.shape[longest]
        spots.append(tuple(where))
    return entries.at[spots[0]].set(least).at[spots[1]].set(top_value)


def strengthened(entries, stream_key, source, target, blocks, factor):
    def block_of(position):
        return (jnp.arange(entries.shape[position]) // (entries.shape[position] // blocks)).reshape((-1,) + (1,) * (entries.ndim - 1 - position))

    one_side = jax.random.permutation(stream_key, blocks)[block_of(target)]
    second = (block_of(target) + blocks // 2) % blocks
    return jnp.where((block_of(source) == one_side) | (block_of(source) == second), factor * entries, entries)


def block_levels(key, extent, cuts, smallest, largest):
    def one(position, blocks):
        heights = jax.random.uniform(jax.random.fold_in(jax.random.fold_in(key, 6), position), (blocks,), jnp.float32, smallest / len(cuts), largest / len(cuts))
        return jnp.repeat(jnp.exp(heights), extent[position] // blocks).reshape((-1,) + (1,) * (len(extent) - position - 1))

    level = one(*cuts[0])
    for cut in cuts[1:]:
        level = level * one(*cut)
    return level


def bell_draw(own_key, extent, width, bound, shards=(), dtype=jnp.bfloat16):
    entries = jax.random.normal(own_key, extent, jnp.float32) * width
    if len(shards) > 0:
        entries = block_levels(own_key, extent, shards, -0.22, 0.18) * entries
    return jnp.clip(entries, min=-bound, max=bound).astype(dtype)


def bell_draw_with(own_key, extent, spread, bound, shards, heavy, held_as=jnp.bfloat16):
    values = spread * jax.random.normal(own_key, extent, jnp.float32)
    if shards:
        values = values * block_levels(own_key, extent, shards, -0.22, 0.18)
    return jnp.clip(strengthened(values, jax.random.fold_in(own_key, 3), *heavy), -bound, bound).astype(held_as)


def setup_inputs(seed: int = 0) -> dict:
    arg_keys = jax.random.split(jax.random.key(seed), 15)
    return {
        "images": bell_draw(arg_keys[0], (IMAGES, P_SIZE, D), 1.0, 6.0, ((0, 8),)),
        "cotangent": bell_draw_with(arg_keys[1], (IMAGES, P_SIZE, D), 1.0, 6.0, ((0, 8),), (0, 2, 8, 2.0)),
        "valid_rows": draw_valid_rows(jax.random.fold_in(arg_keys[14], 71), 0),
        "skip_masks": set_ends((jax.random.randint(arg_keys[3], (IMAGES, 2), 0, 4) < 3).astype(jnp.int32), jax.random.fold_in(arg_keys[3], 1), 0, 1),
        "norm_gain": jnp.clip(1.0 + 0.1 * jax.random.normal(arg_keys[4], (4, D), jnp.float32), 0.5, 1.5).astype(jnp.bfloat16),
        "norm_bias": bell_draw(arg_keys[5], (4, D), 0.3, 3.0, ((0, 4),)),
        "token_up": bell_draw(arg_keys[6], (2 * P_SIZE, TH), P_SIZE ** -0.5, 0.4375, ((0, 4),)),
        "token_up_bias": bell_draw(arg_keys[7], (2 * TH,), 0.3, 3.0, ((0, 4),)),
        "token_down": bell_draw(arg_keys[8], (2 * TH, P_SIZE), TH ** -0.5, 0.3125, ((0, 4),)),
        "token_down_bias": bell_draw(arg_keys[9], (2 * P_SIZE,), 0.3, 3.0, ((0, 4),)),
        "chan_up": bell_draw(arg_keys[10], (2 * D, FF), D ** -0.5, 0.21875, ((0, 4),)),
        "chan_up_bias": bell_draw(arg_keys[11], (2 * FF,), 0.3, 3.0, ((0, 4),)),
        "chan_down": bell_draw(arg_keys[12], (2 * FF, D), FF ** -0.5, 0.109375, ((0, 4),)),
        "chan_down_bias": bell_draw(arg_keys[13], (2 * D,), 0.3, 3.0, ((0, 4),)),
    }


NORM_EPS = 1e-06

@jax.custom_vjp
def low(v):
    return lax.optimization_barrier(v.astype(jnp.bfloat16)).astype(jnp.float32)

@jax.custom_vjp
def low_back(v):
    return v

def low_keep(v):
    return (low(v), None)

def low_pass(kept, grad):
    return (grad,)

def back_keep(v):
    return (v, None)

def back_low(kept, grad):
    return (low(grad),)
low.defvjp(low_keep, low_pass)
low_back.defvjp(back_keep, back_low)

def norm_rows(hidden, gain_row, shift_row):
    row_mean = lax.optimization_barrier(jnp.mean(hidden, axis=-1, keepdims=True))
    centred = hidden - row_mean
    row_scale = lax.rsqrt(lax.optimization_barrier(jnp.mean(centred * centred, axis=-1, keepdims=True)) + NORM_EPS)
    return centred * row_scale * gain_row + shift_row

def token_branch(hidden, gain_row, shift_row, w_up, bias_up, w_down, bias_down):
    normed = low(norm_rows(hidden, gain_row, shift_row))
    pre_act = low_back(jnp.einsum('bpd,pt->bdt', normed, w_up, precision=lax.Precision.HIGHEST) + bias_up)
    activated = low(jax.nn.gelu(pre_act, approximate=True))
    mixed_rows = jnp.einsum('bdt,tp->bpd', activated, w_down, precision=lax.Precision.HIGHEST)
    return low_back(mixed_rows + bias_down[None, :, None])

def chan_branch(hidden, gain_row, shift_row, w_up, bias_up, w_down, bias_down):
    normed = low(norm_rows(hidden, gain_row, shift_row))
    pre_act = low_back(jnp.einsum('bpd,df->bpf', normed, w_up, precision=lax.Precision.HIGHEST) + bias_up)
    activated = low(jax.nn.gelu(pre_act, approximate=True))
    mixed_rows = jnp.einsum('bpf,fd->bpd', activated, w_down, precision=lax.Precision.HIGHEST)
    return low_back(mixed_rows + bias_down)

def boundary(values_in):
    return low_back(low(values_in))

def forward(hidden, skip_rows, valid_f, param_set):
    gains, shifts, t_up, t_ub, t_down, t_db, c_up, c_ub, c_down, c_db = param_set
    for layer_index in range(2):
        gate_rows = skip_rows[:, layer_index][:, None, None]
        token_part = token_branch(hidden, gains[2 * layer_index], shifts[2 * layer_index], t_up[layer_index * P_SIZE:(layer_index + 1) * P_SIZE], t_ub[layer_index * TH:(layer_index + 1) * TH], t_down[layer_index * TH:(layer_index + 1) * TH], t_db[layer_index * P_SIZE:(layer_index + 1) * P_SIZE])
        hidden = boundary(hidden + gate_rows * token_part)
        chan_part = chan_branch(hidden, gains[2 * layer_index + 1], shifts[2 * layer_index + 1], c_up[layer_index * D:(layer_index + 1) * D], c_ub[layer_index * FF:(layer_index + 1) * FF], c_down[layer_index * FF:(layer_index + 1) * FF], c_db[layer_index * D:(layer_index + 1) * D])
        hidden = hidden + gate_rows * chan_part
        if layer_index == 0:
            hidden = boundary(hidden)
    return low(valid_f[:, None, None] * hidden)

def reference(images, cotangent, valid_rows, skip_masks, norm_gain, norm_bias, token_up, token_up_bias, token_down, token_down_bias, chan_up, chan_up_bias, chan_down, chan_down_bias):
    params = tuple((array.astype(jnp.float32) for array in (norm_gain, norm_bias, token_up, token_up_bias, token_down, token_down_bias, chan_up, chan_up_bias, chan_down, chan_down_bias)))
    groups = IMAGES // SLOTS
    image_groups = images.astype(jnp.float32).reshape(groups, SLOTS, P_SIZE, D)
    cot_groups = cotangent.astype(jnp.float32).reshape(groups, SLOTS, P_SIZE, D)
    valid_groups = valid_rows.astype(jnp.float32).reshape(groups, SLOTS)
    skip_groups = skip_masks.astype(jnp.float32).reshape(groups, SLOTS, 2)

    def group_step(running, group_block):
        image_block, cot_block, valid_block, skip_block = group_block
        group_out, pullback = jax.vjp(lambda hidden, param_set: forward(hidden, skip_block, valid_block, param_set), image_block, params)
        grad_images, grad_params = pullback(cot_block)
        running = jax.tree.map(jnp.add, running, grad_params)
        return (running, (group_out, grad_images))
    zero_grads = jax.tree.map(jnp.zeros_like, params)
    running, (group_outs, grad_groups) = lax.scan(group_step, zero_grads, (image_groups, cot_groups, valid_groups, skip_groups))
    mixed = group_outs.reshape(IMAGES, P_SIZE, D).astype(jnp.bfloat16)
    input_grad = grad_groups.reshape(IMAGES, P_SIZE, D).astype(jnp.bfloat16)
    return (mixed, input_grad, running[0], running[1], running[2], running[3], running[4], running[5], running[6], running[7], running[8], running[9])
```

```python
import functools

import jax
import jax.numpy as jnp
from jax import lax
from jax.experimental import pallas as pl
from jax.experimental.pallas import tpu as pltpu
from jax.sharding import PartitionSpec as P

F32 = jnp.float32
BF16 = jnp.bfloat16
NORM_EPS = 1e-06
GELU_SCALE = 0.7978845608
GELU_CUBE = 0.044715
STEPS = 6
SLOTS = 4
VMEM_BYTES = 26 << 20

IN_VMEM = pl.BlockSpec(memory_space=pltpu.VMEM)
IN_ANY = pl.BlockSpec(memory_space=pl.ANY)
IN_SMEM = pl.BlockSpec(memory_space=pltpu.SMEM)

ON, VALID, CROSSING, IMAGE, OTHER = range(5)


def flipped(block, axis, distance):
    count = lax.axis_size(axis)
    route = [(i, i ^ distance) for i in range(count) if i ^ distance < count]
    return lax.ppermute(block, axis, route)


def mm(left, right):
    return lax.dot_general(left, right, (((1,), (0,)), ((), ())), preferred_element_type=F32)


def mm_nt(left, right):
    return lax.dot_general(left, right, (((1,), (1,)), ((), ())), preferred_element_type=F32)


def mm_tn(left, right):
    return lax.dot_general(left, right, (((0,), (0,)), ((), ())), preferred_element_type=F32)


def gelu_pair(pre):
    square = pre * pre
    gate = 0.5 + 0.5 * jnp.tanh(pre * (GELU_SCALE + (GELU_SCALE * GELU_CUBE) * square))
    value = pre * gate
    slope = gate + value * (1.0 - gate) * (2 * GELU_SCALE + (6 * GELU_SCALE * GELU_CUBE) * square)
    return value, slope


def normalised(hidden):
    centred = hidden - jnp.mean(hidden, axis=-1, keepdims=True)
    scale = lax.rsqrt(jnp.mean(centred * centred, axis=-1, keepdims=True) + NORM_EPS)
    return centred * scale, scale


def forward_body(near_slot, far_slot, tab, images, recv, up, down, up_t, down_t, up_col, down_col, u_row, w_row, gains, shifts,
                 send_o, res_o, z_o, gz_o, zt_o, gt_o, h0_o, h1_o, n2_o,
                 x_v, z_v, gz_v, zt_v, gt_v, h1_v, n2_v, h2_v, x_sem, s_sem, o_sems):
    far = tab[5, 0] == 1
    job = jnp.where(far, far_slot, near_slot)
    slot = jnp.maximum(job, 0)
    has_job = job >= 0
    on = has_job & (tab[ON, slot] == 1)
    from_recv = far & (tab[CROSSING, slot] == 1)

    @pl.when(has_job & from_recv)
    def _():
        pltpu.make_async_copy(recv, x_v, x_sem).start()

    @pl.when(has_job & jnp.logical_not(from_recv))
    def _():
        pltpu.make_async_copy(images.at[tab[IMAGE, slot]], x_v, x_sem).start()

    @pl.when(has_job)
    def _():
        pltpu.make_async_copy(recv, x_v, x_sem).wait()

    def deliver():
        copy = pltpu.make_async_copy(h2_v, res_o.at[slot], x_sem)
        copy.start()

        @pl.when(jnp.logical_not(far))
        def _():
            sent = pltpu.make_async_copy(h2_v, send_o, s_sem)
            sent.start()
            sent.wait()

        copy.wait()

    @pl.when(has_job & jnp.logical_not(on))
    def _():
        h2_v[...] = x_v[...] * tab[VALID, slot].astype(F32).astype(BF16)
        deliver()

    @pl.when(on)
    def _():
        started = []

        def put(source, target):
            copy = pltpu.make_async_copy(source, target.at[slot], o_sems.at[len(started)])
            copy.start()
            started.append(copy)

        put(x_v, h0_o)
        h0 = x_v[...].astype(F32)
        centred, _ = normalised(h0)
        n1 = (centred * gains[0:1, :] + shifts[0:1, :]).astype(BF16)
        value, slope = gelu_pair(mm(up_t[...], n1) + up_col[...])
        value = value.astype(BF16)
        zt_v[...] = value
        gt_v[...] = slope.astype(BF16)
        put(zt_v, zt_o)
        put(gt_v, gt_o)
        h1 = (h0 + (mm(down_t[...], value) + down_col[...])).astype(BF16)
        h1_v[...] = h1
        put(h1_v, h1_o)
        h1 = h1.astype(F32)
        centred, _ = normalised(h1)
        n2_v[...] = (centred * gains[1:2, :] + shifts[1:2, :]).astype(BF16)
        put(n2_v, n2_o)
        total = h1 + w_row[...]
        width = up.shape[1] // STEPS
        for step in range(STEPS):
            cols = slice(step * width, (step + 1) * width)
            value, slope = gelu_pair(mm(n2_v[...], up[:, cols]) + u_row[:, cols])
            value = value.astype(BF16)
            z_v[:, cols] = value
            gz_v[:, cols] = slope.astype(BF16)
            total = total + mm(value, down[cols, :])
        put(z_v, z_o)
        put(gz_v, gz_o)
        h2_v[...] = total.astype(BF16)
        deliver()
        for copy in started:
            copy.wait()


def backward_body(near_slot, far_slot, tab, cots, recv, up, down, up_w, down_w, gains, shifts, gz_i, zt_i, gt_i, h0_i, h1_i,
                  send_o, res_o, f_o, dq_o, da_o, db_o, vec_o,
                  e_v, gz_v, zt_v, gt_v, h0_v, h1_v, f_v, dq_v, da_v, db_v, vec_v, e_sem, s_sem, i_sems, o_sems):
    far = tab[5, 0] == 1
    job = jnp.where(far, far_slot, tab[5, 3] if near_slot is None else near_slot)
    slot = jnp.maximum(job, 0)
    has_job = job >= 0
    on = has_job & (tab[ON, slot] == 1)
    from_recv = jnp.logical_not(far) & (tab[CROSSING, slot] == 1)
    channels = up.shape[0]
    rows = e_v.shape[0]
    hidden_t = zt_v.shape[0]
    saved = ((gz_i, gz_v), (h1_i, h1_v), (gt_i, gt_v), (h0_i, h0_v), (zt_i, zt_v))

    def load(i):
        return pltpu.make_async_copy(saved[i][0].at[slot], saved[i][1], i_sems.at[i])

    @pl.when(has_job & from_recv)
    def _():
        pltpu.make_async_copy(recv, e_v, e_sem).start()

    @pl.when(has_job & jnp.logical_not(from_recv))
    def _():
        pltpu.make_async_copy(cots.at[tab[IMAGE, slot]], e_v, e_sem).start()

    @pl.when(on)
    def _():
        for i in range(5):
            load(i).start()

    @pl.when(has_job)
    def _():
        pltpu.make_async_copy(recv, e_v, e_sem).wait()

    def deliver(source):
        copy = pltpu.make_async_copy(source, res_o.at[slot], e_sem)
        copy.start()

        @pl.when(far)
        def _():
            sent = pltpu.make_async_copy(source, send_o, s_sem)
            sent.start()
            sent.wait()

        copy.wait()

    @pl.when(has_job & jnp.logical_not(on))
    def _():
        f_v[...] = e_v[...] * tab[VALID, slot].astype(F32).astype(BF16)
        deliver(f_v)

    @pl.when(on)
    def _():
        started = []

        def put(source, target):
            copy = pltpu.make_async_copy(source, target.at[slot], o_sems.at[len(started)])
            copy.start()
            started.append(copy)

        put(e_v, f_o)
        grad = e_v[...].astype(F32)
        vec_v[...] = jnp.zeros_like(vec_v)
        vec_v[1:2, 0:channels] = jnp.sum(grad, axis=0, keepdims=True)
        dn = jnp.zeros((rows, channels), F32)
        width = up.shape[1] // STEPS
        load(0).wait()
        for step in range(STEPS):
            cols = slice(step * width, (step + 1) * width)
            dq = (mm_nt(e_v[...], down[cols, :]) * gz_v[:, cols].astype(F32)).astype(BF16)
            dq_v[:, cols] = dq
            vec_v[0:1, cols] = jnp.sum(dq.astype(F32), axis=0, keepdims=True)
            dn = dn + mm_nt(dq, up[:, cols])
        put(dq_v, dq_o)

        def norm_back(hidden, dn, grad, row):
            centred, scale = normalised(hidden)
            vec_v[2 + row:3 + row, 0:channels] = jnp.sum(dn * centred, axis=0, keepdims=True)
            vec_v[4 + row:5 + row, 0:channels] = jnp.sum(dn, axis=0, keepdims=True)
            scaled = dn * gains[row:row + 1, :]
            along = jnp.mean(scaled * centred, axis=-1, keepdims=True)
            flat = jnp.mean(scaled, axis=-1, keepdims=True)
            return centred, grad + scale * (scaled - flat - centred * along)

        load(1).wait()
        _, grad = norm_back(h1_v[...].astype(F32), dn, grad, 1)
        f1 = grad.astype(BF16)
        grad = f1.astype(F32)
        load(2).wait()
        dq = (mm(down_w[...], f1) * gt_v[...].astype(F32)).astype(BF16)
        load(3).wait()
        centred, grad = norm_back(h0_v[...].astype(F32), mm(up_w[...], dq), grad, 0)
        f_v[...] = grad.astype(BF16)
        n1 = (centred * gains[0:1, :] + shifts[0:1, :]).astype(BF16)
        load(4).wait()
        da_v[...] = mm_nt(n1, dq)
        db_v[...] = mm_nt(zt_v[...], f1)
        ones = jnp.ones((8, channels), BF16)
        vec_v[6:7, 0:hidden_t] = mm_nt(ones, dq)[0:1]
        vec_v[7:8, 0:rows] = mm_nt(ones, f1)[0:1]
        put(da_v, da_o)
        put(db_v, db_o)
        put(vec_v, vec_o)
        deliver(f_v)
        for copy in started:
            copy.wait()


def kept_call(body, ins, specs, kept, shapes, scratch, cost, name):
    aliases = {}
    passed = 0
    for position, array in enumerate(kept):
        if array is not None:
            aliases[len(ins) + passed] = position
            passed += 1
    first = len(ins)

    def trimmed(*refs):
        body(*refs[:first], *refs[first + passed:])

    return pl.pallas_call(
        trimmed,
        out_shape=shapes,
        in_specs=specs + [IN_ANY] * passed,
        out_specs=[IN_ANY] * len(shapes),
        input_output_aliases=aliases,
        scratch_shapes=scratch,
        compiler_params=pltpu.CompilerParams(vmem_limit_bytes=VMEM_BYTES),
        cost_estimate=cost,
        name=name,
    )(*ins, *[array for array in kept if array is not None])


def forward_call(slots, tab, images, recv, w, kept):
    rows, channels = recv.shape
    ff = w["up"].shape[1]
    hidden_t = w["up_t"].shape[0]
    shape = jax.ShapeDtypeStruct
    shapes = [shape((rows, channels), BF16), shape((SLOTS, rows, channels), BF16),
              shape((SLOTS, rows, ff), BF16), shape((SLOTS, rows, ff), BF16),
              shape((SLOTS, hidden_t, channels), BF16), shape((SLOTS, hidden_t, channels), BF16),
              shape((SLOTS, rows, channels), BF16), shape((SLOTS, rows, channels), BF16),
              shape((SLOTS, rows, channels), BF16)]
    ins = [tab, images, recv] + [w[k] for k in ("up", "down", "up_t", "down_t", "up_col", "down_col", "u_row", "w_row", "gains", "shifts")]
    scratch = [pltpu.VMEM((rows, channels), BF16), pltpu.VMEM((rows, ff), BF16), pltpu.VMEM((rows, ff), BF16),
               pltpu.VMEM((hidden_t, channels), BF16), pltpu.VMEM((hidden_t, channels), BF16),
               pltpu.VMEM((rows, channels), BF16), pltpu.VMEM((rows, channels), BF16), pltpu.VMEM((rows, channels), BF16),
               pltpu.SemaphoreType.DMA, pltpu.SemaphoreType.DMA, pltpu.SemaphoreType.DMA((7,))]
    cost = pl.CostEstimate(flops=4 * rows * channels * (ff + hidden_t), bytes_accessed=8 * rows * ff, transcendentals=rows * ff)
    return kept_call(functools.partial(forward_body, *slots), ins, [IN_SMEM, IN_ANY, IN_ANY] + [IN_VMEM] * 10,
                     kept, shapes, scratch, cost, "forward_slot")


def backward_call(slots, tab, cots, recv, w, saved, kept):
    rows, channels = recv.shape
    ff = w["up"].shape[1]
    hidden_t = w["up_t"].shape[0]
    shape = jax.ShapeDtypeStruct
    shapes = [shape((rows, channels), BF16), shape((SLOTS, rows, channels), BF16),
              shape((SLOTS, rows, channels), BF16), shape((SLOTS, rows, ff), BF16),
              shape((SLOTS, rows, hidden_t), F32), shape((SLOTS, hidden_t, rows), F32), shape((SLOTS, 8, ff), F32)]
    ins = [tab, cots, recv] + [w[k] for k in ("up", "down", "up_w", "down_w", "gains", "shifts")] + list(saved)
    scratch = [pltpu.VMEM((rows, channels), BF16), pltpu.VMEM((rows, ff), BF16),
               pltpu.VMEM((hidden_t, channels), BF16), pltpu.VMEM((hidden_t, channels), BF16),
               pltpu.VMEM((rows, channels), BF16), pltpu.VMEM((rows, channels), BF16), pltpu.VMEM((rows, channels), BF16),
               pltpu.VMEM((rows, ff), BF16), pltpu.VMEM((rows, hidden_t), F32), pltpu.VMEM((hidden_t, rows), F32), pltpu.VMEM((8, ff), F32),
               pltpu.SemaphoreType.DMA, pltpu.SemaphoreType.DMA, pltpu.SemaphoreType.DMA((5,)), pltpu.SemaphoreType.DMA((5,))]
    cost = pl.CostEstimate(flops=4 * rows * channels * (ff + 2 * hidden_t), bytes_accessed=8 * rows * ff, transcendentals=0)
    return kept_call(functools.partial(backward_body, *slots), ins, [IN_SMEM, IN_ANY, IN_ANY] + [IN_VMEM] * 6 + [IN_ANY] * 5,
                     kept, shapes, scratch, cost, "backward_slot")


def down_grad_body(chunk, count, aligned, tab, f_i, recv, cots, z_i, out, f_v, z_v, f_sems, z_sems):
    half = tab[5, 1]
    me = tab[5, 2]
    late = tab[5, 3]
    width = out.shape[-1]
    channels = f_i.shape[2]
    rows = f_i.shape[1]
    size = z_i.shape[2] // 2

    def copies(slot, side):
        first = pl.multiple_of(jnp.where(side == 0, 1 - half, half) * size + chunk * width, 128)
        return pltpu.make_async_copy(z_i.at[slot, :, pl.ds(first, width)], z_v.at[side, pl.ds(slot * rows, rows), :], z_sems.at[side, slot])

    def f_copy(slot, source):
        return pltpu.make_async_copy(source, f_v.at[pl.ds(slot * rows, rows), :], f_sems.at[slot])

    for slot in range(SLOTS):
        on = tab[ON, slot] == 1

        crossed = tab[CROSSING, slot] == 1

        @pl.when(on & (late == slot) & crossed)
        def _():
            f_copy(slot, recv).start()

        @pl.when(on & (late == slot) & jnp.logical_not(crossed))
        def _():
            f_copy(slot, cots.at[tab[IMAGE, slot]]).start()

        @pl.when(on & (late != slot))
        def _():
            f_copy(slot, f_i.at[slot]).start()

        @pl.when(on)
        def _():
            for side in range(2):
                copies(slot, side).start()

        @pl.when(jnp.logical_not(on))
        def _():
            f_v[pl.ds(slot * rows, rows), :] = jnp.zeros((rows, channels), BF16)
            for side in range(2):
                z_v[side, pl.ds(slot * rows, rows), :] = jnp.zeros((rows, width), BF16)

    for slot in range(SLOTS):
        @pl.when(tab[ON, slot] == 1)
        def _():
            f_copy(slot, recv).wait()
            for side in range(2):
                copies(slot, side).wait()

    f_t = f_v[...].T
    piece = channels // count
    for side in range(2):
        total = mm(f_t, z_v[side]).astype(BF16)
        if aligned:
            for d in range(count):
                out[side, d ^ me] = total[d * piece:(d + 1) * piece]
        else:
            out[side] = total


def up_grad_body(chunk, count, aligned, tab, n_i, dq_i, out, n_v, dq_v, n_sems, dq_sems):
    half = tab[5, 1]
    me = tab[5, 2]
    height = out.shape[-2]
    rows = n_i.shape[1]
    size = n_i.shape[2] // 2
    ff = dq_i.shape[2]

    def n_copy(slot):
        return pltpu.make_async_copy(n_i.at[slot], n_v.at[pl.ds(slot * rows, rows), :], n_sems.at[slot])

    def dq_copy(slot):
        return pltpu.make_async_copy(dq_i.at[slot], dq_v.at[pl.ds(slot * rows, rows), :], dq_sems.at[slot])

    for slot in range(SLOTS):
        on = tab[ON, slot] == 1

        @pl.when(on)
        def _():
            n_copy(slot).start()
            dq_copy(slot).start()

        @pl.when(jnp.logical_not(on))
        def _():
            n_v[pl.ds(slot * rows, rows), :] = jnp.zeros((rows, 2 * size), BF16)
            dq_v[pl.ds(slot * rows, rows), :] = jnp.zeros((rows, ff), BF16)

    for slot in range(SLOTS):
        @pl.when(tab[ON, slot] == 1)
        def _():
            n_copy(slot).wait()
            dq_copy(slot).wait()

    piece = ff // count
    for fixed in range(2):
        first = fixed * size + chunk * height
        n_t = n_v[:, first - first % 128:first + height].astype(F32).T[first % 128:].astype(BF16)
        side = jnp.where(half == fixed, 1, 0)
        if aligned:
            for d in range(count):
                out[side, d ^ me] = mm(n_t, dq_v[:, d * piece:(d + 1) * piece]).astype(BF16)
        else:
            out[side] = mm(n_t, dq_v[...]).astype(BF16)


def down_grad_call(chunk, chunks, count, tab, f, recv, cots, z):
    slots, rows, channels = f.shape
    width = z.shape[2] // 2 // chunks
    piece = channels // count
    aligned = piece % 16 == 0
    shape = (2, count, piece, width) if aligned else (2, channels, width)
    out = pl.pallas_call(
        functools.partial(down_grad_body, chunk, count, aligned),
        out_shape=jax.ShapeDtypeStruct(shape, BF16),
        in_specs=[IN_SMEM] + [IN_ANY] * 4,
        out_specs=IN_VMEM,
        scratch_shapes=[pltpu.VMEM((slots * rows, channels), BF16), pltpu.VMEM((2, slots * rows, width), BF16),
                        pltpu.SemaphoreType.DMA((slots,)), pltpu.SemaphoreType.DMA((2, slots))],
        compiler_params=pltpu.CompilerParams(vmem_limit_bytes=VMEM_BYTES),
        cost_estimate=pl.CostEstimate(flops=4 * slots * rows * channels * width, bytes_accessed=8 * channels * width, transcendentals=0),
        name="down_grad",
    )(tab, f, recv, cots, z)
    if not aligned:
        out = out.reshape(2, count, piece, width)[:, jnp.arange(count) ^ lax.axis_index("dp")]
    return out


def up_grad_call(chunk, chunks, count, tab, n, dq):
    slots, rows, channels = n.shape
    ff = dq.shape[2]
    height = channels // 2 // chunks
    piece = ff // count
    aligned = piece % 128 == 0
    shape = (2, count, height, piece) if aligned else (2, height, ff)
    out = pl.pallas_call(
        functools.partial(up_grad_body, chunk, count, aligned),
        out_shape=jax.ShapeDtypeStruct(shape, BF16),
        in_specs=[IN_SMEM] + [IN_ANY] * 2,
        out_specs=IN_VMEM,
        scratch_shapes=[pltpu.VMEM((slots * rows, channels), BF16), pltpu.VMEM((slots * rows, ff), BF16),
                        pltpu.SemaphoreType.DMA((slots,)), pltpu.SemaphoreType.DMA((slots,))],
        compiler_params=pltpu.CompilerParams(vmem_limit_bytes=VMEM_BYTES),
        cost_estimate=pl.CostEstimate(flops=4 * slots * rows * height * ff, bytes_accessed=8 * height * ff, transcendentals=0),
        name="up_grad",
    )(tab, n, dq)
    if not aligned:
        out = jnp.swapaxes(out.reshape(2, height, count, piece), 1, 2)[:, jnp.arange(count) ^ lax.axis_index("dp")]
    return out


def summed_pieces(pair, bits):
    other, mine = pair[0], pair[1]
    got = flipped(other, "pipe", 1)
    depth = len(bits)
    split = (2,) * depth + mine.shape[1:]
    mine = mine.reshape(split)
    got = got.reshape(split)
    axes = list(range(depth))[::-1]
    for bit in bits:
        axis = axes.index(bit)
        keep = [lax.index_in_dim(a, 0, axis, False) for a in (mine, got)]
        send = [lax.index_in_dim(a, 1, axis, False) for a in (mine, got)]
        sent = (send[0].astype(F32) + send[1].astype(F32)).astype(BF16)
        got = flipped(sent, "dp", 1 << bit)
        mine = (keep[0].astype(F32) + keep[1].astype(F32)).astype(BF16)
        axes.remove(bit)
    return mine.astype(F32) + got.astype(F32)


def join_body(half_ref, mine_up, got_up, mine_down, got_down, up_o, down_o, sems):
    half = half_ref[5, 1]
    copies = []
    for i, (mine, got, target) in enumerate(((mine_up, got_up, up_o), (mine_down, got_down, down_o))):
        size = mine.shape[0]
        own = pl.multiple_of(half * size, 16)
        rest = pl.multiple_of((1 - half) * size, 16)
        copies.append(pltpu.make_async_copy(mine, target.at[pl.ds(own, size), :], sems.at[i, 0]))
        copies.append(pltpu.make_async_copy(got, target.at[pl.ds(rest, size), :], sems.at[i, 1]))
    for copy in copies:
        copy.start()
    for copy in copies:
        copy.wait()


def place_body(route, low, high, mixed_o, grad_o, mixed_v, grad_v, sems):
    slots = low.shape[2]
    reads = []
    for place in range(2 * slots):
        source = (low, high)[place % 2]
        for kind, buffer in enumerate((mixed_v, grad_v)):
            image = route[2, place]
            copy = pltpu.make_async_copy(source.at[route[kind, place], kind, place // 2], buffer.at[image], sems.at[kind, place])
            copy.start()
            reads.append(copy)
    for copy in reads:
        copy.wait()
    writes = [pltpu.make_async_copy(mixed_v, mixed_o, sems.at[0, 0]), pltpu.make_async_copy(grad_v, grad_o, sems.at[1, 0])]
    for copy in writes:
        copy.start()
    for copy in writes:
        copy.wait()


def local(images, cotangent, valid_rows, skip_masks, norm_gain, norm_bias, token_up, token_up_bias, token_down,
          token_down_bias, chan_up, chan_up_bias, chan_down, chan_down_bias):
    count = lax.axis_size("dp")
    me = lax.axis_index("dp")
    section = lax.axis_index("pipe")
    half = section % 2
    layer = section // 2
    is_far = layer == 1
    is_first = half == 0
    patches = images.shape[1]
    channels = images.shape[2]
    rows = -(-patches // 16) * 16
    hidden_t = token_up.shape[1]

    own = (chan_up, chan_down, token_up, token_up_bias, token_down, token_down_bias, chan_up_bias, chan_down_bias, norm_gain, norm_bias)
    got = tuple(flipped(part, "pipe", 1) for part in own)

    def joined(i):
        return jnp.concatenate([jnp.where(is_first, own[i], got[i]), jnp.where(is_first, got[i], own[i])], 0)

    first_on = skip_masks[:, 0] * valid_rows
    second_on = skip_masks[:, 1] * valid_rows
    rank_class = jnp.where(first_on * second_on == 1, 0, jnp.where(second_on == 1, 1, jnp.where(first_on == 1, 2, 3)))
    slots_all = rank_class.shape[0]
    numbers = jnp.arange(slots_all)
    key = rank_class * slots_all + numbers
    place = jnp.sum(key[None, :] < key[:, None], axis=1)
    order = jnp.sum(jnp.where(place[None, :] == numbers[:, None], numbers[None, :], 0), axis=1).astype(jnp.int32)
    crossing = jnp.sum(first_on * second_on)
    hops = (crossing + 1) // 2

    own_order = jnp.where(is_first, order[0::2], order[1::2])
    first_here = first_on[own_order]
    second_here = second_on[own_order]
    valid_here = valid_rows[own_order]
    on_here = jnp.where(is_far, second_here, first_here)
    late = jnp.where(is_far, -1, hops - 1)
    tab = jnp.stack([on_here, valid_here, first_here * second_here, own_order, jnp.zeros_like(own_order),
                     jnp.stack([layer, half, me, late])]).astype(jnp.int32)

    up, down = pl.pallas_call(
        join_body,
        out_shape=[jax.ShapeDtypeStruct((2 * chan_up.shape[0], chan_up.shape[1]), BF16),
                   jax.ShapeDtypeStruct((2 * chan_down.shape[0], chan_down.shape[1]), BF16)],
        in_specs=[IN_SMEM] + [IN_ANY] * 4,
        out_specs=[IN_VMEM] * 2,
        scratch_shapes=[pltpu.SemaphoreType.DMA((2, 2))],
        compiler_params=pltpu.CompilerParams(vmem_limit_bytes=VMEM_BYTES),
        name="join",
    )(tab, chan_up, got[0], chan_down, got[1])

    def padded(array, axis):
        extra = [(0, 0)] * array.ndim
        extra[axis] = (0, rows - patches)
        return jnp.pad(array, extra)

    up_w = padded(joined(2), 0)
    down_w = padded(joined(4), 1)
    weights = {
        "up": up, "down": down,
        "up_w": up_w, "down_w": down_w,
        "up_t": up_w.T, "down_t": down_w.T,
        "up_col": joined(3).astype(F32)[:, None],
        "down_col": padded(joined(5).astype(F32), 0)[:, None],
        "u_row": joined(6).astype(F32)[None, :],
        "w_row": joined(7).astype(F32)[None, :],
        "gains": joined(8).astype(F32),
        "shifts": joined(9).astype(F32),
    }
    images_p = padded(images, 1)
    cots_p = padded(cotangent, 1)
    blank = images_p[0]

    def relay(length):
        def run(images_p, cots_p, tab, weights, blank):
            kept_f = [None] * 9
            kept_b = [None] * 7

            def forward(near, far, recv):
                out = forward_call((near, far), tab, images_p, recv, weights, kept_f)
                kept_f[:] = out
                kept_b[0] = out[0]

            def backward(near, far, recv):
                saved = (kept_f[3], kept_f[4], kept_f[5], kept_f[6], kept_f[7])
                out = backward_call((near, far), tab, cots_p, recv, weights, saved, kept_b)
                kept_b[:] = out
                kept_f[0] = out[0]

            def exchange():
                return flipped(kept_f[0], "pipe", 2)

            none = -1
            if length == 0:
                last = blank
                for slot in range(SLOTS):
                    forward(slot, slot, blank)
                    backward(slot, slot, blank)
            elif length == 1:
                forward(0, none, blank)
                x1 = exchange()
                forward(1, 1, blank)
                backward(1, 1, blank)
                forward(2, 0, x1)
                backward(2, 0, x1)
                x3 = exchange()
                forward(3, 2, blank)
                backward(3, 2, blank)
                forward(none, 3, blank)
                backward(none, 3, blank)
                last = x3
            elif length == 2:
                forward(0, none, blank)
                x1 = exchange()
                forward(1, 2, blank)
                backward(none, 2, blank)
                x2 = exchange()
                forward(2, 0, x1)
                backward(2, 0, x1)
                x3 = exchange()
                forward(3, 1, x2)
                backward(3, 1, x2)
                x4 = exchange()
                forward(none, 3, x3)
                backward(0, 3, x3)
                last = x4
            elif length == 3:
                forward(0, none, blank)
                x1 = exchange()
                forward(1, 3, blank)
                backward(none, 3, blank)
                x2 = exchange()
                forward(2, 0, x1)
                backward(none, 0, x1)
                x3 = exchange()
                forward(3, 1, x2)
                backward(3, 1, x2)
                x4 = exchange()
                forward(none, 2, x3)
                backward(0, 2, x3)
                x5 = exchange()
                backward(1, none, x4)
                last = x5
            else:
                forward(0, none, blank)
                x1 = exchange()
                forward(1, none, blank)
                x2 = exchange()
                forward(2, 0, x1)
                backward(none, 0, x1)
                x3 = exchange()
                forward(3, 1, x2)
                backward(none, 1, x2)
                x4 = exchange()
                forward(none, 2, x3)
                backward(0, 2, x3)
                x5 = exchange()
                forward(none, 3, x4)
                backward(1, 3, x4)
                x6 = exchange()
                backward(2, none, x5)
                last = x6
            return last, tuple(kept_f), tuple(kept_b)

        return run

    last, kept_f, kept_b = lax.switch(hops, [relay(n) for n in range(SLOTS + 1)], images_p, cots_p, tab, weights, blank)

    chunks = 2
    bits = list(range(count.bit_length() - 1))
    swapped_bits = [bits[1], bits[0]] + bits[2:]
    down_parts = [down_grad_call(chunk, chunks, count, tab, kept_b[2], last, cots_p, kept_f[2]) for chunk in range(chunks)]
    saved = (kept_f[3], kept_f[4], kept_f[5], kept_f[6], kept_f[7])
    kept_b = backward_call((None, -1), tab, cots_p, last, weights, saved, kept_b)
    up_parts = [up_grad_call(chunk, chunks, count, tab, kept_f[8], kept_b[3]) for chunk in range(chunks)]

    down_sums = [summed_pieces(part, swapped_bits if i == 0 else bits) for i, part in enumerate(down_parts)]
    up_sums = [summed_pieces(part, bits) for part in up_parts]
    chan_down_grad = jnp.concatenate([part.T for part in down_sums], 0)
    chan_up_grad = jnp.concatenate(up_sums, 0)

    live = (tab[ON] == 1)[:, None, None]
    da, db, vec = (jnp.sum(jnp.where(live, part, 0.0), axis=0) for part in kept_b[4:7])

    def halves(array):
        size = array.shape[0] // 2
        low, high = array[:size], array[size:]
        return jnp.where(is_first, low, high).reshape(-1), jnp.where(is_first, high, low).reshape(-1)

    ff = vec.shape[1]
    small = [halves(da[:patches]), halves(db[:, :patches]), halves(vec[6, :hidden_t]), halves(vec[7, :patches]),
             halves(vec[0]), halves(vec[1, :channels]), halves(vec[2:4, :channels]), halves(vec[4:6, :channels])]
    sizes = [pair[0].shape[0] for pair in small]
    padding = -sum(sizes) % 1024
    mine = jnp.concatenate([pair[0] for pair in small] + [jnp.zeros((padding,), F32)])
    theirs = jnp.concatenate([pair[1] for pair in small] + [jnp.zeros((padding,), F32)]).astype(BF16)
    total = mine + flipped(theirs, "pipe", 1).astype(F32)
    for bit in bits:
        sent = lax.optimization_barrier(total.astype(BF16))
        total = sent.astype(F32) + flipped(sent, "dp", 1 << bit).astype(F32)
    pieces = []
    start = 0
    for size in sizes:
        pieces.append(total[start:start + size])
        start += size

    width = channels // lax.axis_size("pipe")
    result = jnp.stack([kept_f[1], kept_b[1]])[:, :, :patches]

    def slab(flip):
        return lax.dynamic_slice_in_dim(result, (section ^ flip) * width, width, 3)

    here = slab(0)
    beside, across, corner = (flipped(slab(flip), "pipe", flip) for flip in (1, 2, 3))

    def by_layer(own_layer, other_layer):
        return jnp.where(is_far, jnp.stack([other_layer, own_layer]), jnp.stack([own_layer, other_layer]))

    low = by_layer(jnp.where(is_first, here, beside), jnp.where(is_first, across, corner))
    high = by_layer(jnp.where(is_first, beside, here), jnp.where(is_first, corner, across))
    only_first = first_on * (1 - second_on)
    only_second = second_on * (1 - first_on)
    route = jnp.stack([1 - only_first[order], only_second[order], order]).astype(jnp.int32)
    out_shape = jax.ShapeDtypeStruct((images.shape[0], patches, width), BF16)
    mixed, input_grad = pl.pallas_call(
        place_body,
        out_shape=[out_shape, out_shape],
        in_specs=[IN_SMEM] + [IN_ANY] * 2,
        out_specs=[IN_ANY] * 2,
        scratch_shapes=[pltpu.VMEM(out_shape.shape, BF16), pltpu.VMEM(out_shape.shape, BF16), pltpu.SemaphoreType.DMA((2, 2 * SLOTS))],
        compiler_params=pltpu.CompilerParams(vmem_limit_bytes=VMEM_BYTES),
        name="place",
    )(route, low, high)

    return (
        mixed,
        input_grad,
        pieces[6][None, :],
        pieces[7][None, :],
        pieces[0].reshape(token_up.shape),
        pieces[2],
        pieces[1].reshape(token_down.shape),
        pieces[3],
        chan_up_grad,
        pieces[4],
        chan_down_grad,
        pieces[5],
    )


def solution(mesh):
    placed = (
        P("dp", None, None),
        P("dp", None, None),
        P("dp"),
        P("dp", None),
        P("pipe", None),
        P("pipe", None),
        P("pipe", None),
        P("pipe"),
        P("pipe", None),
        P("pipe"),
        P("pipe", None),
        P("pipe"),
        P("pipe", None),
        P("pipe"),
    )
    return jax.shard_map(
        local,
        mesh=mesh,
        in_specs=placed,
        out_specs=(
            P("dp", None, "pipe"),
            P("dp", None, "pipe"),
            P("pipe", None),
            P("pipe", None),
            P("pipe", None),
            P("pipe"),
            P("pipe", None),
            P("pipe"),
            P("pipe", "dp"),
            P("pipe"),
            P("pipe", "dp"),
            P("pipe"),
        ),
        check_vma=False,
    )
```

```python
import functools

import jax
import jax.numpy as jnp
import numpy as np
from jax import lax
from jax.experimental import pallas as pl
from jax.experimental.pallas import tpu as pltpu
from jax.sharding import PartitionSpec as P

F32 = jnp.float32
BF16 = jnp.bfloat16
NORM_EPS = 1e-06
GELU_SCALE = 0.7978845608
GELU_CUBE = 0.044715
STEPS = 2
SLOTS = 4
VMEM_BYTES = 40 << 20

IN_VMEM = pl.BlockSpec(memory_space=pltpu.VMEM)
IN_ANY = pl.BlockSpec(memory_space=pl.ANY)
IN_SMEM = pl.BlockSpec(memory_space=pltpu.SMEM)


def lasting(microseconds):
    return pl.CostEstimate(flops=int(microseconds * 10e9), bytes_accessed=1, transcendentals=0)


ON, VALID, CROSSING, IMAGE, PLACE, FORWARD, BACKWARD, ORDER, MIXED_FAR, GRAD_FAR = range(10)
LAYER, HALF, ME, LATE, HOPS, TICKS = range(6)

JOBS = [
    [(0, 0, 0, 0), (1, 1, 1, 1), (2, 2, 2, 2), (3, 3, 3, 3)],
    [(0, 3, -1, 3), (1, 1, 1, 1), (2, 0, 2, 0), (3, 2, 3, 2)],
    [(0, -1, -1, -1), (1, 2, -1, 2), (2, 0, 2, 0), (3, 1, 3, 1), (-1, 3, 0, 3)],
    [(0, -1, -1, -1), (1, 3, -1, 3), (2, 0, -1, 0), (3, 1, 3, 1), (-1, 2, 0, 2), (-1, -1, 1, -1)],
    [(0, -1, -1, -1), (1, -1, -1, -1), (2, 0, -1, 0), (3, 1, -1, 1), (-1, 2, 0, 2), (-1, 3, 1, 3), (-1, -1, 2, -1)],
]
MOST = 8
JOB_TABLE = np.full((len(JOBS), 4, MOST), -1, np.int32)
for _hops, _rows in enumerate(JOBS):
    for _tick, _row in enumerate(_rows):
        JOB_TABLE[_hops, :, _tick] = _row
TICK_TABLE = np.array([len(_rows) for _rows in JOBS], np.int32)


def flipped(block, axis, distance):
    count = lax.axis_size(axis)
    route = [(i, i ^ distance) for i in range(count) if i ^ distance < count]
    return lax.ppermute(block, axis, route)


def mm(left, right):
    return lax.dot_general(left, right, (((1,), (0,)), ((), ())), preferred_element_type=F32)


def mm_nt(left, right):
    return lax.dot_general(left, right, (((1,), (1,)), ((), ())), preferred_element_type=F32)


def gelu_pair(pre):
    square = pre * pre
    gate = 0.5 + 0.5 * jnp.tanh(pre * (GELU_SCALE + (GELU_SCALE * GELU_CUBE) * square))
    value = pre * gate
    slope = gate + value * (1.0 - gate) * (2 * GELU_SCALE + (6 * GELU_SCALE * GELU_CUBE) * square)
    return value, slope


def normalised(hidden):
    centred = hidden - jnp.mean(hidden, axis=-1, keepdims=True)
    scale = lax.rsqrt(jnp.mean(centred * centred, axis=-1, keepdims=True) + NORM_EPS)
    return centred * scale, scale


def launch(body, ins, specs, after, **options):
    first = len(ins)

    def trimmed(*refs):
        body(*refs[:first], *refs[first + len(after):])

    return pl.pallas_call(trimmed, in_specs=specs + [IN_ANY] * len(after), **options)(*ins, *after)


def table_body(own, jobs, ticks, valid, skip, tab):
    layer, half, me = own[0, 0], own[0, 1], own[0, 2]
    total = valid.shape[1]
    far = layer == 1
    firsts = [valid[0, i] * skip[0, i] for i in range(total)]
    seconds = [valid[0, i] * skip[1, i] for i in range(total)]
    kinds = [jnp.where(a * b == 1, 0, jnp.where(b == 1, 1, jnp.where(a == 1, 2, 3))) for a, b in zip(firsts, seconds)]
    crossing = sum(a * b for a, b in zip(firsts, seconds))
    hops = (crossing + 1) // 2
    for row in range(tab.shape[0]):
        for col in range(tab.shape[1]):
            tab[row, col] = 0
    for i in range(total):
        place = sum(((kinds[j] < kinds[i]) if j > i else (kinds[j] <= kinds[i])).astype(jnp.int32) for j in range(total) if j != i)
        tab[ORDER, place] = i
        tab[MIXED_FAR, place] = 1 - firsts[i] * (1 - seconds[i])
        tab[GRAD_FAR, place] = seconds[i] * (1 - firsts[i])

        @pl.when(place % 2 == half)
        def _():
            slot = place // 2
            tab[ON, slot] = jnp.where(far, seconds[i], firsts[i])
            tab[VALID, slot] = valid[0, i]
            tab[CROSSING, slot] = firsts[i] * seconds[i]
            tab[IMAGE, slot] = i

    tab[PLACE, LAYER] = layer
    tab[PLACE, HALF] = half
    tab[PLACE, ME] = me
    tab[PLACE, LATE] = jnp.where(far, -1, hops - 1)
    tab[PLACE, HOPS] = hops
    tab[PLACE, TICKS] = ticks[0, hops]
    for tick in range(MOST):
        tab[FORWARD, tick] = jobs[hops * 4 + layer, tick]
        tab[BACKWARD, tick] = jobs[hops * 4 + 2 + layer, tick]


KEPT = ("slab0", "slab1", "slab23", "z", "gz", "zt", "gt", "h0", "h1", "n2", "f", "dq", "da", "db", "vec")


def tick_body(late_call, *refs):
    refs = list(refs)
    tick_ref = None if late_call else refs.pop(0)
    (tab, images, cots, recv, own_up, got_up, own_down, got_down,
     up_w, up_t, down_w, down_t, up_col, down_col, u_row, w_row, gains, shifts,
     send_o, slab0, slab1, slab23, z_o, gz_o, zt_o, gt_o, h0_o, h1_o, n2_o, f_o, dq_o, da_o, db_o, vec_o,
     up_v, down_v, raw_v, e_v, h0_v, h1_v, n2_v, z_v, gz_v, zt_v, gt_v, dq_v, acc_v, out_v, part_v, da_v, db_v, vec_v,
     w_sems, in_sems, load_sems, slab_sems, keep_sems, back_sems) = refs
    far = tab[PLACE, LAYER] == 1
    half = tab[PLACE, HALF]
    section = tab[PLACE, LAYER] * 2 + half
    slabs = (slab0, slab1, slab23.at[0], slab23.at[1])
    patches, channels = raw_v.shape[1:]
    rows = h0_v.shape[0]
    ff = up_v.shape[1]
    hidden_t = zt_v.shape[0]
    width = ff // STEPS
    part = channels // len(slabs)
    if late_call:
        f_job = jnp.int32(-1)
        b_job = tab[PLACE, LATE]
    else:
        f_job = tab[FORWARD, tick_ref[0]]
        b_job = tab[BACKWARD, tick_ref[0]]
    f_slot = jnp.maximum(f_job, 0)
    b_slot = jnp.maximum(b_job, 0)
    f_on = (f_job >= 0) & (tab[ON, f_slot] == 1)
    b_on = (b_job >= 0) & (tab[ON, b_slot] == 1)
    any_on = f_on | b_on

    def weight_copies(step):
        size = channels // 2
        cols = pl.ds(pl.multiple_of(step * width, width), width)
        own = pl.ds(pl.multiple_of(half * size, 16), size)
        rest = pl.ds(pl.multiple_of((1 - half) * size, 16), size)
        local = pl.ds(pl.multiple_of((step % (STEPS // 2)) * width, width), width)
        return (lambda: pltpu.make_async_copy(own_up.at[:, cols], up_v.at[own, cols], w_sems.at[0, step]),
                lambda: pltpu.make_async_copy(got_up.at[:, cols], up_v.at[rest, cols], w_sems.at[1, step]),
                lambda: pltpu.make_async_copy(own_down.at[local, :], down_v.at[cols, :], w_sems.at[2, step]),
                lambda: pltpu.make_async_copy(got_down.at[local, :], down_v.at[cols, :], w_sems.at[2, step]))

    def start_weights(step):
        own, rest, mine, theirs = weight_copies(step)
        own().start()
        rest().start()

        @pl.when(step // (STEPS // 2) == half)
        def _():
            mine().start()

        @pl.when(step // (STEPS // 2) != half)
        def _():
            theirs().start()

    def await_weights(step):
        own, rest, mine, _ = weight_copies(step)
        own().wait()
        rest().wait()
        mine().wait()

    def fetch(kind, job, slot, crossed, source, target):
        @pl.when((job >= 0) & crossed)
        def _():
            pltpu.make_async_copy(recv, target, in_sems.at[kind]).start()

        @pl.when((job >= 0) & jnp.logical_not(crossed))
        def _():
            pltpu.make_async_copy(source.at[tab[IMAGE, slot]], raw_v.at[kind], in_sems.at[kind]).start()

    def fetched(kind, job, slot, crossed, source, target):
        @pl.when((job >= 0) & crossed)
        def _():
            pltpu.make_async_copy(recv, target, in_sems.at[kind]).wait()

        @pl.when((job >= 0) & jnp.logical_not(crossed))
        def _():
            pltpu.make_async_copy(source.at[tab[IMAGE, slot]], raw_v.at[kind], in_sems.at[kind]).wait()
            target[pl.ds(rows - 16, 16), :] = jnp.zeros((16, channels), BF16)
            target[pl.ds(0, patches), :] = raw_v[kind]

    forward_in = (0, f_job, f_slot, far & (tab[CROSSING, f_slot] == 1), images, h0_v)
    backward_in = (1, b_job, b_slot, jnp.logical_not(far) & (tab[CROSSING, b_slot] == 1), cots, e_v)
    loads = ((gz_o, gz_v), (h1_o, h1_v), (gt_o, gt_v), (h0_o, h0_v), (zt_o, zt_v))

    def load(i):
        return pltpu.make_async_copy(loads[i][0].at[b_slot], loads[i][1], load_sems.at[i])

    def reload(i):
        @pl.when(jnp.logical_not(f_on))
        def _():
            load(i).wait()

    if not late_call:
        fetch(*forward_in)
    fetch(*backward_in)

    @pl.when(any_on)
    def _():
        start_weights(0)

    @pl.when(b_on & jnp.logical_not(f_on))
    def _():
        for i in range(len(loads)):
            load(i).start()

    @pl.when(any_on)
    def _():
        @pl.loop(1, STEPS)
        def _(step):
            start_weights(step)

    def slab_copy(kind, slot, flip):
        return pltpu.make_async_copy(part_v.at[kind, section ^ flip], slabs[flip].at[kind, slot], slab_sems.at[kind, flip])

    def send_copy(kind):
        return pltpu.make_async_copy(out_v.at[kind], send_o, slab_sems.at[kind, len(slabs)])

    def deliver(kind, slot, sends):
        whole = out_v[kind]
        upper = part_v.shape[2]
        for d in range(len(slabs)):
            part_v[kind, d, :, 0:part] = whole[:upper, d * part:(d + 1) * part]
            part_v[kind, d, 0:rows - upper, part:2 * part] = whole[upper:, d * part:(d + 1) * part]
        for flip in range(len(slabs)):
            slab_copy(kind, slot, flip).start()

        @pl.when(sends)
        def _():
            send_copy(kind).start()

    def delivered(kind, slot, sends):
        for flip in range(len(slabs)):
            slab_copy(kind, slot, flip).wait()

        @pl.when(sends)
        def _():
            send_copy(kind).wait()

    saves = ((gz_v, gz_o), (zt_v, zt_o), (gt_v, gt_o), (h0_v, h0_o), (h1_v, h1_o), (z_v, z_o), (n2_v, n2_o))

    def save(i):
        return pltpu.make_async_copy(saves[i][0], saves[i][1].at[f_slot], keep_sems.at[i])

    def run_forward():
        h0 = h0_v[...].astype(F32)
        centred, _ = normalised(h0)
        n1 = (centred * gains[0:1, :] + shifts[0:1, :]).astype(BF16)
        value, slope = gelu_pair(mm(up_t[...], n1) + up_col[...])
        value = value.astype(BF16)
        zt_v[...] = value
        gt_v[...] = slope.astype(BF16)
        h1 = (h0 + (mm(down_t[...], value) + down_col[...])).astype(BF16)
        h1_v[...] = h1
        h1 = h1.astype(F32)
        centred, _ = normalised(h1)
        n2_v[...] = (centred * gains[1:2, :] + shifts[1:2, :]).astype(BF16)
        save(6).start()

        @pl.when(jnp.logical_not(b_on))
        def _():
            for i in range(1, 5):
                save(i).start()

        acc_v[...] = h1 + w_row[...]

        @pl.loop(0, STEPS)
        def _(step):
            cols = pl.ds(pl.multiple_of(step * width, width), width)
            await_weights(step)
            value, slope = gelu_pair(mm(n2_v[...], up_v[:, cols]) + u_row[:, cols])
            value = value.astype(BF16)
            z_v[:, cols] = value
            gz_v[:, cols] = slope.astype(BF16)
            acc_v[...] += mm(value, down_v[cols, :])

        save(5).start()

        @pl.when(jnp.logical_not(b_on))
        def _():
            save(0).start()

        out_v[0] = acc_v[...].astype(BF16)

    def norm_back(hidden, dn, grad, row):
        centred, scale = normalised(hidden)
        vec_v[2 + row:3 + row, 0:channels] = jnp.sum(dn * centred, axis=0, keepdims=True)
        vec_v[4 + row:5 + row, 0:channels] = jnp.sum(dn, axis=0, keepdims=True)
        scaled = dn * gains[row:row + 1, :]
        along = jnp.mean(scaled * centred, axis=-1, keepdims=True)
        flat = jnp.mean(scaled, axis=-1, keepdims=True)
        return centred, grad + scale * (scaled - flat - centred * along)

    backs = ((e_v, f_o), (dq_v, dq_o), (da_v, da_o), (db_v, db_o), (vec_v, vec_o))

    def back(i):
        return pltpu.make_async_copy(backs[i][0], backs[i][1].at[b_slot], back_sems.at[i])

    def run_backward():
        back(0).start()
        grad = e_v[...].astype(F32)
        vec_v[...] = jnp.zeros_like(vec_v)
        vec_v[1:2, 0:channels] = jnp.sum(grad, axis=0, keepdims=True)
        acc_v[...] = jnp.zeros_like(acc_v)
        reload(0)

        @pl.loop(0, STEPS)
        def _(step):
            cols = pl.ds(pl.multiple_of(step * width, width), width)

            @pl.when(jnp.logical_not(f_on))
            def _():
                await_weights(step)

            dq = (mm_nt(e_v[...], down_v[cols, :]) * gz_v[:, cols].astype(F32)).astype(BF16)
            dq_v[:, cols] = dq
            vec_v[0:1, cols] = jnp.sum(dq.astype(F32), axis=0, keepdims=True)
            acc_v[...] += mm_nt(dq, up_v[:, cols])

        back(1).start()
        reload(1)
        _, grad = norm_back(h1_v[...].astype(F32), acc_v[...], grad, 1)
        f1 = grad.astype(BF16)
        reload(2)
        dq = (mm(down_w[...], f1) * gt_v[...].astype(F32)).astype(BF16)
        reload(3)
        centred, grad = norm_back(h0_v[...].astype(F32), mm(up_w[...], dq), f1.astype(F32), 0)
        out_v[1] = grad.astype(BF16)
        n1 = (centred * gains[0:1, :] + shifts[0:1, :]).astype(BF16)
        reload(4)
        da_v[...] = mm_nt(n1, dq)
        db_v[...] = mm_nt(f1, zt_v[...])
        ones = jnp.ones((8, channels), BF16)
        vec_v[6:7, 0:hidden_t] = mm_nt(ones, dq)[0:1]
        vec_v[7:8, 0:rows] = mm_nt(ones, f1)[0:1]
        for i in range(2, 5):
            back(i).start()

    near = jnp.logical_not(far)
    if not late_call:
        fetched(*forward_in)

        @pl.when(f_on)
        def _():
            run_forward()

        @pl.when((f_job >= 0) & jnp.logical_not(f_on))
        def _():
            out_v[0] = h0_v[...] * tab[VALID, f_slot].astype(F32).astype(BF16)

        @pl.when(f_job >= 0)
        def _():
            deliver(0, f_slot, near)

    fetched(*backward_in)

    @pl.when(b_on)
    def _():
        run_backward()

    @pl.when((b_job >= 0) & jnp.logical_not(b_on))
    def _():
        out_v[1] = e_v[...] * tab[VALID, b_slot].astype(F32).astype(BF16)

    @pl.when(b_job >= 0)
    def _():
        deliver(1, b_slot, far)
        delivered(1, b_slot, far)

    @pl.when(b_on)
    def _():
        for i in range(5):
            back(i).wait()

    if not late_call:
        @pl.when(f_job >= 0)
        def _():
            delivered(0, f_slot, near)

        @pl.when(f_on)
        def _():
            save(5).wait()
            save(6).wait()

        @pl.when(f_on & jnp.logical_not(b_on))
        def _():
            for i in range(5):
                save(i).wait()


def tick_call(tick, tab, images, cots, recv, w, kept, after=()):
    patches, channels = images.shape[1:]
    rows = recv.shape[0]
    ff = w["own_up"].shape[1]
    hidden_t = w["up_t"].shape[0]
    sections = 4
    shape = jax.ShapeDtypeStruct
    upper = -(-rows // 32) * 16
    slab = shape((2, SLOTS, upper, 2 * channels // sections), BF16)
    wide = shape((SLOTS, rows, ff), BF16)
    tall = shape((SLOTS, hidden_t, channels), BF16)
    plain = shape((SLOTS, rows, channels), BF16)
    shapes = [shape((rows, channels), BF16), slab, slab, shape((2,) + slab.shape, BF16)] + [wide, wide, tall, tall, plain, plain, plain, plain, wide,
              shape((SLOTS, rows, hidden_t), F32), shape((SLOTS, rows, hidden_t), F32), shape((SLOTS, 8, ff), F32)]
    names = ("own_up", "got_up", "own_down", "got_down", "up_w", "up_t", "down_w", "down_t", "up_col", "down_col", "u_row", "w_row", "gains", "shifts")
    ins = [tab, images, cots, recv] + [w[k] for k in names]
    specs = [IN_SMEM] + [IN_ANY] * 7 + [IN_VMEM] * 10
    if tick is not None:
        ins.insert(0, tick.reshape(1))
        specs.insert(0, IN_SMEM)
    ins += list(after)
    specs += [IN_ANY] * len(after)
    first = len(ins)
    passed = 0
    aliases = {}
    if kept is not None:
        passed = len(kept)
        aliases = {first + i: 1 + i for i in range(passed)}
        ins += list(kept)
        specs += [IN_ANY] * passed

    def trimmed(*refs):
        tick_body(tick is None, *refs[:first - len(after)], *refs[first + passed:])

    vmem = pltpu.VMEM
    line = vmem((rows, channels), BF16)
    broad = vmem((rows, ff), BF16)
    high = vmem((hidden_t, channels), BF16)
    dma = pltpu.SemaphoreType.DMA
    out = pl.pallas_call(
        trimmed,
        out_shape=shapes,
        in_specs=specs,
        out_specs=[IN_ANY] * len(shapes),
        input_output_aliases=aliases,
        scratch_shapes=[vmem((channels, ff), BF16), vmem((ff, channels), BF16), vmem((2, patches, channels), BF16), line, line, line, line,
                        broad, broad, high, high, broad, vmem((rows, channels), F32), vmem((2, rows, channels), BF16),
                        vmem((2, sections, upper, 2 * channels // sections), BF16),
                        vmem((rows, hidden_t), F32), vmem((rows, hidden_t), F32), vmem((8, ff), F32),
                        dma((3, STEPS)), dma((2,)), dma((5,)), dma((2, sections + 1)), dma((7,)), dma((5,))],
        compiler_params=pltpu.CompilerParams(vmem_limit_bytes=VMEM_BYTES),
        cost_estimate=lasting(8),
        name="tick" if tick is not None else "late_tick",
    )(*ins)
    return out[0], tuple(out[1:])


def position(relative, bits):
    place = 0
    for bit in bits:
        place = place * 2 + ((relative >> bit) & 1)
    return place


def down_grad_body(chunks, count, orders, aligned, tab, f_i, z_i, rider_i, *refs):
    outs, (f_v, ft_v, z_v, f_sems, z_sems) = refs[:2 * chunks], refs[2 * chunks:]
    half = tab[PLACE, HALF]
    me = tab[PLACE, ME]
    width = outs[0].shape[-1]
    channels = f_i.shape[2]
    rows = f_i.shape[1]
    size = z_i.shape[2] // 2
    tile = 256 if width % 256 == 0 else width
    piece = channels // count
    extra = rider_i.shape[1] // count if aligned else 0

    def z_copy(slot, which):
        first = pl.multiple_of(jnp.where(half == which % 2, 1, 0) * size + which // 2 * width, 128)
        return pltpu.make_async_copy(z_i.at[slot, :, pl.ds(first, width)], z_v.at[which, pl.ds(slot * rows, rows), :], z_sems.at[which, slot])

    def f_copy(slot):
        return pltpu.make_async_copy(f_i.at[slot], f_v.at[pl.ds(slot * rows, rows), :], f_sems.at[slot])

    for slot in range(SLOTS):
        @pl.when(tab[ON, slot] == 1)
        def _():
            f_copy(slot).start()

        @pl.when(tab[ON, slot] != 1)
        def _():
            f_v[pl.ds(slot * rows, rows), :] = jnp.zeros((rows, channels), BF16)

    for which in range(2 * chunks):
        for slot in range(SLOTS):
            @pl.when(tab[ON, slot] == 1)
            def _():
                z_copy(slot, which).start()

            @pl.when(tab[ON, slot] != 1)
            def _():
                z_v[which, pl.ds(slot * rows, rows), :] = jnp.zeros((rows, width), BF16)

    for slot in range(SLOTS):
        @pl.when(tab[ON, slot] == 1)
        def _():
            f_copy(slot).wait()

    ft_v[...] = f_v[...].T
    for which, out in enumerate(outs):
        for slot in range(SLOTS):
            @pl.when(tab[ON, slot] == 1)
            def _():
                z_copy(slot, which).wait()

        each = piece + (extra if which < 2 else 0)
        first = [pl.multiple_of(position(d ^ me, orders[which // 2]) * each, 16) for d in range(count)]

        @pl.loop(0, width // tile)
        def _(step):
            cols = pl.ds(pl.multiple_of(step * tile, tile), tile)
            total = mm(ft_v[...], z_v[which, :, cols]).astype(BF16)
            if aligned:
                for d in range(count):
                    out[pl.ds(first[d], piece), cols] = total[d * piece:(d + 1) * piece]
            else:
                out[:, cols] = total

        if extra and which < 2:
            for d in range(count):
                out[pl.ds(first[d] + piece, extra), :] = rider_i[which, d * extra:(d + 1) * extra, :]


def up_grad_body(chunks, height, count, orders, aligned, tab, n_i, dq_i, *refs):
    outs, (n_v, nt_v, dq_v, n_sems, dq_sems) = refs[:2 * chunks], refs[2 * chunks:]
    half = tab[PLACE, HALF]
    me = tab[PLACE, ME]
    rows = n_i.shape[1]
    size = n_i.shape[2] // 2
    ff = dq_i.shape[2]

    def n_copy(slot):
        return pltpu.make_async_copy(n_i.at[slot], n_v.at[pl.ds(slot * rows, rows), :], n_sems.at[slot])

    def dq_copy(slot):
        return pltpu.make_async_copy(dq_i.at[slot], dq_v.at[pl.ds(slot * rows, rows), :], dq_sems.at[slot])

    for slot in range(SLOTS):
        on = tab[ON, slot] == 1

        @pl.when(on)
        def _():
            n_copy(slot).start()
            dq_copy(slot).start()

        @pl.when(jnp.logical_not(on))
        def _():
            n_v[pl.ds(slot * rows, rows), :] = jnp.zeros((rows, 2 * size), BF16)
            dq_v[pl.ds(slot * rows, rows), :] = jnp.zeros((rows, ff), BF16)

    for slot in range(SLOTS):
        @pl.when(tab[ON, slot] == 1)
        def _():
            n_copy(slot).wait()

    turned = n_v[...].T
    for fixed in range(2):
        side = jnp.where(half == fixed, 1, 0)
        for chunk in range(chunks):
            first = fixed * size + chunk * height
            nt_v[chunk, pl.ds(pl.multiple_of(side * height, 16), height), :] = turned[first:first + height]

    for slot in range(SLOTS):
        @pl.when(tab[ON, slot] == 1)
        def _():
            dq_copy(slot).wait()

    piece = ff // count if aligned else 384
    for chunk in range(chunks):
        theirs_o, mine_o = outs[2 * chunk:2 * chunk + 2]

        @pl.loop(0, ff // piece)
        def _(d):
            cols = pl.ds(pl.multiple_of(d * piece, 128), piece)
            total = mm(nt_v[chunk], dq_v[:, cols]).astype(BF16)
            if not aligned:
                theirs_o[:, cols] = total[:height]
                mine_o[:, cols] = total[height:]
                return
            place = pl.ds(pl.multiple_of(position(d ^ me, orders[chunk]) * height, 16), height)
            theirs_o[place, :] = total[:height]
            mine_o[place, :] = total[height:]


def arranged(pieces, bits):
    count = pieces.shape[0]
    order = [0] * count
    for relative in range(count):
        order[position(relative, bits)] = relative
    return jnp.take(pieces, jnp.array(order) ^ lax.axis_index("dp"), axis=0)


def down_grad_call(chunks, count, orders, tab, f, z, rider, after):
    slots, rows, channels = f.shape
    width = z.shape[2] // 2 // chunks
    piece = channels // count
    aligned = piece % 16 == 0
    extra = rider.shape[1] if aligned else 0
    shapes = [(channels + (extra if i == 0 else 0), width) for i in range(chunks)]
    out = launch(
        functools.partial(down_grad_body, chunks, count, orders, aligned), [tab, f, z, rider], [IN_SMEM, IN_ANY, IN_ANY, IN_VMEM], after,
        out_shape=[jax.ShapeDtypeStruct(shapes[i // 2], BF16) for i in range(2 * chunks)],
        out_specs=[IN_VMEM] * (2 * chunks),
        scratch_shapes=[pltpu.VMEM((slots * rows, channels), BF16), pltpu.VMEM((channels, slots * rows), BF16),
                        pltpu.VMEM((2 * chunks, slots * rows, width), BF16),
                        pltpu.SemaphoreType.DMA((slots,)), pltpu.SemaphoreType.DMA((2 * chunks, slots))],
        compiler_params=pltpu.CompilerParams(vmem_limit_bytes=VMEM_BYTES),
        cost_estimate=lasting(9),
        name="down_grad",
    )
    if not aligned:
        out = [arranged(part.reshape(count, piece, width), orders[i // 2]).reshape(part.shape) for i, part in enumerate(out)]
    return [out[2 * i:2 * i + 2] for i in range(chunks)]


def up_grad_call(chunks, count, orders, tab, n, dq, after):
    slots, rows, channels = n.shape
    ff = dq.shape[2]
    height = channels // 2 // chunks
    piece = ff // count
    aligned = piece % 128 == 0
    shape = (count * height, piece) if aligned else (height, ff)
    out = launch(
        functools.partial(up_grad_body, chunks, height, count, orders, aligned), [tab, n, dq], [IN_SMEM, IN_ANY, IN_ANY], after,
        out_shape=[jax.ShapeDtypeStruct(shape, BF16)] * (2 * chunks),
        out_specs=[IN_VMEM] * (2 * chunks),
        scratch_shapes=[pltpu.VMEM((slots * rows, channels), BF16), pltpu.VMEM((chunks, 2 * height, slots * rows), BF16), pltpu.VMEM((slots * rows, ff), BF16),
                        pltpu.SemaphoreType.DMA((slots,)), pltpu.SemaphoreType.DMA((slots,))],
        compiler_params=pltpu.CompilerParams(vmem_limit_bytes=VMEM_BYTES),
        cost_estimate=lasting(9),
        name="up_grad",
    )
    if not aligned:
        out = [arranged(jnp.swapaxes(part.reshape(height, count, piece), 0, 1), orders[i // 2]).reshape(count * height, piece) for i, part in enumerate(out)]
    return [out[2 * i:2 * i + 2] for i in range(chunks)]


def halved_body(mine, got, kept, sent):
    middle = kept.shape[0]
    low, high = pl.ds(0, middle), pl.ds(middle, middle)
    sent[...] = (mine[high, :].astype(F32) + got[high, :].astype(F32)).astype(BF16)
    kept[...] = (mine[low, :].astype(F32) + got[low, :].astype(F32)).astype(BF16)


def halved(mine, got, after):
    size, width = mine.shape
    return launch(halved_body, [mine, got], [IN_VMEM] * 2, after,
                  out_shape=[jax.ShapeDtypeStruct((size // 2, width), BF16)] * 2, out_specs=[IN_VMEM] * 2,
                  compiler_params=pltpu.CompilerParams(vmem_limit_bytes=VMEM_BYTES), cost_estimate=lasting(2), name="halved")


def summed_body(turn, mine, got, out, *rest):
    size = out.shape[1] if turn else out.shape[0]
    total = mine[...].astype(F32) + got[...].astype(F32)
    out[...] = total[:size].T if turn else total[:size]
    for rider in rest:
        rider[...] = total[size:].astype(BF16)


def summed(mine, got, size, turn, after):
    rows, width = mine.shape
    shapes = [jax.ShapeDtypeStruct((width, size) if turn else (size, width), F32)]
    if rows > size:
        shapes.append(jax.ShapeDtypeStruct((rows - size, width), BF16))
    return launch(functools.partial(summed_body, turn), [mine, got], [IN_VMEM] * 2, after,
                  out_shape=shapes, out_specs=[IN_VMEM] * len(shapes),
                  compiler_params=pltpu.CompilerParams(vmem_limit_bytes=VMEM_BYTES), cost_estimate=lasting(2), name="summed")


def packing(patches, hidden_t, channels, ff):
    spans = {}
    row = 0
    for name, height in (("token", -(-patches // 2 // 8) * 8), ("chan_up_bias", ff // 2 // channels), ("biases", 1), ("gain", 1), ("shift", 1)):
        spans[name] = row
        row += height
    return spans, -(-row // 128) * 128, channels


def pack_body(spans, patches, tab, da_i, db_i, vec_i, out, da_v, db_v, vec_v, both_v, sems):
    half = tab[PLACE, HALF]
    lanes = both_v.shape[-1]
    hidden_t = db_v.shape[2]
    upper = patches // 2
    sources = ((da_i, da_v), (db_i, db_v), (vec_i, vec_v))

    def copy(kind, slot):
        return pltpu.make_async_copy(sources[kind][0].at[slot], sources[kind][1].at[slot], sems.at[kind, slot])

    for slot in range(SLOTS):
        @pl.when(tab[ON, slot] == 1)
        def _():
            for kind in range(3):
                copy(kind, slot).start()

        @pl.when(tab[ON, slot] != 1)
        def _():
            for _, buffer in sources:
                buffer[slot] = jnp.zeros(buffer.shape[1:], F32)

    for slot in range(SLOTS):
        @pl.when(tab[ON, slot] == 1)
        def _():
            for kind in range(3):
                copy(kind, slot).wait()

    da = (da_v[0] + da_v[1]) + (da_v[2] + da_v[3])
    db = (db_v[0] + db_v[1]) + (db_v[2] + db_v[3])
    vec = (vec_v[0] + vec_v[1]) + (vec_v[2] + vec_v[3])
    both_v[...] = jnp.zeros_like(both_v)
    ff = vec.shape[1]
    channels = spans["channels"]
    for side in range(2):
        at = spans["token"]
        both_v[side, at:at + upper, 0:hidden_t] = da[side * upper:(side + 1) * upper]
        block = db[:, side * (hidden_t // 2):(side + 1) * (hidden_t // 2)]
        both_v[side, at:at + upper, hidden_t:hidden_t + hidden_t // 2] = block[:upper]
        both_v[side, at:at + upper, hidden_t + hidden_t // 2:2 * hidden_t] = block[upper:patches]

        def line(name, row, first, length, left=0):
            at = spans[name]
            for step in range(-(-length // lanes)):
                size = min(lanes, length - step * lanes)
                both_v[side, at + step:at + step + 1, left:left + size] = vec[row:row + 1, first + step * lanes:first + step * lanes + size]

        line("chan_up_bias", 0, side * (ff // 2), ff // 2)
        line("biases", 1, side * (channels // 2), channels // 2)
        line("biases", 6, side * (hidden_t // 2), hidden_t // 2, channels // 2)
        line("biases", 7, side * upper, upper, channels // 2 + hidden_t // 2)
        line("gain", 2 + side, 0, channels)
        line("shift", 4 + side, 0, channels)
    out[0] = both_v[1 - half].astype(BF16)
    out[1] = both_v[half].astype(BF16)


def unpack_body(spans, patches, hidden_t, relative, tab, parts, gain_o, shift_o, up_o, up_bias_o, down_o, down_bias_o, chan_up_bias_o, chan_down_bias_o, all_v):
    size = parts.shape[1]
    for i, shift in enumerate(relative):
        first = pl.multiple_of((tab[PLACE, ME] ^ shift) * size, 8) if len(relative) > 1 else 0
        all_v[pl.ds(first, size), :] = parts[i].astype(F32)
    upper = patches // 2
    lanes = all_v.shape[1]
    at = spans["token"]
    up_o[...] = all_v[at:at + upper, 0:hidden_t]
    block = all_v[at:at + -(-upper // 8) * 8, hidden_t:2 * hidden_t]
    down_o[:, 0:upper] = block[:, :hidden_t // 2].T[:, :upper]
    down_o[:, upper:patches] = block[:, hidden_t // 2:].T[:, :upper]
    gain_o[...] = all_v[spans["gain"]:spans["gain"] + 1, :]
    shift_o[...] = all_v[spans["shift"]:spans["shift"] + 1, :]
    for step in range(chan_up_bias_o.shape[1] // lanes):
        at = spans["chan_up_bias"] + step
        chan_up_bias_o[:, step * lanes:(step + 1) * lanes] = all_v[at:at + 1, :]
    row = all_v[spans["biases"]:spans["biases"] + 1, :]
    first = chan_down_bias_o.shape[1]
    chan_down_bias_o[...] = row[:, :first]
    up_bias_o[...] = row[:, first:first + hidden_t // 2]
    down_bias_o[...] = row[:, first + hidden_t // 2:first + hidden_t // 2 + upper]


def unpack(spans, patches, hidden_t, channels, ff, relative, tab, parts, after):
    sizes = [(1, channels), (1, channels), (patches // 2, hidden_t), (1, hidden_t // 2), (hidden_t // 2, patches), (1, patches // 2), (1, ff // 2), (1, channels // 2)]
    return launch(
        functools.partial(unpack_body, spans, patches, hidden_t, relative), [tab, parts], [IN_SMEM, IN_VMEM], after,
        out_shape=[jax.ShapeDtypeStruct(size, F32) for size in sizes],
        out_specs=[IN_VMEM] * len(sizes),
        scratch_shapes=[pltpu.VMEM((parts.shape[0] * parts.shape[1], parts.shape[2]), F32)],
        compiler_params=pltpu.CompilerParams(vmem_limit_bytes=VMEM_BYTES),
        cost_estimate=lasting(2),
        name="unpack",
    )


def both_body(first, second, out):
    out[0:first.shape[0]] = first[...]
    out[first.shape[0]:] = second[...]


def both(first, second, after):
    shape = (2 * first.shape[0],) + first.shape[1:]
    return launch(both_body, [first, second], [IN_VMEM] * 2, after, out_shape=jax.ShapeDtypeStruct(shape, first.dtype), out_specs=IN_VMEM,
                  compiler_params=pltpu.CompilerParams(vmem_limit_bytes=VMEM_BYTES), cost_estimate=lasting(2), name="both")


def split_body(both, first_o, second_o, sems):
    copies = [pltpu.make_async_copy(both.at[i], target, sems.at[i]) for i, target in enumerate((first_o, second_o))]
    for copy in copies:
        copy.start()
    for copy in copies:
        copy.wait()


def split(both, after):
    return launch(split_body, [both], [IN_ANY], after, out_shape=[jax.ShapeDtypeStruct(both.shape[1:], both.dtype)] * 2,
                  out_specs=[IN_VMEM] * 2, scratch_shapes=[pltpu.SemaphoreType.DMA((2,))],
                  compiler_params=pltpu.CompilerParams(vmem_limit_bytes=VMEM_BYTES), cost_estimate=lasting(0.1), name="split")


def place_body(tab, here, beside, across, corner, mixed_o, grad_o, mixed_v, grad_v, sems):
    layer = tab[PLACE, LAYER]
    half = tab[PLACE, HALF]
    sources = (here, beside, across, corner)
    patches = mixed_o.shape[1]
    places = mixed_o.shape[0]
    width = mixed_o.shape[2]
    upper = mixed_v.shape[1]
    buffers = (mixed_v, grad_v)

    def copy(kind, place, source):
        return pltpu.make_async_copy(source.at[kind, place // 2], buffers[kind].at[tab[ORDER, place]], sems.at[kind, place])

    for place in range(places):
        for kind, row in enumerate((MIXED_FAR, GRAD_FAR)):
            which = jnp.where(tab[row, place] == layer, 0, 2) + jnp.where(half == place % 2, 0, 1)
            for i, source in enumerate(sources):
                @pl.when(which == i)
                def _():
                    copy(kind, place, source).start()

    for place in range(places):
        for kind in range(2):
            copy(kind, place, here).wait()

    @pl.loop(0, places)
    def _(i):
        for source, target in ((mixed_v, mixed_o), (grad_v, grad_o)):
            target[i, 0:upper] = source[i, :, 0:width]
            target[i, upper:patches] = source[i, 0:patches - upper, width:2 * width]


def pack_call(spans, packed_rows, lanes, patches, channels, tab, da, db, vec, after):
    return launch(
        functools.partial(pack_body, dict(spans, channels=channels), patches), [tab, da, db, vec], [IN_SMEM] + [IN_ANY] * 3, after,
        out_shape=jax.ShapeDtypeStruct((2, packed_rows, lanes), BF16),
        out_specs=IN_VMEM,
        scratch_shapes=[pltpu.VMEM(da.shape, F32), pltpu.VMEM(db.shape, F32), pltpu.VMEM(vec.shape, F32),
                        pltpu.VMEM((2, packed_rows, lanes), F32), pltpu.SemaphoreType.DMA((3, SLOTS))],
        compiler_params=pltpu.CompilerParams(vmem_limit_bytes=VMEM_BYTES),
        cost_estimate=lasting(2.5),
        name="pack",
    )


def place_call(slot_count, patches, width, tab, slabs, after):
    out_shape = jax.ShapeDtypeStruct((slot_count, patches, width), BF16)
    buffer = pltpu.VMEM((slot_count,) + slabs[0].shape[2:], BF16)
    return launch(
        place_body, [tab] + list(slabs), [IN_SMEM] + [IN_ANY] * 4, after,
        out_shape=[out_shape, out_shape],
        out_specs=[IN_VMEM] * 2,
        scratch_shapes=[buffer, buffer, pltpu.SemaphoreType.DMA((2, slot_count))],
        compiler_params=pltpu.CompilerParams(vmem_limit_bytes=VMEM_BYTES),
        cost_estimate=lasting(4),
        name="place",
    )


def local(images, cotangent, valid_rows, skip_masks, norm_gain, norm_bias, token_up, token_up_bias, token_down,
          token_down_bias, chan_up, chan_up_bias, chan_down, chan_down_bias):
    count = lax.axis_size("dp")
    section = lax.axis_index("pipe")
    half = section % 2
    is_first = half == 0
    slot_count, patches, channels = images.shape
    rows = -(-patches // 16) * 16
    hidden_t = token_up.shape[1]
    ff = chan_up.shape[1]

    own = (token_up, token_up_bias, token_down, token_down_bias, chan_up_bias, chan_down_bias, norm_gain, norm_bias)
    got_up = flipped(chan_up, "pipe", 1)
    got_down = flipped(chan_down, "pipe", 1)
    got = tuple(flipped(part, "pipe", 1) for part in own)

    def joined(i):
        return jnp.concatenate([jnp.where(is_first, own[i], got[i]), jnp.where(is_first, got[i], own[i])], 0)

    def padded(array, axis):
        extra = [(0, 0)] * array.ndim
        extra[axis] = (0, rows - patches)
        return jnp.pad(array, extra)

    place = jnp.stack([section // 2, half, lax.axis_index("dp"), jnp.zeros_like(half)]).astype(jnp.int32)[None, :]
    tab = pl.pallas_call(
        table_body,
        out_shape=jax.ShapeDtypeStruct((10, MOST), jnp.int32),
        in_specs=[IN_SMEM] * 5,
        out_specs=IN_SMEM,
        name="table",
    )(place, jnp.asarray(JOB_TABLE.reshape(-1, MOST)), jnp.asarray(TICK_TABLE[None, :]), valid_rows[None, :], skip_masks.T)

    up_w = padded(joined(0), 0)
    down_w = padded(joined(2), 1)
    weights = {
        "own_up": chan_up, "got_up": got_up, "own_down": chan_down, "got_down": got_down,
        "up_w": up_w, "down_w": down_w,
        "up_t": up_w.T, "down_t": down_w.T,
        "up_col": joined(1).astype(F32)[:, None],
        "down_col": padded(joined(3).astype(F32), 0)[:, None],
        "u_row": joined(4).astype(F32)[None, :],
        "w_row": joined(5).astype(F32)[None, :],
        "gains": joined(6).astype(F32),
        "shifts": joined(7).astype(F32),
    }

    blank = jnp.zeros((rows, channels), BF16)
    send, kept = tick_call(jnp.int32(0), tab, images, cotangent, blank, weights, None)

    def one(tick, carried):
        send, recv, kept = carried
        arriving = flipped(send, "pipe", 2)
        send, kept = tick_call(tick, tab, images, cotangent, recv, weights, kept)
        return send, arriving, kept

    _, last, kept = lax.fori_loop(1, tab[PLACE, TICKS], one, (send, blank, kept))
    kept = dict(zip(KEPT, kept))

    chunks = 2
    bits = tuple(range(count.bit_length() - 1))
    other_bits = (bits[1], bits[0]) + bits[2:]
    orders = (bits, other_bits, bits, other_bits)
    spans, packed_rows, lanes = packing(patches, hidden_t, channels, ff)

    made = []

    def step(function, *arrays):
        out = function(*arrays, after=tuple(made))
        made[:] = jax.tree.leaves(out)[:1]
        return out

    pieces = [None] * (2 * chunks)
    moving = [None] * (2 * chunks)

    def begin(which, pair):
        pieces[which] = pair[1]
        moving[which] = flipped(pair[0], "pipe", 1)

    def advance(which, stage):
        pieces[which], sent = step(halved, pieces[which], moving[which])
        moving[which] = flipped(sent, "dp", 1 << orders[which][stage])

    def finished(which):
        size = channels // 2 // chunks if which >= chunks else channels // count
        return step(summed, pieces[which], moving[which], size, which < chunks)

    _, late_kept = step(tick_call, None, tab, images, cotangent, last, weights, tuple(kept[k] for k in KEPT))
    made[:] = late_kept[:1]
    kept = dict(zip(KEPT, late_kept))
    over = flipped(kept["slab23"], "pipe", 2)
    beside = flipped(kept["slab1"], "pipe", 1)
    rider = step(pack_call, spans, packed_rows, lanes, patches, channels, tab, kept["da"], kept["db"], kept["vec"])
    made.append(beside)
    for i, pair in enumerate(step(down_grad_call, chunks, count, orders[:chunks], tab, kept["f"], kept["z"], rider)):
        begin(i, pair)
    advance(0, 0)
    advance(1, 0)
    for i, pair in enumerate(step(up_grad_call, chunks, count, orders[chunks:], tab, kept["n2"], kept["dq"])):
        begin(chunks + i, pair)
    advance(0, 1)
    advance(1, 1)
    advance(2, 0)
    advance(3, 0)
    across, turned = step(split, over)
    corner = flipped(turned, "pipe", 1)
    for stage in range(2, len(bits)):
        advance(0, stage)
        advance(1, stage)
    advance(2, 1)
    advance(3, 1)
    down_first, *small = finished(0)
    parts = small[0][None] if small else None
    relative = [0]
    gathered = list(reversed(bits)) if small else []

    def gather():
        nonlocal parts, relative
        if gathered:
            bit = gathered.pop(0)
            parts = step(both, parts, flipped(parts, "dp", 1 << bit))
            relative += [i ^ (1 << bit) for i in relative]

    width = channels // 4
    mixed, input_grad = step(place_call, slot_count, patches, width, tab, (kept["slab0"], beside, across, corner))
    down_second, = finished(1)
    gather()
    for stage in range(2, len(bits)):
        advance(2, stage)
        advance(3, stage)
    while gathered:
        gather()
    if parts is None:
        total = rider[1].astype(F32) + flipped(rider[0], "pipe", 1).astype(F32)
        for bit in bits:
            sent = lax.optimization_barrier(total.astype(BF16))
            total = sent.astype(F32) + flipped(sent, "dp", 1 << bit).astype(F32)
        parts = total[None]
    gain, shift, token_up_grad, up_bias, token_down_grad, down_bias, chan_up_bias_grad, chan_down_bias_grad = step(
        unpack, spans, patches, hidden_t, channels, ff, relative, tab, parts)
    up_first, = finished(2)
    up_second, = finished(3)
    chan_down_grad = jnp.concatenate([down_first, down_second], 0)
    chan_up_grad = jnp.concatenate([up_first, up_second], 0)

    return (
        mixed,
        input_grad,
        gain,
        shift,
        token_up_grad,
        up_bias[0],
        token_down_grad,
        down_bias[0],
        chan_up_grad,
        chan_up_bias_grad[0],
        chan_down_grad,
        chan_down_bias_grad[0],
    )


def solution(mesh):
    placed = (
        P("dp", None, None),
        P("dp", None, None),
        P("dp"),
        P("dp", None),
        P("pipe", None),
        P("pipe", None),
        P("pipe", None),
        P("pipe"),
        P("pipe", None),
        P("pipe"),
        P("pipe", None),
        P("pipe"),
        P("pipe", None),
        P("pipe"),
    )
    return jax.shard_map(
        local,
        mesh=mesh,
        in_specs=placed,
        out_specs=(
            P("dp", None, "pipe"),
            P("dp", None, "pipe"),
            P("pipe", None),
            P("pipe", None),
            P("pipe", None),
            P("pipe"),
            P("pipe", None),
            P("pipe"),
            P("pipe", "dp"),
            P("pipe"),
            P("pipe", "dp"),
            P("pipe"),
        ),
        check_vma=False,
    )
```

```python
import functools

import jax
import jax.numpy as jnp
import numpy as np
from jax import lax
from jax.experimental import pallas as pl
from jax.experimental.pallas import tpu as pltpu
from jax.sharding import PartitionSpec as P

F32 = jnp.float32
BF16 = jnp.bfloat16
NORM_EPS = 1e-06
GELU_SCALE = 0.7978845608
GELU_CUBE = 0.044715
STEPS = 2
SLOTS = 4
VMEM_BYTES = 40 << 20

IN_VMEM = pl.BlockSpec(memory_space=pltpu.VMEM)
IN_ANY = pl.BlockSpec(memory_space=pl.ANY)
IN_SMEM = pl.BlockSpec(memory_space=pltpu.SMEM)


def lasting(microseconds):
    return pl.CostEstimate(flops=int(microseconds * 10e9), bytes_accessed=1, transcendentals=0)


ON, VALID, CROSSING, IMAGE, PLACE, FORWARD, BACKWARD, ORDER, MIXED_FAR, GRAD_FAR = range(10)
LAYER, HALF, ME, LATE, HOPS = range(5)

JOBS = [
    [(0, 0, 0, 0), (1, 1, 1, 1), (2, 2, 2, 2), (3, 3, 3, 3)],
    [(0, 3, -1, 3), (1, 1, 1, 1), (2, 0, 2, 0), (3, 2, 3, 2)],
    [(0, -1, -1, -1), (1, 2, -1, 2), (2, 0, 2, 0), (3, 1, 3, 1), (-1, 3, 0, 3)],
    [(0, -1, -1, -1), (1, -1, -1, -1), (2, 0, -1, 0), (3, 1, 3, 1), (-1, 2, 0, 2), (-1, 3, 1, 3)],
    [(0, -1, -1, -1), (1, -1, -1, -1), (2, 0, -1, 0), (3, 1, -1, 1), (-1, 2, 0, 2), (-1, 3, 1, 3), (-1, -1, 2, -1)],
]
MOST = 8
JOB_TABLE = np.full((len(JOBS), 4, MOST), -1, np.int32)
for _hops, _rows in enumerate(JOBS):
    for _tick, _row in enumerate(_rows):
        JOB_TABLE[_hops, :, _tick] = _row
TICK_TABLE = np.array([len(_rows) for _rows in JOBS], np.int32)


def flipped(block, axis, distance):
    count = lax.axis_size(axis)
    route = [(i, i ^ distance) for i in range(count) if i ^ distance < count]
    return lax.ppermute(block, axis, route)


def mm(left, right):
    return lax.dot_general(left, right, (((1,), (0,)), ((), ())), preferred_element_type=F32)


def mm_nt(left, right):
    return lax.dot_general(left, right, (((1,), (1,)), ((), ())), preferred_element_type=F32)


def gelu_pair(pre):
    square = pre * pre
    gate = 0.5 + 0.5 * jnp.tanh(pre * (GELU_SCALE + (GELU_SCALE * GELU_CUBE) * square))
    value = pre * gate
    slope = gate + value * (1.0 - gate) * (2 * GELU_SCALE + (6 * GELU_SCALE * GELU_CUBE) * square)
    return value.astype(BF16), slope.astype(BF16)


def normalised(hidden):
    centred = hidden - jnp.mean(hidden, axis=-1, keepdims=True)
    scale = lax.rsqrt(jnp.mean(centred * centred, axis=-1, keepdims=True) + NORM_EPS)
    return centred * scale, scale


def launch(body, ins, specs, after, **options):
    first = len(ins)

    def trimmed(*refs):
        body(*refs[:first], *refs[first + len(after):])

    return pl.pallas_call(trimmed, in_specs=specs + [IN_ANY] * len(after), **options)(*ins, *after)


def table_body(jobs, ticks, valid, skip, tab, ticks_o):
    section = lax.axis_index("pipe")
    layer, half, me = section // 2, section % 2, lax.axis_index("dp")
    total = valid.shape[1]
    far = layer == 1
    firsts = [valid[0, i] * skip[0, i] for i in range(total)]
    seconds = [valid[0, i] * skip[1, i] for i in range(total)]
    kinds = [jnp.where(a * b == 1, 0, jnp.where(b == 1, 1, jnp.where(a == 1, 2, 3))) for a, b in zip(firsts, seconds)]
    crossing = sum(a * b for a, b in zip(firsts, seconds))
    hops = (crossing + 1) // 2
    for i in range(total):
        place = sum(((kinds[j] < kinds[i]) if j > i else (kinds[j] <= kinds[i])).astype(jnp.int32) for j in range(total) if j != i)
        tab[ORDER, place] = i
        tab[MIXED_FAR, place] = 1 - firsts[i] * (1 - seconds[i])
        tab[GRAD_FAR, place] = seconds[i] * (1 - firsts[i])

        @pl.when(place % 2 == half)
        def _():
            slot = place // 2
            tab[ON, slot] = jnp.where(far, seconds[i], firsts[i])
            tab[VALID, slot] = valid[0, i]
            tab[CROSSING, slot] = firsts[i] * seconds[i]
            tab[IMAGE, slot] = i

    tab[PLACE, LAYER] = layer
    tab[PLACE, HALF] = half
    tab[PLACE, ME] = me
    tab[PLACE, LATE] = jnp.where(far, -1, hops - 1)
    tab[PLACE, HOPS] = hops
    ticks_o[0] = ticks[0, hops]
    for tick in range(MOST):
        tab[FORWARD, tick] = jobs[hops * 4 + layer, tick]
        tab[BACKWARD, tick] = jobs[hops * 4 + 2 + layer, tick]


KEPT = ("slab0", "slab1", "slab23", "z", "gz", "zt", "gt", "h0", "h1", "n2", "f", "dq", "da", "db", "vec")


def tick_body(late_call, *refs):
    refs = list(refs)
    tick_ref = None if late_call else refs.pop(0)
    (tab, images, cots, recv, own_up, got_up, own_down, got_down,
     up_w, up_t, down_w, down_t, up_col, down_col, u_row, w_row, gains, shifts,
     send_o, slab0, slab1, slab23, z_o, gz_o, zt_o, gt_o, h0_o, h1_o, n2_o, f_o, dq_o, da_o, db_o, vec_o,
     up_v, down_v, raw_v, e_v, h0_v, h1_v, n2_v, z_v, gz_v, zt_v, gt_v, dq_v, acc_v, out_v, part_v, da_v, db_v, vec_v,
     w_sems, in_sems, load_sems, slab_sems, keep_sems, back_sems) = refs
    far = tab[PLACE, LAYER] == 1
    half = tab[PLACE, HALF]
    section = tab[PLACE, LAYER] * 2 + half
    slabs = (slab0, slab1, slab23.at[0], slab23.at[1])
    patches, channels = raw_v.shape[1:]
    rows = h0_v.shape[0]
    ff = up_v.shape[1]
    hidden_t = zt_v.shape[0]
    width = ff // STEPS
    part = channels // len(slabs)
    if late_call:
        f_job = jnp.int32(-1)
        b_job = tab[PLACE, LATE]
    else:
        f_job = tab[FORWARD, tick_ref[0]]
        b_job = tab[BACKWARD, tick_ref[0]]
    f_slot = jnp.maximum(f_job, 0)
    b_slot = jnp.maximum(b_job, 0)
    f_on = (f_job >= 0) & (tab[ON, f_slot] == 1)
    b_on = (b_job >= 0) & (tab[ON, b_slot] == 1)
    any_on = f_on | b_on

    def weight_copies(step):
        size = channels // 2
        cols = pl.ds(pl.multiple_of(step * width, width), width)
        own = pl.ds(pl.multiple_of(half * size, 16), size)
        rest = pl.ds(pl.multiple_of((1 - half) * size, 16), size)
        local = pl.ds(pl.multiple_of((step % (STEPS // 2)) * width, width), width)
        return (lambda: pltpu.make_async_copy(own_up.at[:, cols], up_v.at[own, cols], w_sems.at[0, step]),
                lambda: pltpu.make_async_copy(got_up.at[:, cols], up_v.at[rest, cols], w_sems.at[1, step]),
                lambda: pltpu.make_async_copy(own_down.at[local, :], down_v.at[cols, :], w_sems.at[2, step]),
                lambda: pltpu.make_async_copy(got_down.at[local, :], down_v.at[cols, :], w_sems.at[2, step]))

    def start_up(step):
        own, rest, _, _ = weight_copies(step)
        own().start()
        rest().start()

    def start_down(step):
        _, _, mine, theirs = weight_copies(step)

        @pl.when(step // (STEPS // 2) == half)
        def _():
            mine().start()

        @pl.when(step // (STEPS // 2) != half)
        def _():
            theirs().start()

    def await_up(step):
        own, rest, _, _ = weight_copies(step)
        own().wait()
        rest().wait()

    def await_down(step):
        weight_copies(step)[2]().wait()

    def fetch(kind, job, slot, crossed, source, target):
        @pl.when((job >= 0) & crossed)
        def _():
            pltpu.make_async_copy(recv, target, in_sems.at[kind]).start()

        @pl.when((job >= 0) & jnp.logical_not(crossed))
        def _():
            pltpu.make_async_copy(source.at[tab[IMAGE, slot]], raw_v.at[kind], in_sems.at[kind]).start()

    def fetched(kind, job, slot, crossed, source, target):
        @pl.when((job >= 0) & crossed)
        def _():
            pltpu.make_async_copy(recv, target, in_sems.at[kind]).wait()

        @pl.when((job >= 0) & jnp.logical_not(crossed))
        def _():
            pltpu.make_async_copy(source.at[tab[IMAGE, slot]], raw_v.at[kind], in_sems.at[kind]).wait()
            target[pl.ds(rows - 16, 16), :] = jnp.zeros((16, channels), BF16)
            target[pl.ds(0, patches), :] = raw_v[kind]

    forward_in = (0, f_job, f_slot, far & (tab[CROSSING, f_slot] == 1), images, h0_v)
    backward_in = (1, b_job, b_slot, jnp.logical_not(far) & (tab[CROSSING, b_slot] == 1), cots, e_v)
    loads = ((gz_o, gz_v), (h1_o, h1_v), (gt_o, gt_v), (h0_o, h0_v), (zt_o, zt_v))

    def load(i):
        return pltpu.make_async_copy(loads[i][0].at[b_slot], loads[i][1], load_sems.at[i])

    def reload(i):
        @pl.when(jnp.logical_not(f_on))
        def _():
            load(i).wait()

    if not late_call:
        fetch(*forward_in)

    @pl.when(f_on)
    def _():
        for step in range(STEPS):
            start_up(step)
        for step in range(STEPS):
            start_down(step)

    fetch(*backward_in)

    @pl.when(b_on & jnp.logical_not(f_on))
    def _():
        load(0).start()
        start_down(0)
        start_up(0)

    def slab_copy(kind, slot, flip):
        return pltpu.make_async_copy(part_v.at[kind, section ^ flip], slabs[flip].at[kind, slot], slab_sems.at[kind, flip])

    def send_copy(kind):
        return pltpu.make_async_copy(out_v.at[kind], send_o, slab_sems.at[kind, len(slabs)])

    def deliver(kind, slot, sends):
        @pl.when(sends)
        def _():
            send_copy(kind).start()

        @pl.when(jnp.logical_not(sends & (tab[CROSSING, slot] == 1)))
        def _():
            whole = out_v[kind]
            upper = part_v.shape[2]
            for d in range(len(slabs)):
                part_v[kind, d, :, 0:part] = whole[:upper, d * part:(d + 1) * part]
                part_v[kind, d, 0:rows - upper, part:2 * part] = whole[upper:, d * part:(d + 1) * part]
            for flip in range(len(slabs)):
                slab_copy(kind, slot, flip).start()

    def delivered(kind, slot, sends):
        @pl.when(jnp.logical_not(sends & (tab[CROSSING, slot] == 1)))
        def _():
            for flip in range(len(slabs)):
                slab_copy(kind, slot, flip).wait()

        @pl.when(sends)
        def _():
            send_copy(kind).wait()

    saves = ((gz_v, gz_o), (zt_v, zt_o), (gt_v, gt_o), (h0_v, h0_o), (h1_v, h1_o), (z_v, z_o), (n2_v, n2_o))

    def save(i):
        return pltpu.make_async_copy(saves[i][0], saves[i][1].at[f_slot], keep_sems.at[i])

    def run_forward():
        h0 = h0_v[...].astype(F32)
        centred, _ = normalised(h0)
        n1 = (centred * gains[0:1, :] + shifts[0:1, :]).astype(BF16)
        value, slope = gelu_pair(mm(up_t[...], n1) + up_col[...])
        zt_v[...] = value
        gt_v[...] = slope
        h1 = (h0 + (mm(down_t[...], value) + down_col[...])).astype(BF16)
        h1_v[...] = h1
        h1 = h1.astype(F32)
        centred, _ = normalised(h1)
        n2_v[...] = (centred * gains[1:2, :] + shifts[1:2, :]).astype(BF16)
        save(6).start()

        @pl.when(jnp.logical_not(b_on))
        def _():
            for i in range(1, 5):
                save(i).start()

        for step in range(STEPS):
            await_up(step)
        value, slope = gelu_pair(mm(n2_v[...], up_v[...]) + u_row[...])
        z_v[...] = value
        gz_v[...] = slope
        save(5).start()

        @pl.when(jnp.logical_not(b_on))
        def _():
            save(0).start()

        for step in range(STEPS):
            await_down(step)
        out_v[0] = (h1 + w_row[...] + mm(z_v[...], down_v[...])).astype(BF16)

    def norm_back(hidden, dn, grad, row):
        centred, scale = normalised(hidden)
        vec_v[2 + row:3 + row, 0:channels] = jnp.sum(dn * centred, axis=0, keepdims=True)
        vec_v[4 + row:5 + row, 0:channels] = jnp.sum(dn, axis=0, keepdims=True)
        scaled = dn * gains[row:row + 1, :]
        along = jnp.mean(scaled * centred, axis=-1, keepdims=True)
        flat = jnp.mean(scaled, axis=-1, keepdims=True)
        return centred, grad + scale * (scaled - flat - centred * along)

    backs = ((e_v, f_o), (dq_v, dq_o), (da_v, da_o), (db_v, db_o), (vec_v, vec_o))

    def back(i):
        return pltpu.make_async_copy(backs[i][0], backs[i][1].at[b_slot], back_sems.at[i])

    def run_backward():
        back(0).start()
        grad = e_v[...].astype(F32)
        vec_v[...] = jnp.zeros_like(vec_v)
        vec_v[1:2, 0:channels] = jnp.sum(grad, axis=0, keepdims=True)
        acc_v[...] = jnp.zeros_like(acc_v)
        reload(0)

        @pl.when(jnp.logical_not(f_on))
        def _():
            await_down(0)
            await_up(0)
            for step in range(1, STEPS):
                start_down(step)
                start_up(step)
            for i in range(1, len(loads)):
                load(i).start()

        @pl.loop(0, STEPS)
        def _(step):
            cols = pl.ds(pl.multiple_of(step * width, width), width)

            @pl.when(jnp.logical_not(f_on) & (step > 0))
            def _():
                await_down(step)
                await_up(step)

            dq = (mm_nt(e_v[...], down_v[cols, :]) * gz_v[:, cols].astype(F32)).astype(BF16)
            dq_v[:, cols] = dq
            vec_v[0:1, cols] = jnp.sum(dq.astype(F32), axis=0, keepdims=True)
            acc_v[...] += mm_nt(dq, up_v[:, cols])

        back(1).start()
        reload(1)
        _, grad = norm_back(h1_v[...].astype(F32), acc_v[...], grad, 1)
        f1 = grad.astype(BF16)
        reload(2)
        dq = (mm(down_w[...], f1) * gt_v[...].astype(F32)).astype(BF16)
        reload(3)
        centred, grad = norm_back(h0_v[...].astype(F32), mm(up_w[...], dq), f1.astype(F32), 0)
        out_v[1] = grad.astype(BF16)
        deliver(1, b_slot, far)
        n1 = (centred * gains[0:1, :] + shifts[0:1, :]).astype(BF16)
        reload(4)
        da_v[...] = mm_nt(n1, dq)
        db_v[...] = mm_nt(f1, zt_v[...])
        ones = jnp.ones((8, channels), BF16)
        vec_v[6:7, 0:hidden_t] = mm_nt(ones, dq)[0:1]
        vec_v[7:8, 0:rows] = mm_nt(ones, f1)[0:1]
        for i in range(2, 5):
            back(i).start()

    near = jnp.logical_not(far)

    if not late_call:
        fetched(*forward_in)

        @pl.when(f_on)
        def _():
            run_forward()

        @pl.when((f_job >= 0) & jnp.logical_not(f_on))
        def _():
            out_v[0] = h0_v[...] * tab[VALID, f_slot].astype(F32).astype(BF16)

        @pl.when(f_job >= 0)
        def _():
            deliver(0, f_slot, near)

    fetched(*backward_in)

    @pl.when(b_on)
    def _():
        run_backward()

    @pl.when((b_job >= 0) & jnp.logical_not(b_on))
    def _():
        out_v[1] = e_v[...] * tab[VALID, b_slot].astype(F32).astype(BF16)
        deliver(1, b_slot, far)

    @pl.when(b_job >= 0)
    def _():
        delivered(1, b_slot, far)

    @pl.when(b_on)
    def _():
        for i in range(5):
            back(i).wait()

    if not late_call:
        @pl.when(f_job >= 0)
        def _():
            delivered(0, f_slot, near)

        @pl.when(f_on)
        def _():
            save(5).wait()
            save(6).wait()

        @pl.when(f_on & jnp.logical_not(b_on))
        def _():
            for i in range(5):
                save(i).wait()


def parcel_rows(patches, hidden_t):
    spans = {}
    row = hidden_t // 2
    for name, height in (("up_bias", 1), ("down_bias", 1), ("w", 1), ("gain", 1), ("shift", 1), ("u", 2)):
        spans[name] = row
        row += height
    return spans, -(-row // 16) * 16


def parcel_body(spans, up, down, up_bias, down_bias, u, w, gain, shift, out, all_v):
    hidden_t = up.shape[1]
    lanes = all_v.shape[1]
    all_v[...] = jnp.zeros_like(all_v)
    all_v[0:up.shape[0], 0:hidden_t] = up[...].astype(F32)
    all_v[0:down.shape[0], hidden_t:hidden_t + down.shape[1]] = down[...].astype(F32)
    for name, part in (("up_bias", up_bias), ("down_bias", down_bias), ("w", w), ("gain", gain), ("shift", shift)):
        row = part[...].astype(F32).reshape(1, -1)
        all_v[spans[name]:spans[name] + 1, 0:row.shape[1]] = row
    row = u[...].astype(F32).reshape(1, -1)
    for step in range(row.shape[1] // lanes):
        all_v[spans["u"] + step:spans["u"] + step + 1, :] = row[:, step * lanes:(step + 1) * lanes]
    out[...] = all_v[...].astype(BF16)


def parcel(spans, height, parts):
    channels = parts[6].shape[1]
    return pl.pallas_call(
        functools.partial(parcel_body, spans),
        out_shape=jax.ShapeDtypeStruct((height, channels), BF16),
        in_specs=[IN_VMEM] * len(parts),
        out_specs=IN_VMEM,
        scratch_shapes=[pltpu.VMEM((height, channels), F32)],
        cost_estimate=lasting(0.1),
        name="parcel",
    )(*parts)


def prep_body(spans, patches, tab, own_i, got_i, up_w, up_t, down_w, down_t, up_col, down_col, u_row, w_row, gains, shifts, up_v, down_v):
    first = tab[PLACE, HALF] == 0
    own = own_i[...].astype(F32)
    got = got_i[...].astype(F32)
    halves = jnp.where(first, own, got), jnp.where(first, got, own)
    hidden_t = up_w.shape[1]
    lanes = own.shape[1]

    def column(row):
        return jnp.broadcast_to(row, (8, row.shape[1])).T[:, 0:1]

    up_v[...] = jnp.zeros_like(up_v)
    down_v[...] = jnp.zeros_like(down_v)
    down_col[...] = jnp.zeros_like(down_col)
    for side, half in enumerate(halves):
        size = patches // 2
        up_v[side * size:(side + 1) * size, :] = half[0:size, 0:hidden_t]
        down_col[side * size:(side + 1) * size, :] = column(half[spans["down_bias"]:spans["down_bias"] + 1, 0:size])
        size = hidden_t // 2
        down_v[side * size:(side + 1) * size, 0:patches] = half[0:size, hidden_t:hidden_t + patches]
        up_col[side * size:(side + 1) * size, :] = column(half[spans["up_bias"]:spans["up_bias"] + 1, 0:size])
        size = w_row.shape[1] // 2
        w_row[:, side * size:(side + 1) * size] = half[spans["w"]:spans["w"] + 1, 0:size]
        gains[side:side + 1, :] = half[spans["gain"]:spans["gain"] + 1, :]
        shifts[side:side + 1, :] = half[spans["shift"]:spans["shift"] + 1, :]
        steps = u_row.shape[1] // 2 // lanes
        for step in range(steps):
            at = (side * steps + step) * lanes
            u_row[:, at:at + lanes] = half[spans["u"] + step:spans["u"] + step + 1, :]
    up_w[...] = up_v[...].astype(BF16)
    up_t[...] = up_v[...].T.astype(BF16)
    down_w[...] = down_v[...].astype(BF16)
    down_t[...] = down_v[...].T.astype(BF16)


def prep(spans, patches, rows, hidden_t, ff, tab, own, got):
    channels = own.shape[1]
    names = ("up_w", "up_t", "down_w", "down_t", "up_col", "down_col", "u_row", "w_row", "gains", "shifts")
    sizes = [(rows, hidden_t), (hidden_t, rows), (hidden_t, rows), (rows, hidden_t), (hidden_t, 1), (rows, 1),
             (1, ff), (1, channels), (2, channels), (2, channels)]
    out = pl.pallas_call(
        functools.partial(prep_body, spans, patches),
        out_shape=[jax.ShapeDtypeStruct(size, BF16 if i < 4 else F32) for i, size in enumerate(sizes)],
        in_specs=[IN_SMEM] + [IN_VMEM] * 2,
        out_specs=[IN_VMEM] * len(sizes),
        scratch_shapes=[pltpu.VMEM((rows, hidden_t), F32), pltpu.VMEM((hidden_t, rows), F32)],
        compiler_params=pltpu.CompilerParams(vmem_limit_bytes=VMEM_BYTES),
        cost_estimate=lasting(0.1),
        name="prep",
    )(tab, own, got)
    return dict(zip(names, out))


def tick_call(tick, tab, images, cots, recv, w, kept, after=()):
    patches, channels = images.shape[1:]
    rows = recv.shape[0]
    ff = w["own_up"].shape[1]
    hidden_t = w["up_t"].shape[0]
    sections = 4
    shape = jax.ShapeDtypeStruct
    upper = -(-rows // 32) * 16
    slab = shape((2, SLOTS, upper, 2 * channels // sections), BF16)
    wide = shape((SLOTS, rows, ff), BF16)
    tall = shape((SLOTS, hidden_t, channels), BF16)
    plain = shape((SLOTS, rows, channels), BF16)
    shapes = [shape((rows, channels), BF16), slab, slab, shape((2,) + slab.shape, BF16)] + [wide, wide, tall, tall, plain, plain, plain, plain, wide,
              shape((SLOTS, rows, hidden_t), F32), shape((SLOTS, rows, hidden_t), F32), shape((SLOTS, 8, ff), F32)]
    names = ("own_up", "got_up", "own_down", "got_down", "up_w", "up_t", "down_w", "down_t", "up_col", "down_col", "u_row", "w_row", "gains", "shifts")
    ins = [tab, images, cots, recv] + [w[k] for k in names]
    specs = [IN_SMEM] + [IN_ANY] * 7 + [IN_VMEM] * 10
    if tick is not None:
        ins.insert(0, tick.reshape(1))
        specs.insert(0, IN_SMEM)
    ins += list(after)
    specs += [IN_ANY] * len(after)
    first = len(ins)
    passed = 0
    aliases = {}
    if kept is not None:
        passed = len(kept)
        aliases = {first + i: 1 + i for i in range(passed)}
        ins += list(kept)
        specs += [IN_ANY] * passed

    def trimmed(*refs):
        tick_body(tick is None, *refs[:first - len(after)], *refs[first + passed:])

    vmem = pltpu.VMEM
    line = vmem((rows, channels), BF16)
    broad = vmem((rows, ff), BF16)
    high = vmem((hidden_t, channels), BF16)
    dma = pltpu.SemaphoreType.DMA
    out = pl.pallas_call(
        trimmed,
        out_shape=shapes,
        in_specs=specs,
        out_specs=[IN_ANY] * len(shapes),
        input_output_aliases=aliases,
        scratch_shapes=[vmem((channels, ff), BF16), vmem((ff, channels), BF16), vmem((2, patches, channels), BF16), line, line, line, line,
                        broad, broad, high, high, broad, vmem((rows, channels), F32), vmem((2, rows, channels), BF16),
                        vmem((2, sections, upper, 2 * channels // sections), BF16),
                        vmem((rows, hidden_t), F32), vmem((rows, hidden_t), F32), vmem((8, ff), F32),
                        dma((3, STEPS)), dma((2,)), dma((5,)), dma((2, sections + 1)), dma((7,)), dma((5,))],
        compiler_params=pltpu.CompilerParams(vmem_limit_bytes=VMEM_BYTES),
        cost_estimate=lasting(8),
        name="tick" if tick is not None else "late_tick",
    )(*ins)
    return out[0], tuple(out[1:])


def position(relative, bits):
    place = 0
    for bit in bits:
        place = place * 2 + ((relative >> bit) & 1)
    return place


def down_grad_body(chunks, count, orders, aligned, tab, f_i, z_i, rider_i, *refs):
    outs, made, (f_v, ft_v, z_v, f_sems, z_sems, out_sems) = refs[:2 * chunks], refs[2 * chunks:4 * chunks], refs[4 * chunks:]
    half = tab[PLACE, HALF]
    me = tab[PLACE, ME]
    width = outs[0].shape[-1]
    channels = f_i.shape[2]
    rows = f_i.shape[1]
    size = z_i.shape[2] // 2
    tile = width
    piece = channels // count
    extra = rider_i.shape[1] // count if aligned else 0

    def z_copy(slot, which):
        first = pl.multiple_of(jnp.where(half == which % 2, 1, 0) * size + which // 2 * width, 128)
        return pltpu.make_async_copy(z_i.at[slot, :, pl.ds(first, width)], z_v.at[which, pl.ds(slot * rows, rows), :], z_sems.at[which, slot])

    def f_copy(slot):
        return pltpu.make_async_copy(f_i.at[slot], f_v.at[pl.ds(slot * rows, rows), :], f_sems.at[slot])

    for slot in range(SLOTS):
        @pl.when(tab[ON, slot] == 1)
        def _():
            f_copy(slot).start()

        @pl.when(tab[ON, slot] != 1)
        def _():
            f_v[pl.ds(slot * rows, rows), :] = jnp.zeros((rows, channels), BF16)

    for which in range(2 * chunks):
        for slot in range(SLOTS):
            @pl.when(tab[ON, slot] == 1)
            def _():
                z_copy(slot, which).start()

            @pl.when(tab[ON, slot] != 1)
            def _():
                z_v[which, pl.ds(slot * rows, rows), :] = jnp.zeros((rows, width), BF16)

    for slot in range(SLOTS):
        @pl.when(tab[ON, slot] == 1)
        def _():
            f_copy(slot).wait()

    ft_v[...] = f_v[...].T
    copies = [pltpu.make_async_copy(made[which], outs[which], out_sems.at[which]) for which in range(2 * chunks)]
    for which, out in enumerate(made):
        for slot in range(SLOTS):
            @pl.when(tab[ON, slot] == 1)
            def _():
                z_copy(slot, which).wait()

        each = piece + (extra if which < 2 else 0)
        first = [pl.multiple_of(position(d ^ me, orders[which // 2]) * each, 16) for d in range(count)]

        @pl.loop(0, width // tile)
        def _(step):
            cols = pl.ds(pl.multiple_of(step * tile, tile), tile)
            total = mm(ft_v[...], z_v[which, :, cols]).astype(BF16)
            if aligned:
                for d in range(count):
                    out[pl.ds(first[d], piece), cols] = total[d * piece:(d + 1) * piece]
            else:
                out[:, cols] = total

        if extra and which < 2:
            for d in range(count):
                out[pl.ds(first[d] + piece, extra), :] = rider_i[which, d * extra:(d + 1) * extra, :]

        copies[which].start()

    for copy in copies:
        copy.wait()


def up_grad_body(chunks, height, count, orders, aligned, tab, n_i, dq_i, *refs):
    outs, made, (n_v, nt_v, dq_v, n_sems, dq_sems, out_sems) = refs[:2 * chunks], refs[2 * chunks:4 * chunks], refs[4 * chunks:]
    half = tab[PLACE, HALF]
    me = tab[PLACE, ME]
    rows = n_i.shape[1]
    size = n_i.shape[2] // 2
    ff = dq_i.shape[2]

    def n_copy(slot):
        return pltpu.make_async_copy(n_i.at[slot], n_v.at[pl.ds(slot * rows, rows), :], n_sems.at[slot])

    def dq_copy(side, slot):
        cols = pl.ds(side * (ff // 2), ff // 2)
        return pltpu.make_async_copy(dq_i.at[slot, :, cols], dq_v.at[pl.ds(slot * rows, rows), cols], dq_sems.at[side, slot])

    for slot in range(SLOTS):
        @pl.when(tab[ON, slot] == 1)
        def _():
            n_copy(slot).start()

        @pl.when(tab[ON, slot] != 1)
        def _():
            n_v[pl.ds(slot * rows, rows), :] = jnp.zeros((rows, 2 * size), BF16)
            dq_v[pl.ds(slot * rows, rows), :] = jnp.zeros((rows, ff), BF16)

    for side in range(2):
        for slot in range(SLOTS):
            @pl.when(tab[ON, slot] == 1)
            def _():
                dq_copy(side, slot).start()

    for slot in range(SLOTS):
        @pl.when(tab[ON, slot] == 1)
        def _():
            n_copy(slot).wait()

    turned = n_v[...].T
    for fixed in range(2):
        side = jnp.where(half == fixed, 1, 0)
        for chunk in range(chunks):
            first = fixed * size + chunk * height
            nt_v[chunk, pl.ds(pl.multiple_of(side * height, 16), height), :] = turned[first:first + height]

    piece = ff // count if aligned else 384
    copies = [pltpu.make_async_copy(made[i], outs[i], out_sems.at[i]) for i in range(2 * chunks)]
    for chunk in range(chunks):
        theirs_v, mine_v = made[2 * chunk:2 * chunk + 2]
        for side in range(2):
            if chunk == 0:
                for slot in range(SLOTS):
                    @pl.when(tab[ON, slot] == 1)
                    def _():
                        dq_copy(side, slot).wait()

            @pl.loop(side * (ff // piece // 4), (side + 1) * (ff // piece // 4))
            def _(pair):
                cols = pl.ds(pl.multiple_of(pair * 2 * piece, 128), 2 * piece)
                total = mm(nt_v[chunk], dq_v[:, cols]).astype(BF16)
                if not aligned:
                    theirs_v[:, cols] = total[:height]
                    mine_v[:, cols] = total[height:]
                    return
                for i in range(2):
                    place = pl.ds(pl.multiple_of(position((2 * pair + i) ^ me, orders[chunk]) * height, 16), height)
                    theirs_v[place, :] = total[:height, i * piece:(i + 1) * piece]
                    mine_v[place, :] = total[height:, i * piece:(i + 1) * piece]

        copies[2 * chunk].start()
        copies[2 * chunk + 1].start()

    for copy in copies:
        copy.wait()


def arranged(pieces, bits):
    count = pieces.shape[0]
    order = [0] * count
    for relative in range(count):
        order[position(relative, bits)] = relative
    return jnp.take(pieces, jnp.array(order) ^ lax.axis_index("dp"), axis=0)


def down_grad_call(chunks, count, orders, tab, f, z, rider, after):
    slots, rows, channels = f.shape
    width = z.shape[2] // 2 // chunks
    piece = channels // count
    aligned = piece % 16 == 0
    extra = rider.shape[1] if aligned else 0
    shapes = [(channels + (extra if i == 0 else 0), width) for i in range(chunks)]
    out = launch(
        functools.partial(down_grad_body, chunks, count, orders, aligned), [tab, f, z, rider], [IN_SMEM, IN_ANY, IN_ANY, IN_VMEM], after,
        out_shape=[jax.ShapeDtypeStruct(shapes[i // 2], BF16) for i in range(2 * chunks)],
        out_specs=[IN_ANY] * (2 * chunks),
        scratch_shapes=[pltpu.VMEM(shapes[i // 2], BF16) for i in range(2 * chunks)]
                       + [pltpu.VMEM((slots * rows, channels), BF16), pltpu.VMEM((channels, slots * rows), BF16),
                          pltpu.VMEM((2 * chunks, slots * rows, width), BF16),
                          pltpu.SemaphoreType.DMA((slots,)), pltpu.SemaphoreType.DMA((2 * chunks, slots)), pltpu.SemaphoreType.DMA((2 * chunks,))],
        compiler_params=pltpu.CompilerParams(vmem_limit_bytes=VMEM_BYTES),
        cost_estimate=lasting(9),
        name="down_grad",
    )
    if not aligned:
        out = [arranged(part.reshape(count, piece, width), orders[i // 2]).reshape(part.shape) for i, part in enumerate(out)]
    return [out[2 * i:2 * i + 2] for i in range(chunks)]


def up_grad_call(chunks, count, orders, tab, n, dq, after):
    slots, rows, channels = n.shape
    ff = dq.shape[2]
    height = channels // 2 // chunks
    piece = ff // count
    aligned = piece % 128 == 0
    shape = (count * height, piece) if aligned else (height, ff)
    out = launch(
        functools.partial(up_grad_body, chunks, height, count, orders, aligned), [tab, n, dq], [IN_SMEM, IN_ANY, IN_ANY], after,
        out_shape=[jax.ShapeDtypeStruct(shape, BF16)] * (2 * chunks),
        out_specs=[IN_ANY] * (2 * chunks),
        scratch_shapes=[pltpu.VMEM(shape, BF16)] * (2 * chunks)
                       + [pltpu.VMEM((slots * rows, channels), BF16), pltpu.VMEM((chunks, 2 * height, slots * rows), BF16),
                          pltpu.VMEM((slots * rows, ff), BF16),
                          pltpu.SemaphoreType.DMA((slots,)), pltpu.SemaphoreType.DMA((2, slots)), pltpu.SemaphoreType.DMA((2 * chunks,))],
        compiler_params=pltpu.CompilerParams(vmem_limit_bytes=VMEM_BYTES),
        cost_estimate=lasting(9),
        name="up_grad",
    )
    if not aligned:
        out = [arranged(jnp.swapaxes(part.reshape(height, count, piece), 0, 1), orders[i // 2]).reshape(count * height, piece) for i, part in enumerate(out)]
    return [out[2 * i:2 * i + 2] for i in range(chunks)]


def halved_body(mine, got, kept, sent):
    middle = kept.shape[0]
    low, high = pl.ds(0, middle), pl.ds(middle, middle)
    sent[...] = (mine[high, :].astype(F32) + got[high, :].astype(F32)).astype(BF16)
    kept[...] = (mine[low, :].astype(F32) + got[low, :].astype(F32)).astype(BF16)


def halved(mine, got, after):
    size, width = mine.shape
    return launch(halved_body, [mine, got], [IN_VMEM] * 2, after,
                  out_shape=[jax.ShapeDtypeStruct((size // 2, width), BF16)] * 2, out_specs=[IN_VMEM] * 2,
                  compiler_params=pltpu.CompilerParams(vmem_limit_bytes=VMEM_BYTES), cost_estimate=lasting(2), name="halved")


def summed_body(kind, mine, got, *refs):
    total = mine[...].astype(F32) + got[...].astype(F32)
    if kind == "above":
        first, out = refs
        out[0:first.shape[0]] = first[...]
        out[first.shape[0]:] = total
    elif kind == "beside":
        first, out = refs
        out[:, 0:first.shape[1]] = first[...]
        out[:, first.shape[1]:] = total
    else:
        out, *rest = refs
        out[...] = total[:out.shape[0]]
        for rider in rest:
            rider[...] = total[out.shape[0]:].astype(BF16)


def summed(kind, mine, got, size, first, after):
    rows, width = mine.shape
    shape = jax.ShapeDtypeStruct
    ins = [mine, got]
    if kind == "above":
        shapes = [shape((first.shape[0] + rows, width), F32)]
    elif kind == "beside":
        shapes = [shape((rows, first.shape[1] + width), F32)]
    else:
        shapes = [shape((size, width), F32)] + [shape((rows - size, width), BF16)] * (rows > size)
    if first is not None:
        ins.append(first)
    return launch(functools.partial(summed_body, kind), ins, [IN_VMEM] * len(ins), after,
                  out_shape=shapes, out_specs=[IN_VMEM] * len(shapes),
                  compiler_params=pltpu.CompilerParams(vmem_limit_bytes=VMEM_BYTES), cost_estimate=lasting(0.1), name="summed")


def packing(patches, hidden_t, channels, ff):
    spans = {}
    row = 0
    for name, height in (("token", -(-patches // 2 // 8) * 8), ("chan_up_bias", ff // 2 // channels), ("biases", 1), ("gain", 1), ("shift", 1)):
        spans[name] = row
        row += height
    return spans, -(-row // 128) * 128, channels


def pack_body(spans, patches, tab, da_i, db_i, vec_i, out, da_v, db_v, vec_v, both_v, sems):
    half = tab[PLACE, HALF]
    lanes = both_v.shape[-1]
    hidden_t = db_v.shape[2]
    upper = patches // 2
    sources = ((da_i, da_v), (db_i, db_v), (vec_i, vec_v))

    def copy(kind, slot):
        return pltpu.make_async_copy(sources[kind][0].at[slot], sources[kind][1].at[slot], sems.at[kind, slot])

    for slot in range(SLOTS):
        @pl.when(tab[ON, slot] == 1)
        def _():
            for kind in range(3):
                copy(kind, slot).start()

        @pl.when(tab[ON, slot] != 1)
        def _():
            for _, buffer in sources:
                buffer[slot] = jnp.zeros(buffer.shape[1:], F32)

    for slot in range(SLOTS):
        @pl.when(tab[ON, slot] == 1)
        def _():
            for kind in range(3):
                copy(kind, slot).wait()

    da = (da_v[0] + da_v[1]) + (da_v[2] + da_v[3])
    db = (db_v[0] + db_v[1]) + (db_v[2] + db_v[3])
    vec = (vec_v[0] + vec_v[1]) + (vec_v[2] + vec_v[3])
    both_v[...] = jnp.zeros_like(both_v)
    ff = vec.shape[1]
    channels = spans["channels"]
    for side in range(2):
        at = spans["token"]
        both_v[side, at:at + upper, 0:hidden_t] = da[side * upper:(side + 1) * upper]
        block = db[:, side * (hidden_t // 2):(side + 1) * (hidden_t // 2)]
        both_v[side, at:at + upper, hidden_t:hidden_t + hidden_t // 2] = block[:upper]
        both_v[side, at:at + upper, hidden_t + hidden_t // 2:2 * hidden_t] = block[upper:patches]

        def line(name, row, first, length, left=0):
            at = spans[name]
            for step in range(-(-length // lanes)):
                size = min(lanes, length - step * lanes)
                both_v[side, at + step:at + step + 1, left:left + size] = vec[row:row + 1, first + step * lanes:first + step * lanes + size]

        line("chan_up_bias", 0, side * (ff // 2), ff // 2)
        line("biases", 1, side * (channels // 2), channels // 2)
        line("biases", 6, side * (hidden_t // 2), hidden_t // 2, channels // 2)
        line("biases", 7, side * upper, upper, channels // 2 + hidden_t // 2)
        line("gain", 2 + side, 0, channels)
        line("shift", 4 + side, 0, channels)
    out[0] = both_v[1 - half].astype(BF16)
    out[1] = both_v[half].astype(BF16)


def unpack_body(spans, patches, hidden_t, relative, tab, parts, gain_o, shift_o, up_o, up_bias_o, down_o, down_bias_o, chan_up_bias_o, chan_down_bias_o, all_v):
    size = parts.shape[1]
    for i, shift in enumerate(relative):
        first = pl.multiple_of((tab[PLACE, ME] ^ shift) * size, 8) if len(relative) > 1 else 0
        all_v[pl.ds(first, size), :] = parts[i].astype(F32)
    upper = patches // 2
    lanes = all_v.shape[1]
    at = spans["token"]
    up_o[...] = all_v[at:at + upper, 0:hidden_t]
    block = all_v[at:at + -(-upper // 8) * 8, hidden_t:2 * hidden_t]
    down_o[:, 0:upper] = block[:, :hidden_t // 2].T[:, :upper]
    down_o[:, upper:patches] = block[:, hidden_t // 2:].T[:, :upper]
    gain_o[...] = all_v[spans["gain"]:spans["gain"] + 1, :]
    shift_o[...] = all_v[spans["shift"]:spans["shift"] + 1, :]
    for step in range(chan_up_bias_o.shape[1] // lanes):
        at = spans["chan_up_bias"] + step
        chan_up_bias_o[:, step * lanes:(step + 1) * lanes] = all_v[at:at + 1, :]
    row = all_v[spans["biases"]:spans["biases"] + 1, :]
    first = chan_down_bias_o.shape[1]
    chan_down_bias_o[...] = row[:, :first]
    up_bias_o[...] = row[:, first:first + hidden_t // 2]
    down_bias_o[...] = row[:, first + hidden_t // 2:first + hidden_t // 2 + upper]


def unpack(spans, patches, hidden_t, channels, ff, relative, tab, parts, after):
    sizes = [(1, channels), (1, channels), (patches // 2, hidden_t), (1, hidden_t // 2), (hidden_t // 2, patches), (1, patches // 2), (1, ff // 2), (1, channels // 2)]
    return launch(
        functools.partial(unpack_body, spans, patches, hidden_t, relative), [tab, parts], [IN_SMEM, IN_VMEM], after,
        out_shape=[jax.ShapeDtypeStruct(size, F32) for size in sizes],
        out_specs=[IN_VMEM] * len(sizes),
        scratch_shapes=[pltpu.VMEM((parts.shape[0] * parts.shape[1], parts.shape[2]), F32)],
        compiler_params=pltpu.CompilerParams(vmem_limit_bytes=VMEM_BYTES),
        cost_estimate=lasting(2),
        name="unpack",
    )


def both_body(first, second, out):
    out[0:first.shape[0]] = first[...]
    out[first.shape[0]:] = second[...]


def both(first, second, after):
    shape = (2 * first.shape[0],) + first.shape[1:]
    return launch(both_body, [first, second], [IN_VMEM] * 2, after, out_shape=jax.ShapeDtypeStruct(shape, first.dtype), out_specs=IN_VMEM,
                  compiler_params=pltpu.CompilerParams(vmem_limit_bytes=VMEM_BYTES), cost_estimate=lasting(2), name="both")


def split_body(both, first_o, second_o, sems):
    copies = [pltpu.make_async_copy(both.at[i], target, sems.at[i]) for i, target in enumerate((first_o, second_o))]
    for copy in copies:
        copy.start()
    for copy in copies:
        copy.wait()


def split(both, after):
    return launch(split_body, [both], [IN_ANY], after, out_shape=[jax.ShapeDtypeStruct(both.shape[1:], both.dtype)] * 2,
                  out_specs=[IN_VMEM] * 2, scratch_shapes=[pltpu.SemaphoreType.DMA((2,))],
                  compiler_params=pltpu.CompilerParams(vmem_limit_bytes=VMEM_BYTES), cost_estimate=lasting(0.1), name="split")


def place_body(tab, here, beside, across, corner, mixed_o, grad_o, mixed_v, grad_v, sems):
    layer = tab[PLACE, LAYER]
    half = tab[PLACE, HALF]
    sources = (here, beside, across, corner)
    places, width, patches = mixed_o.shape
    upper = mixed_v.shape[1]
    buffers = (mixed_v, grad_v)

    def copy(kind, place, source):
        return pltpu.make_async_copy(source.at[kind, place // 2], buffers[kind].at[tab[ORDER, place]], sems.at[kind, place])

    for place in range(places):
        for kind, row in enumerate((MIXED_FAR, GRAD_FAR)):
            which = jnp.where(tab[row, place] == layer, 0, 2) + jnp.where(half == place % 2, 0, 1)
            for i, source in enumerate(sources):
                @pl.when(which == i)
                def _():
                    copy(kind, place, source).start()

    for place in range(places):
        for kind in range(2):
            copy(kind, place, here).wait()

    @pl.loop(0, places)
    def _(i):
        for source, target in ((mixed_v, mixed_o), (grad_v, grad_o)):
            whole = jnp.concatenate([source[i, :, 0:width], source[i, :, width:2 * width]], 0)
            target[i] = whole.T[:, 0:patches]


def pack_call(spans, packed_rows, lanes, patches, channels, tab, da, db, vec, after):
    return launch(
        functools.partial(pack_body, dict(spans, channels=channels), patches), [tab, da, db, vec], [IN_SMEM] + [IN_ANY] * 3, after,
        out_shape=jax.ShapeDtypeStruct((2, packed_rows, lanes), BF16),
        out_specs=IN_VMEM,
        scratch_shapes=[pltpu.VMEM(da.shape, F32), pltpu.VMEM(db.shape, F32), pltpu.VMEM(vec.shape, F32),
                        pltpu.VMEM((2, packed_rows, lanes), F32), pltpu.SemaphoreType.DMA((3, SLOTS))],
        compiler_params=pltpu.CompilerParams(vmem_limit_bytes=VMEM_BYTES),
        cost_estimate=lasting(2.5),
        name="pack",
    )


def place_call(slot_count, patches, width, tab, slabs, after):
    out_shape = jax.ShapeDtypeStruct((slot_count, width, patches), BF16)
    buffer = pltpu.VMEM((slot_count,) + slabs[0].shape[2:], BF16)
    return launch(
        place_body, [tab] + list(slabs), [IN_SMEM] + [IN_ANY] * 4, after,
        out_shape=[out_shape, out_shape],
        out_specs=[IN_VMEM] * 2,
        scratch_shapes=[buffer, buffer, pltpu.SemaphoreType.DMA((2, slot_count))],
        compiler_params=pltpu.CompilerParams(vmem_limit_bytes=VMEM_BYTES),
        cost_estimate=lasting(4),
        name="place",
    )


def local(images, cotangent, valid_rows, skip_masks, norm_gain, norm_bias, token_up, token_up_bias, token_down,
          token_down_bias, chan_up, chan_up_bias, chan_down, chan_down_bias):
    count = lax.axis_size("dp")
    slot_count, patches, channels = images.shape
    rows = -(-patches // 16) * 16
    hidden_t = token_up.shape[1]
    ff = chan_up.shape[1]

    parcel_spans, height = parcel_rows(patches, hidden_t)
    own = parcel(parcel_spans, height, (token_up, token_down, token_up_bias, token_down_bias, chan_up_bias, chan_down_bias, norm_gain, norm_bias))
    got = flipped(own, "pipe", 1)
    got_up = flipped(chan_up, "pipe", 1)
    got_down = flipped(chan_down, "pipe", 1)

    tab, ticks = pl.pallas_call(
        table_body,
        out_shape=[jax.ShapeDtypeStruct((10, MOST), jnp.int32), jax.ShapeDtypeStruct((1,), jnp.int32)],
        in_specs=[IN_SMEM] * 4,
        out_specs=[IN_SMEM] * 2,
        cost_estimate=lasting(0.1),
        name="table",
    )(jnp.asarray(JOB_TABLE.reshape(-1, MOST)), jnp.asarray(TICK_TABLE[None, :]), valid_rows[None, :], skip_masks.T)

    weights = dict(prep(parcel_spans, patches, rows, hidden_t, ff, tab, own, got), own_up=chan_up, got_up=got_up, own_down=chan_down, got_down=got_down)
    blank = jnp.zeros((rows, channels), BF16)
    send, kept = tick_call(jnp.int32(0), tab, images, cotangent, blank, weights, None)

    def one(tick, carried):
        send, recv, kept = carried
        arriving = flipped(send, "pipe", 2)
        send, kept = tick_call(tick, tab, images, cotangent, recv, weights, kept)
        return send, arriving, kept

    _, last, kept = lax.fori_loop(1, ticks[0], one, (send, blank, kept))
    kept = dict(zip(KEPT, kept))

    chunks = 2
    bits = tuple(range(count.bit_length() - 1))
    other_bits = (bits[1], bits[0]) + bits[2:]
    orders = (bits, other_bits, bits, other_bits)
    spans, packed_rows, lanes = packing(patches, hidden_t, channels, ff)

    made = []

    def step(function, *arrays):
        out = function(*arrays, after=tuple(made))
        made[:] = jax.tree.leaves(out)[:1]
        return out

    pieces = [None] * (2 * chunks)
    moving = [None] * (2 * chunks)

    def begin(which, pair):
        pieces[which] = pair[1]
        moving[which] = flipped(pair[0], "pipe", 1)

    def advance(which, stage):
        pieces[which], sent = step(halved, pieces[which], moving[which])
        moving[which] = flipped(sent, "dp", 1 << orders[which][stage])

    def finished(which, kind, first=None):
        size = channels // count if which < chunks else channels // 2 // chunks
        return step(summed, kind, pieces[which], moving[which], size, first)

    _, late_kept = step(tick_call, None, tab, images, cotangent, last, weights, tuple(kept[k] for k in KEPT))
    made[:] = late_kept[:1]
    kept = dict(zip(KEPT, late_kept))
    over = flipped(kept["slab23"], "pipe", 2)
    beside = flipped(kept["slab1"], "pipe", 1)
    rider = step(pack_call, spans, packed_rows, lanes, patches, channels, tab, kept["da"], kept["db"], kept["vec"])
    made.append(beside)
    for i, pair in enumerate(step(down_grad_call, chunks, count, orders[:chunks], tab, kept["f"], kept["z"], rider)):
        begin(i, pair)
    advance(0, 0)
    advance(1, 0)
    for i, pair in enumerate(step(up_grad_call, chunks, count, orders[chunks:], tab, kept["n2"], kept["dq"])):
        begin(chunks + i, pair)
    advance(0, 1)
    advance(1, 1)
    advance(2, 0)
    advance(3, 0)
    across, turned = step(split, over)
    corner = flipped(turned, "pipe", 1)
    for stage in range(2, len(bits)):
        advance(0, stage)
        advance(1, stage)
    advance(2, 1)
    width = channels // 4
    mixed, input_grad = step(place_call, slot_count, patches, width, tab, (kept["slab0"], beside, across, corner))
    advance(3, 1)
    down_first, *small = finished(0, "alone")
    parts = small[0][None] if small else None
    relative = [0]
    gathered = list(reversed(bits)) if small else []

    def gather():
        nonlocal parts, relative
        if gathered:
            bit = gathered.pop(0)
            parts = step(both, parts, flipped(parts, "dp", 1 << bit))
            relative += [i ^ (1 << bit) for i in relative]

    chan_down_grad, = finished(1, "beside", down_first)
    gather()
    for stage in range(2, len(bits)):
        advance(2, stage)
        advance(3, stage)
    while gathered:
        gather()
    if parts is None:
        total = rider[1].astype(F32) + flipped(rider[0], "pipe", 1).astype(F32)
        for bit in bits:
            sent = lax.optimization_barrier(total.astype(BF16))
            total = sent.astype(F32) + flipped(sent, "dp", 1 << bit).astype(F32)
        parts = total[None]
    gain, shift, token_up_grad, up_bias, token_down_grad, down_bias, chan_up_bias_grad, chan_down_bias_grad = step(
        unpack, spans, patches, hidden_t, channels, ff, relative, tab, parts)
    up_first, = finished(2, "alone")
    chan_up_grad, = finished(3, "above", up_first)

    return (
        jnp.swapaxes(mixed, 1, 2),
        jnp.swapaxes(input_grad, 1, 2),
        gain,
        shift,
        token_up_grad,
        up_bias[0],
        token_down_grad,
        down_bias[0],
        chan_up_grad,
        chan_up_bias_grad[0],
        chan_down_grad.T,
        chan_down_bias_grad[0],
    )


def solution(mesh):
    placed = (
        P("dp", None, None),
        P("dp", None, None),
        P("dp"),
        P("dp", None),
        P("pipe", None),
        P("pipe", None),
        P("pipe", None),
        P("pipe"),
        P("pipe", None),
        P("pipe"),
        P("pipe", None),
        P("pipe"),
        P("pipe", None),
        P("pipe"),
    )
    return jax.shard_map(
        local,
        mesh=mesh,
        in_specs=placed,
        out_specs=(
            P("dp", None, "pipe"),
            P("dp", None, "pipe"),
            P("pipe", None),
            P("pipe", None),
            P("pipe", None),
            P("pipe"),
            P("pipe", None),
            P("pipe"),
            P("pipe", "dp"),
            P("pipe"),
            P("pipe", "dp"),
            P("pipe"),
        ),
        check_vma=False,
    )
```

```python
import functools

import jax
import jax.numpy as jnp
import numpy as np
from jax import lax
from jax.experimental import pallas as pl
from jax.experimental.pallas import tpu as pltpu
from jax.sharding import PartitionSpec as P

F32 = jnp.float32
BF16 = jnp.bfloat16
NORM_EPS = 1e-06
GELU_SCALE = 0.7978845608
GELU_CUBE = 0.044715
STEPS = 2
SLOTS = 4
VMEM_BYTES = 40 << 20

IN_VMEM = pl.BlockSpec(memory_space=pltpu.VMEM)
IN_ANY = pl.BlockSpec(memory_space=pl.ANY)
IN_SMEM = pl.BlockSpec(memory_space=pltpu.SMEM)


def lasting(microseconds):
    return pl.CostEstimate(flops=int(microseconds * 10e9), bytes_accessed=1, transcendentals=0)


ON, VALID, CROSSING, IMAGE, PLACE, FORWARD, BACKWARD, ORDER, MIXED_FAR, GRAD_FAR = range(10)
LAYER, HALF, ME, LATE, HOPS = range(5)

JOBS = [
    [(-1, -1, -1, -1), (0, 0, 0, 0), (1, 1, 1, 1), (2, 2, 2, 2), (3, 3, 3, 3)],
    [(0, -1, -1, -1), (1, 1, 1, 1), (2, 0, 2, 0), (3, 2, 3, 2), (-1, 3, 0, 3)],
    [(0, -1, -1, -1), (1, 2, -1, 2), (2, 0, 2, 0), (3, 1, 3, 1), (-1, 3, 0, 3)],
    [(0, -1, -1, -1), (1, -1, -1, -1), (2, 0, -1, 0), (3, 1, 3, 1), (-1, 2, 0, 2), (-1, 3, 1, 3)],
    [(0, -1, -1, -1), (1, -1, -1, -1), (2, 0, -1, 0), (3, 1, -1, 1), (-1, 2, 0, 2), (-1, 3, 1, 3), (-1, -1, 2, -1)],
]
MOST = 8
JOB_TABLE = np.full((len(JOBS), 4, MOST), -1, np.int32)
for _hops, _rows in enumerate(JOBS):
    for _tick, _row in enumerate(_rows):
        JOB_TABLE[_hops, :, _tick] = _row
TICK_TABLE = np.array([len(_rows) for _rows in JOBS], np.int32)


def flipped(block, axis, distance):
    count = lax.axis_size(axis)
    route = [(i, i ^ distance) for i in range(count) if i ^ distance < count]
    return lax.ppermute(block, axis, route)


def mm(left, right):
    return lax.dot_general(left, right, (((1,), (0,)), ((), ())), preferred_element_type=F32)


def mm_nt(left, right):
    return lax.dot_general(left, right, (((1,), (1,)), ((), ())), preferred_element_type=F32)


def gelu_pair(pre):
    square = pre * pre
    gate = 0.5 + 0.5 * jnp.tanh(pre * (GELU_SCALE + (GELU_SCALE * GELU_CUBE) * square))
    value = pre * gate
    slope = gate + value * (1.0 - gate) * (2 * GELU_SCALE + (6 * GELU_SCALE * GELU_CUBE) * square)
    return value.astype(BF16), slope.astype(BF16)


def normalised(hidden):
    centred = hidden - jnp.mean(hidden, axis=-1, keepdims=True)
    scale = lax.rsqrt(jnp.mean(centred * centred, axis=-1, keepdims=True) + NORM_EPS)
    return centred * scale, scale


def launch(body, ins, specs, after, **options):
    first = len(ins)

    def trimmed(*refs):
        body(*refs[:first], *refs[first + len(after):])

    return pl.pallas_call(trimmed, in_specs=specs + [IN_ANY] * len(after), **options)(*ins, *after)


def table_body(jobs, ticks, valid, skip, tab, ticks_o):
    section = lax.axis_index("pipe")
    layer, half, me = section // 2, section % 2, lax.axis_index("dp")
    total = valid.shape[1]
    far = layer == 1
    firsts = [valid[0, i] * skip[0, i] for i in range(total)]
    seconds = [valid[0, i] * skip[1, i] for i in range(total)]
    kinds = [jnp.where(a * b == 1, 0, jnp.where(b == 1, 1, jnp.where(a == 1, 2, 3))) for a, b in zip(firsts, seconds)]
    crossing = sum(a * b for a, b in zip(firsts, seconds))
    hops = (crossing + 1) // 2
    for i in range(total):
        place = sum(((kinds[j] < kinds[i]) if j > i else (kinds[j] <= kinds[i])).astype(jnp.int32) for j in range(total) if j != i)
        tab[ORDER, place] = i
        tab[MIXED_FAR, place] = 1 - firsts[i] * (1 - seconds[i])
        tab[GRAD_FAR, place] = seconds[i] * (1 - firsts[i])

        @pl.when(place % 2 == half)
        def _():
            slot = place // 2
            tab[ON, slot] = jnp.where(far, seconds[i], firsts[i])
            tab[VALID, slot] = valid[0, i]
            tab[CROSSING, slot] = firsts[i] * seconds[i]
            tab[IMAGE, slot] = i

    tab[PLACE, LAYER] = layer
    tab[PLACE, HALF] = half
    tab[PLACE, ME] = me
    tab[PLACE, LATE] = jnp.where(far | (hops == 1), -1, hops - 1)
    tab[PLACE, HOPS] = hops
    ticks_o[0] = ticks[0, hops]
    for tick in range(MOST):
        tab[FORWARD, tick] = jobs[hops * 4 + layer, tick]
        tab[BACKWARD, tick] = jobs[hops * 4 + 2 + layer, tick]


KEPT = ("slab0", "slab1", "slab23", "z", "gz", "zt", "gt", "h0", "h1", "n2", "f", "dq", "da", "db", "vec")


def tick_body(phases, *refs):
    late_call = phases == "last"
    first_call = phases == "first"
    refs = list(refs)
    tick_ref = None if late_call or first_call else refs.pop(0)
    (tab, images, cots, recv, own_up, got_up, own_down, got_down,
     up_w, up_t, down_w, down_t, up_col, down_col, u_row, w_row, gains, shifts,
     send_o, slab0, slab1, slab23, z_o, gz_o, zt_o, gt_o, h0_o, h1_o, n2_o, f_o, dq_o, da_o, db_o, vec_o,
     up_v, down_v, raw_v, e_v, h0_v, h1_v, n2_v, z_v, gz_v, zt_v, gt_v, dq_v, acc_v, out_v, part_v, da_v, db_v, vec_v,
     w_sems, in_sems, load_sems, slab_sems, keep_sems, back_sems) = refs
    far = tab[PLACE, LAYER] == 1
    half = tab[PLACE, HALF]
    section = tab[PLACE, LAYER] * 2 + half
    slabs = (slab0, slab1, slab23.at[0], slab23.at[1])
    patches, channels = raw_v.shape[1:]
    rows = h0_v.shape[0]
    ff = up_v.shape[1]
    hidden_t = zt_v.shape[0]
    width = ff // STEPS
    part = channels // len(slabs)
    if late_call:
        f_job = jnp.int32(-1)
        b_job = tab[PLACE, LATE]
    elif first_call:
        f_job = tab[FORWARD, 0]
        b_job = jnp.int32(-1)
    else:
        f_job = tab[FORWARD, tick_ref[0]]
        b_job = tab[BACKWARD, tick_ref[0]]
    f_slot = jnp.maximum(f_job, 0)
    b_slot = jnp.maximum(b_job, 0)
    f_on = (f_job >= 0) & (tab[ON, f_slot] == 1)
    b_on = (b_job >= 0) & (tab[ON, b_slot] == 1)
    any_on = f_on | b_on

    def weight_copies(step):
        size = channels // 2
        cols = pl.ds(pl.multiple_of(step * width, width), width)
        own = pl.ds(pl.multiple_of(half * size, 16), size)
        rest = pl.ds(pl.multiple_of((1 - half) * size, 16), size)
        local = pl.ds(pl.multiple_of((step % (STEPS // 2)) * width, width), width)
        return (lambda: pltpu.make_async_copy(own_up.at[:, cols], up_v.at[own, cols], w_sems.at[0, step]),
                lambda: pltpu.make_async_copy(got_up.at[:, cols], up_v.at[rest, cols], w_sems.at[1, step]),
                lambda: pltpu.make_async_copy(own_down.at[local, :], down_v.at[cols, :], w_sems.at[2, step]),
                lambda: pltpu.make_async_copy(got_down.at[local, :], down_v.at[cols, :], w_sems.at[2, step]))

    def start_up(step):
        own, rest, _, _ = weight_copies(step)
        own().start()
        rest().start()

    def start_down(step):
        _, _, mine, theirs = weight_copies(step)

        @pl.when(step // (STEPS // 2) == half)
        def _():
            mine().start()

        @pl.when(step // (STEPS // 2) != half)
        def _():
            theirs().start()

    def await_up(step):
        own, rest, _, _ = weight_copies(step)
        own().wait()
        rest().wait()

    def await_down(step):
        weight_copies(step)[2]().wait()

    def fetch(kind, job, slot, crossed, source, target):
        @pl.when((job >= 0) & crossed)
        def _():
            pltpu.make_async_copy(recv, target, in_sems.at[kind]).start()

        @pl.when((job >= 0) & jnp.logical_not(crossed))
        def _():
            pltpu.make_async_copy(source.at[tab[IMAGE, slot]], raw_v.at[kind], in_sems.at[kind]).start()

    def fetched(kind, job, slot, crossed, source, target):
        @pl.when((job >= 0) & crossed)
        def _():
            pltpu.make_async_copy(recv, target, in_sems.at[kind]).wait()

        @pl.when((job >= 0) & jnp.logical_not(crossed))
        def _():
            pltpu.make_async_copy(source.at[tab[IMAGE, slot]], raw_v.at[kind], in_sems.at[kind]).wait()
            target[pl.ds(rows - 16, 16), :] = jnp.zeros((16, channels), BF16)
            target[pl.ds(0, patches), :] = raw_v[kind]

    forward_in = (0, f_job, f_slot, far & (tab[CROSSING, f_slot] == 1), images, h0_v)
    backward_in = (1, b_job, b_slot, jnp.logical_not(far) & (tab[CROSSING, b_slot] == 1), cots, e_v)
    loads = ((gz_o, gz_v), (h1_o, h1_v), (gt_o, gt_v), (h0_o, h0_v), (zt_o, zt_v))

    def load(i):
        return pltpu.make_async_copy(loads[i][0].at[b_slot], loads[i][1], load_sems.at[i])

    def reload(i):
        @pl.when(jnp.logical_not(f_on))
        def _():
            load(i).wait()

    if not late_call:
        fetch(*forward_in)

    @pl.when(f_on)
    def _():
        for step in range(STEPS):
            start_up(step)
        for step in range(STEPS):
            start_down(step)

    fetch(*backward_in)

    @pl.when(b_on & jnp.logical_not(f_on))
    def _():
        load(0).start()
        start_down(0)
        start_up(0)

    def slab_copy(kind, slot, flip):
        return pltpu.make_async_copy(part_v.at[kind, section ^ flip], slabs[flip].at[kind, slot], slab_sems.at[kind, flip])

    def send_copy(kind):
        return pltpu.make_async_copy(out_v.at[kind], send_o, slab_sems.at[kind, len(slabs)])

    def deliver(kind, slot, sends):
        @pl.when(sends)
        def _():
            send_copy(kind).start()

        @pl.when(jnp.logical_not(sends & (tab[CROSSING, slot] == 1)))
        def _():
            whole = out_v[kind]
            upper = part_v.shape[2]
            for d in range(len(slabs)):
                part_v[kind, d, :, 0:part] = whole[:upper, d * part:(d + 1) * part]
                part_v[kind, d, 0:rows - upper, part:2 * part] = whole[upper:, d * part:(d + 1) * part]
            for flip in range(len(slabs)):
                slab_copy(kind, slot, flip).start()

    def delivered(kind, slot, sends):
        @pl.when(jnp.logical_not(sends & (tab[CROSSING, slot] == 1)))
        def _():
            for flip in range(len(slabs)):
                slab_copy(kind, slot, flip).wait()

        @pl.when(sends)
        def _():
            send_copy(kind).wait()

    saves = ((gz_v, gz_o), (zt_v, zt_o), (gt_v, gt_o), (h0_v, h0_o), (h1_v, h1_o), (z_v, z_o), (n2_v, n2_o))

    def save(i):
        return pltpu.make_async_copy(saves[i][0], saves[i][1].at[f_slot], keep_sems.at[i])

    def run_forward():
        h0 = h0_v[...].astype(F32)
        centred, _ = normalised(h0)
        n1 = (centred * gains[0:1, :] + shifts[0:1, :]).astype(BF16)
        value, slope = gelu_pair(mm(up_t[...], n1) + up_col[...])
        zt_v[...] = value
        gt_v[...] = slope
        h1 = (h0 + (mm(down_t[...], value) + down_col[...])).astype(BF16)
        h1_v[...] = h1
        h1 = h1.astype(F32)
        centred, _ = normalised(h1)
        n2_v[...] = (centred * gains[1:2, :] + shifts[1:2, :]).astype(BF16)
        save(6).start()

        @pl.when(jnp.logical_not(b_on))
        def _():
            for i in range(1, 5):
                save(i).start()

        for step in range(STEPS):
            await_up(step)
        part_width = ff // 2

        @pl.loop(0, 2)
        def _(step):
            cols = pl.ds(pl.multiple_of(step * part_width, part_width), part_width)
            value, slope = gelu_pair(mm(n2_v[...], up_v[:, cols]) + u_row[:, cols])
            z_v[:, cols] = value
            gz_v[:, cols] = slope

        save(5).start()

        @pl.when(jnp.logical_not(b_on))
        def _():
            save(0).start()

        for step in range(STEPS):
            await_down(step)
        out_v[0] = (h1 + w_row[...] + mm(z_v[...], down_v[...])).astype(BF16)

    def norm_back(hidden, dn, grad, row):
        centred, scale = normalised(hidden)
        vec_v[2 + row:3 + row, 0:channels] = jnp.sum(dn * centred, axis=0, keepdims=True)
        vec_v[4 + row:5 + row, 0:channels] = jnp.sum(dn, axis=0, keepdims=True)
        scaled = dn * gains[row:row + 1, :]
        along = jnp.mean(scaled * centred, axis=-1, keepdims=True)
        flat = jnp.mean(scaled, axis=-1, keepdims=True)
        return centred, grad + scale * (scaled - flat - centred * along)

    backs = ((e_v, f_o), (dq_v, dq_o), (da_v, da_o), (db_v, db_o), (vec_v, vec_o))

    def back(i):
        return pltpu.make_async_copy(backs[i][0], backs[i][1].at[b_slot], back_sems.at[i])

    def run_backward():
        back(0).start()
        grad = e_v[...].astype(F32)
        vec_v[...] = jnp.zeros_like(vec_v)
        vec_v[1:2, 0:channels] = jnp.sum(grad, axis=0, keepdims=True)
        acc_v[...] = jnp.zeros_like(acc_v)
        reload(0)

        @pl.when(jnp.logical_not(f_on))
        def _():
            await_down(0)
            await_up(0)
            for step in range(1, STEPS):
                start_down(step)
                start_up(step)
            for i in range(1, len(loads)):
                load(i).start()

        @pl.loop(0, STEPS)
        def _(step):
            cols = pl.ds(pl.multiple_of(step * width, width), width)

            @pl.when(jnp.logical_not(f_on) & (step > 0))
            def _():
                await_down(step)
                await_up(step)

            dq = (mm_nt(e_v[...], down_v[cols, :]) * gz_v[:, cols].astype(F32)).astype(BF16)
            dq_v[:, cols] = dq
            vec_v[0:1, cols] = jnp.sum(dq.astype(F32), axis=0, keepdims=True)
            acc_v[...] += mm_nt(dq, up_v[:, cols])

        back(1).start()
        reload(1)
        _, grad = norm_back(h1_v[...].astype(F32), acc_v[...], grad, 1)
        f1 = grad.astype(BF16)
        reload(2)
        dq = (mm(down_w[...], f1) * gt_v[...].astype(F32)).astype(BF16)
        reload(3)
        centred, grad = norm_back(h0_v[...].astype(F32), mm(up_w[...], dq), f1.astype(F32), 0)
        out_v[1] = grad.astype(BF16)
        deliver(1, b_slot, far)
        n1 = (centred * gains[0:1, :] + shifts[0:1, :]).astype(BF16)
        reload(4)
        da_v[...] = mm_nt(n1, dq)
        db_v[...] = mm_nt(f1, zt_v[...])
        ones = jnp.ones((8, channels), BF16)
        vec_v[6:7, 0:hidden_t] = mm_nt(ones, dq)[0:1]
        vec_v[7:8, 0:rows] = mm_nt(ones, f1)[0:1]
        for i in range(2, 5):
            back(i).start()

    near = jnp.logical_not(far)

    if not late_call:
        fetched(*forward_in)

        @pl.when(f_on)
        def _():
            run_forward()

        @pl.when((f_job >= 0) & jnp.logical_not(f_on))
        def _():
            out_v[0] = h0_v[...] * tab[VALID, f_slot].astype(F32).astype(BF16)

        @pl.when(f_job >= 0)
        def _():
            deliver(0, f_slot, near)

    if not first_call:
        fetched(*backward_in)

        @pl.when(b_on)
        def _():
            run_backward()

        @pl.when((b_job >= 0) & jnp.logical_not(b_on))
        def _():
            out_v[1] = e_v[...] * tab[VALID, b_slot].astype(F32).astype(BF16)
            deliver(1, b_slot, far)

        @pl.when(b_job >= 0)
        def _():
            delivered(1, b_slot, far)

        @pl.when(b_on)
        def _():
            for i in range(5):
                back(i).wait()

    if not late_call:
        @pl.when(f_job >= 0)
        def _():
            delivered(0, f_slot, near)

        @pl.when(f_on)
        def _():
            save(5).wait()
            save(6).wait()

        @pl.when(f_on & jnp.logical_not(b_on))
        def _():
            for i in range(5):
                save(i).wait()


def parcel_rows(patches, hidden_t):
    spans = {}
    row = hidden_t // 2
    for name, height in (("up_bias", 1), ("down_bias", 1), ("w", 1), ("gain", 1), ("shift", 1), ("u", 2)):
        spans[name] = row
        row += height
    return spans, -(-row // 16) * 16


def parcel_body(spans, up, down, up_bias, down_bias, u, w, gain, shift, out, all_v):
    hidden_t = up.shape[1]
    lanes = all_v.shape[1]
    all_v[...] = jnp.zeros_like(all_v)
    all_v[0:up.shape[0], 0:hidden_t] = up[...].astype(F32)
    all_v[0:down.shape[0], hidden_t:hidden_t + down.shape[1]] = down[...].astype(F32)
    for name, part in (("up_bias", up_bias), ("down_bias", down_bias), ("w", w), ("gain", gain), ("shift", shift)):
        row = part[...].astype(F32).reshape(1, -1)
        all_v[spans[name]:spans[name] + 1, 0:row.shape[1]] = row
    row = u[...].astype(F32).reshape(1, -1)
    for step in range(row.shape[1] // lanes):
        all_v[spans["u"] + step:spans["u"] + step + 1, :] = row[:, step * lanes:(step + 1) * lanes]
    out[...] = all_v[...].astype(BF16)


def parcel(spans, height, parts):
    channels = parts[6].shape[1]
    return pl.pallas_call(
        functools.partial(parcel_body, spans),
        out_shape=jax.ShapeDtypeStruct((height, channels), BF16),
        in_specs=[IN_VMEM] * len(parts),
        out_specs=IN_VMEM,
        scratch_shapes=[pltpu.VMEM((height, channels), F32)],
        cost_estimate=lasting(0.1),
        name="parcel",
    )(*parts)


def prep_body(spans, patches, tab, own_i, got_i, up_w, up_t, down_w, down_t, up_col, down_col, u_row, w_row, gains, shifts, up_v, down_v):
    first = tab[PLACE, HALF] == 0
    own = own_i[...].astype(F32)
    got = got_i[...].astype(F32)
    halves = jnp.where(first, own, got), jnp.where(first, got, own)
    hidden_t = up_w.shape[1]
    lanes = own.shape[1]

    def column(row):
        return jnp.broadcast_to(row, (8, row.shape[1])).T[:, 0:1]

    up_v[...] = jnp.zeros_like(up_v)
    down_v[...] = jnp.zeros_like(down_v)
    down_col[...] = jnp.zeros_like(down_col)
    for side, half in enumerate(halves):
        size = patches // 2
        up_v[side * size:(side + 1) * size, :] = half[0:size, 0:hidden_t]
        down_col[side * size:(side + 1) * size, :] = column(half[spans["down_bias"]:spans["down_bias"] + 1, 0:size])
        size = hidden_t // 2
        down_v[side * size:(side + 1) * size, 0:patches] = half[0:size, hidden_t:hidden_t + patches]
        up_col[side * size:(side + 1) * size, :] = column(half[spans["up_bias"]:spans["up_bias"] + 1, 0:size])
        size = w_row.shape[1] // 2
        w_row[:, side * size:(side + 1) * size] = half[spans["w"]:spans["w"] + 1, 0:size]
        gains[side:side + 1, :] = half[spans["gain"]:spans["gain"] + 1, :]
        shifts[side:side + 1, :] = half[spans["shift"]:spans["shift"] + 1, :]
        steps = u_row.shape[1] // 2 // lanes
        for step in range(steps):
            at = (side * steps + step) * lanes
            u_row[:, at:at + lanes] = half[spans["u"] + step:spans["u"] + step + 1, :]
    up_w[...] = up_v[...].astype(BF16)
    up_t[...] = up_v[...].T.astype(BF16)
    down_w[...] = down_v[...].astype(BF16)
    down_t[...] = down_v[...].T.astype(BF16)


def prep(spans, patches, rows, hidden_t, ff, tab, own, got):
    channels = own.shape[1]
    names = ("up_w", "up_t", "down_w", "down_t", "up_col", "down_col", "u_row", "w_row", "gains", "shifts")
    sizes = [(rows, hidden_t), (hidden_t, rows), (hidden_t, rows), (rows, hidden_t), (hidden_t, 1), (rows, 1),
             (1, ff), (1, channels), (2, channels), (2, channels)]
    out = pl.pallas_call(
        functools.partial(prep_body, spans, patches),
        out_shape=[jax.ShapeDtypeStruct(size, BF16 if i < 4 else F32) for i, size in enumerate(sizes)],
        in_specs=[IN_SMEM] + [IN_VMEM] * 2,
        out_specs=[IN_VMEM] * len(sizes),
        scratch_shapes=[pltpu.VMEM((rows, hidden_t), F32), pltpu.VMEM((hidden_t, rows), F32)],
        compiler_params=pltpu.CompilerParams(vmem_limit_bytes=VMEM_BYTES),
        cost_estimate=lasting(0.1),
        name="prep",
    )(tab, own, got)
    return dict(zip(names, out))


def tick_call(tick, tab, images, cots, recv, w, kept, after=()):
    patches, channels = images.shape[1:]
    rows = recv.shape[0]
    ff = w["own_up"].shape[1]
    hidden_t = w["up_t"].shape[0]
    sections = 4
    shape = jax.ShapeDtypeStruct
    upper = -(-rows // 32) * 16
    slab = shape((2, SLOTS, upper, 2 * channels // sections), BF16)
    wide = shape((SLOTS, rows, ff), BF16)
    tall = shape((SLOTS, hidden_t, channels), BF16)
    plain = shape((SLOTS, rows, channels), BF16)
    shapes = [shape((rows, channels), BF16), slab, slab, shape((2,) + slab.shape, BF16)] + [wide, wide, tall, tall, plain, plain, plain, plain, wide,
              shape((SLOTS, rows, hidden_t), F32), shape((SLOTS, rows, hidden_t), F32), shape((SLOTS, 8, ff), F32)]
    names = ("own_up", "got_up", "own_down", "got_down", "up_w", "up_t", "down_w", "down_t", "up_col", "down_col", "u_row", "w_row", "gains", "shifts")
    ins = [tab, images, cots, recv] + [w[k] for k in names]
    specs = [IN_SMEM] + [IN_ANY] * 7 + [IN_VMEM] * 10
    if tick is not None:
        ins.insert(0, tick.reshape(1))
        specs.insert(0, IN_SMEM)
    ins += list(after)
    specs += [IN_ANY] * len(after)
    first = len(ins)
    passed = 0
    aliases = {}
    if kept is not None:
        passed = len(kept)
        aliases = {first + i: 1 + i for i in range(passed)}
        ins += list(kept)
        specs += [IN_ANY] * passed

    def trimmed(*refs):
        tick_body("both" if tick is not None else "first" if kept is None else "last", *refs[:first - len(after)], *refs[first + passed:])

    vmem = pltpu.VMEM
    line = vmem((rows, channels), BF16)
    broad = vmem((rows, ff), BF16)
    high = vmem((hidden_t, channels), BF16)
    dma = pltpu.SemaphoreType.DMA
    out = pl.pallas_call(
        trimmed,
        out_shape=shapes,
        in_specs=specs,
        out_specs=[IN_ANY] * len(shapes),
        input_output_aliases=aliases,
        scratch_shapes=[vmem((channels, ff), BF16), vmem((ff, channels), BF16), vmem((2, patches, channels), BF16), line, line, line, line,
                        broad, broad, high, high, broad, vmem((rows, channels), F32), vmem((2, rows, channels), BF16),
                        vmem((2, sections, upper, 2 * channels // sections), BF16),
                        vmem((rows, hidden_t), F32), vmem((rows, hidden_t), F32), vmem((8, ff), F32),
                        dma((3, STEPS)), dma((2,)), dma((5,)), dma((2, sections + 1)), dma((7,)), dma((5,))],
        compiler_params=pltpu.CompilerParams(vmem_limit_bytes=VMEM_BYTES),
        cost_estimate=lasting(8),
        name="tick" if tick is not None else "late_tick",
    )(*ins)
    return out[0], tuple(out[1:])


def position(relative, bits):
    place = 0
    for bit in bits:
        place = place * 2 + ((relative >> bit) & 1)
    return place


def down_grad_body(chunks, count, orders, aligned, tab, f_i, z_i, rider_i, *refs):
    outs, made, (f_v, ft_v, z_v, f_sems, z_sems, out_sems) = refs[:2 * chunks], refs[2 * chunks:4 * chunks], refs[4 * chunks:]
    half = tab[PLACE, HALF]
    me = tab[PLACE, ME]
    width = outs[0].shape[-1]
    channels = f_i.shape[2]
    rows = f_i.shape[1]
    size = z_i.shape[2] // 2
    tile = 256 if width % 256 == 0 else width
    piece = channels // count
    extra = rider_i.shape[1] // count if aligned else 0

    def z_copy(slot, which):
        first = pl.multiple_of(jnp.where(half == which % 2, 1, 0) * size + which // 2 * width, 128)
        return pltpu.make_async_copy(z_i.at[slot, :, pl.ds(first, width)], z_v.at[which, pl.ds(slot * rows, rows), :], z_sems.at[which, slot])

    def f_copy(slot):
        return pltpu.make_async_copy(f_i.at[slot], f_v.at[pl.ds(slot * rows, rows), :], f_sems.at[slot])

    for slot in range(SLOTS):
        @pl.when(tab[ON, slot] == 1)
        def _():
            f_copy(slot).start()

        @pl.when(tab[ON, slot] != 1)
        def _():
            f_v[pl.ds(slot * rows, rows), :] = jnp.zeros((rows, channels), BF16)

    for which in range(2 * chunks):
        for slot in range(SLOTS):
            @pl.when(tab[ON, slot] == 1)
            def _():
                z_copy(slot, which).start()

            @pl.when(tab[ON, slot] != 1)
            def _():
                z_v[which, pl.ds(slot * rows, rows), :] = jnp.zeros((rows, width), BF16)

    for slot in range(SLOTS):
        @pl.when(tab[ON, slot] == 1)
        def _():
            f_copy(slot).wait()

    ft_v[...] = f_v[...].T
    copies = [pltpu.make_async_copy(made[which], outs[which], out_sems.at[which]) for which in range(2 * chunks)]
    for which, out in enumerate(made):
        for slot in range(SLOTS):
            @pl.when(tab[ON, slot] == 1)
            def _():
                z_copy(slot, which).wait()

        each = piece + (extra if which < 2 else 0)
        first = [pl.multiple_of(position(d ^ me, orders[which // 2]) * each, 16) for d in range(count)]

        @pl.loop(0, width // tile)
        def _(step):
            cols = pl.ds(pl.multiple_of(step * tile, tile), tile)
            total = mm(ft_v[...], z_v[which, :, cols]).astype(BF16)
            if aligned:
                for d in range(count):
                    out[pl.ds(first[d], piece), cols] = total[d * piece:(d + 1) * piece]
            else:
                out[:, cols] = total

        if extra and which < 2:
            for d in range(count):
                out[pl.ds(first[d] + piece, extra), :] = rider_i[which, d * extra:(d + 1) * extra, :]

        copies[which].start()

    for copy in copies:
        copy.wait()


def up_grad_body(chunks, height, count, orders, aligned, tab, n_i, dq_i, *refs):
    outs, made, (n_v, nt_v, dq_v, n_sems, dq_sems, out_sems) = refs[:2 * chunks], refs[2 * chunks:4 * chunks], refs[4 * chunks:]
    half = tab[PLACE, HALF]
    me = tab[PLACE, ME]
    rows = n_i.shape[1]
    size = n_i.shape[2] // 2
    ff = dq_i.shape[2]

    def n_copy(slot):
        return pltpu.make_async_copy(n_i.at[slot], n_v.at[pl.ds(slot * rows, rows), :], n_sems.at[slot])

    def dq_copy(side, slot):
        cols = pl.ds(side * (ff // 2), ff // 2)
        return pltpu.make_async_copy(dq_i.at[slot, :, cols], dq_v.at[pl.ds(slot * rows, rows), cols], dq_sems.at[side, slot])

    for slot in range(SLOTS):
        @pl.when(tab[ON, slot] == 1)
        def _():
            n_copy(slot).start()

        @pl.when(tab[ON, slot] != 1)
        def _():
            n_v[pl.ds(slot * rows, rows), :] = jnp.zeros((rows, 2 * size), BF16)
            dq_v[pl.ds(slot * rows, rows), :] = jnp.zeros((rows, ff), BF16)

    for side in range(2):
        for slot in range(SLOTS):
            @pl.when(tab[ON, slot] == 1)
            def _():
                dq_copy(side, slot).start()

    for slot in range(SLOTS):
        @pl.when(tab[ON, slot] == 1)
        def _():
            n_copy(slot).wait()

    turned = n_v[...].T
    for fixed in range(2):
        side = jnp.where(half == fixed, 1, 0)
        for chunk in range(chunks):
            first = fixed * size + chunk * height
            nt_v[chunk, pl.ds(pl.multiple_of(side * height, 16), height), :] = turned[first:first + height]

    piece = ff // count if aligned else 384
    copies = [pltpu.make_async_copy(made[i], outs[i], out_sems.at[i]) for i in range(2 * chunks)]
    for chunk in range(chunks):
        theirs_v, mine_v = made[2 * chunk:2 * chunk + 2]
        for side in range(2):
            if chunk == 0:
                for slot in range(SLOTS):
                    @pl.when(tab[ON, slot] == 1)
                    def _():
                        dq_copy(side, slot).wait()

            @pl.loop(side * (ff // piece // 4), (side + 1) * (ff // piece // 4))
            def _(pair):
                cols = pl.ds(pl.multiple_of(pair * 2 * piece, 128), 2 * piece)
                total = mm(nt_v[chunk], dq_v[:, cols]).astype(BF16)
                if not aligned:
                    theirs_v[:, cols] = total[:height]
                    mine_v[:, cols] = total[height:]
                    return
                for i in range(2):
                    place = pl.ds(pl.multiple_of(position((2 * pair + i) ^ me, orders[chunk]) * height, 16), height)
                    theirs_v[place, :] = total[:height, i * piece:(i + 1) * piece]
                    mine_v[place, :] = total[height:, i * piece:(i + 1) * piece]

        copies[2 * chunk].start()
        copies[2 * chunk + 1].start()

    for copy in copies:
        copy.wait()


def arranged(pieces, bits):
    count = pieces.shape[0]
    order = [0] * count
    for relative in range(count):
        order[position(relative, bits)] = relative
    return jnp.take(pieces, jnp.array(order) ^ lax.axis_index("dp"), axis=0)


def down_grad_call(chunks, count, orders, tab, f, z, rider, after):
    slots, rows, channels = f.shape
    width = z.shape[2] // 2 // chunks
    piece = channels // count
    aligned = piece % 16 == 0
    extra = rider.shape[1] if aligned else 0
    shapes = [(channels + (extra if i == 0 else 0), width) for i in range(chunks)]
    out = launch(
        functools.partial(down_grad_body, chunks, count, orders, aligned), [tab, f, z, rider], [IN_SMEM, IN_ANY, IN_ANY, IN_VMEM], after,
        out_shape=[jax.ShapeDtypeStruct(shapes[i // 2], BF16) for i in range(2 * chunks)],
        out_specs=[IN_ANY] * (2 * chunks),
        scratch_shapes=[pltpu.VMEM(shapes[i // 2], BF16) for i in range(2 * chunks)]
                       + [pltpu.VMEM((slots * rows, channels), BF16), pltpu.VMEM((channels, slots * rows), BF16),
                          pltpu.VMEM((2 * chunks, slots * rows, width), BF16),
                          pltpu.SemaphoreType.DMA((slots,)), pltpu.SemaphoreType.DMA((2 * chunks, slots)), pltpu.SemaphoreType.DMA((2 * chunks,))],
        compiler_params=pltpu.CompilerParams(vmem_limit_bytes=VMEM_BYTES),
        cost_estimate=lasting(9),
        name="down_grad",
    )
    if not aligned:
        out = [arranged(part.reshape(count, piece, width), orders[i // 2]).reshape(part.shape) for i, part in enumerate(out)]
    return [out[2 * i:2 * i + 2] for i in range(chunks)]


def up_grad_call(chunks, count, orders, tab, n, dq, after):
    slots, rows, channels = n.shape
    ff = dq.shape[2]
    height = channels // 2 // chunks
    piece = ff // count
    aligned = piece % 128 == 0
    shape = (count * height, piece) if aligned else (height, ff)
    out = launch(
        functools.partial(up_grad_body, chunks, height, count, orders, aligned), [tab, n, dq], [IN_SMEM, IN_ANY, IN_ANY], after,
        out_shape=[jax.ShapeDtypeStruct(shape, BF16)] * (2 * chunks),
        out_specs=[IN_ANY] * (2 * chunks),
        scratch_shapes=[pltpu.VMEM(shape, BF16)] * (2 * chunks)
                       + [pltpu.VMEM((slots * rows, channels), BF16), pltpu.VMEM((chunks, 2 * height, slots * rows), BF16),
                          pltpu.VMEM((slots * rows, ff), BF16),
                          pltpu.SemaphoreType.DMA((slots,)), pltpu.SemaphoreType.DMA((2, slots)), pltpu.SemaphoreType.DMA((2 * chunks,))],
        compiler_params=pltpu.CompilerParams(vmem_limit_bytes=VMEM_BYTES),
        cost_estimate=lasting(9),
        name="up_grad",
    )
    if not aligned:
        out = [arranged(jnp.swapaxes(part.reshape(height, count, piece), 0, 1), orders[i // 2]).reshape(count * height, piece) for i, part in enumerate(out)]
    return [out[2 * i:2 * i + 2] for i in range(chunks)]


def halved_body(mine, got, kept, sent):
    middle = kept.shape[0]
    low, high = pl.ds(0, middle), pl.ds(middle, middle)
    sent[...] = (mine[high, :].astype(F32) + got[high, :].astype(F32)).astype(BF16)
    kept[...] = (mine[low, :].astype(F32) + got[low, :].astype(F32)).astype(BF16)


def halved(mine, got, after):
    size, width = mine.shape
    return launch(halved_body, [mine, got], [IN_VMEM] * 2, after,
                  out_shape=[jax.ShapeDtypeStruct((size // 2, width), BF16)] * 2, out_specs=[IN_VMEM] * 2,
                  compiler_params=pltpu.CompilerParams(vmem_limit_bytes=VMEM_BYTES), cost_estimate=lasting(2), name="halved")


def summed_body(kind, mine, got, *refs):
    total = mine[...].astype(F32) + got[...].astype(F32)
    if kind == "above":
        first, out = refs
        out[0:first.shape[0]] = first[...]
        out[first.shape[0]:] = total
    elif kind == "beside":
        first, out = refs
        out[:, 0:first.shape[1]] = first[...]
        out[:, first.shape[1]:] = total
    else:
        out, *rest = refs
        out[...] = total[:out.shape[0]]
        for rider in rest:
            rider[...] = total[out.shape[0]:].astype(BF16)


def summed(kind, mine, got, size, first, after):
    rows, width = mine.shape
    shape = jax.ShapeDtypeStruct
    ins = [mine, got]
    if kind == "above":
        shapes = [shape((first.shape[0] + rows, width), F32)]
    elif kind == "beside":
        shapes = [shape((rows, first.shape[1] + width), F32)]
    else:
        shapes = [shape((size, width), F32)] + [shape((rows - size, width), BF16)] * (rows > size)
    if first is not None:
        ins.append(first)
    return launch(functools.partial(summed_body, kind), ins, [IN_VMEM] * len(ins), after,
                  out_shape=shapes, out_specs=[IN_VMEM] * len(shapes),
                  compiler_params=pltpu.CompilerParams(vmem_limit_bytes=VMEM_BYTES), cost_estimate=lasting(0.1), name="summed")


def packing(patches, hidden_t, channels, ff):
    spans = {}
    row = 0
    for name, height in (("token", -(-patches // 2 // 8) * 8), ("chan_up_bias", ff // 2 // channels), ("biases", 1), ("gain", 1), ("shift", 1)):
        spans[name] = row
        row += height
    return spans, -(-row // 128) * 128, channels


def pack_body(spans, patches, tab, da_i, db_i, vec_i, out, da_v, db_v, vec_v, both_v, sems):
    half = tab[PLACE, HALF]
    lanes = both_v.shape[-1]
    hidden_t = db_v.shape[2]
    upper = patches // 2
    sources = ((da_i, da_v), (db_i, db_v), (vec_i, vec_v))

    def copy(kind, slot):
        return pltpu.make_async_copy(sources[kind][0].at[slot], sources[kind][1].at[slot], sems.at[kind, slot])

    for slot in range(SLOTS):
        @pl.when(tab[ON, slot] == 1)
        def _():
            for kind in range(3):
                copy(kind, slot).start()

        @pl.when(tab[ON, slot] != 1)
        def _():
            for _, buffer in sources:
                buffer[slot] = jnp.zeros(buffer.shape[1:], F32)

    for slot in range(SLOTS):
        @pl.when(tab[ON, slot] == 1)
        def _():
            for kind in range(3):
                copy(kind, slot).wait()

    da = (da_v[0] + da_v[1]) + (da_v[2] + da_v[3])
    db = (db_v[0] + db_v[1]) + (db_v[2] + db_v[3])
    vec = (vec_v[0] + vec_v[1]) + (vec_v[2] + vec_v[3])
    both_v[...] = jnp.zeros_like(both_v)
    ff = vec.shape[1]
    channels = spans["channels"]
    for side in range(2):
        at = spans["token"]
        both_v[side, at:at + upper, 0:hidden_t] = da[side * upper:(side + 1) * upper]
        block = db[:, side * (hidden_t // 2):(side + 1) * (hidden_t // 2)]
        both_v[side, at:at + upper, hidden_t:hidden_t + hidden_t // 2] = block[:upper]
        both_v[side, at:at + upper, hidden_t + hidden_t // 2:2 * hidden_t] = block[upper:patches]

        def line(name, row, first, length, left=0):
            at = spans[name]
            for step in range(-(-length // lanes)):
                size = min(lanes, length - step * lanes)
                both_v[side, at + step:at + step + 1, left:left + size] = vec[row:row + 1, first + step * lanes:first + step * lanes + size]

        line("chan_up_bias", 0, side * (ff // 2), ff // 2)
        line("biases", 1, side * (channels // 2), channels // 2)
        line("biases", 6, side * (hidden_t // 2), hidden_t // 2, channels // 2)
        line("biases", 7, side * upper, upper, channels // 2 + hidden_t // 2)
        line("gain", 2 + side, 0, channels)
        line("shift", 4 + side, 0, channels)
    out[0] = both_v[1 - half].astype(BF16)
    out[1] = both_v[half].astype(BF16)


def unpack_body(spans, patches, hidden_t, relative, tab, parts, gain_o, shift_o, up_o, up_bias_o, down_o, down_bias_o, chan_up_bias_o, chan_down_bias_o, all_v):
    size = parts.shape[1]
    for i, shift in enumerate(relative):
        first = pl.multiple_of((tab[PLACE, ME] ^ shift) * size, 8) if len(relative) > 1 else 0
        all_v[pl.ds(first, size), :] = parts[i].astype(F32)
    upper = patches // 2
    lanes = all_v.shape[1]
    at = spans["token"]
    up_o[...] = all_v[at:at + upper, 0:hidden_t]
    block = all_v[at:at + -(-upper // 8) * 8, hidden_t:2 * hidden_t]
    down_o[:, 0:upper] = block[:, :hidden_t // 2].T[:, :upper]
    down_o[:, upper:patches] = block[:, hidden_t // 2:].T[:, :upper]
    gain_o[...] = all_v[spans["gain"]:spans["gain"] + 1, :]
    shift_o[...] = all_v[spans["shift"]:spans["shift"] + 1, :]
    for step in range(chan_up_bias_o.shape[1] // lanes):
        at = spans["chan_up_bias"] + step
        chan_up_bias_o[:, step * lanes:(step + 1) * lanes] = all_v[at:at + 1, :]
    row = all_v[spans["biases"]:spans["biases"] + 1, :]
    first = chan_down_bias_o.shape[1]
    chan_down_bias_o[...] = row[:, :first]
    up_bias_o[...] = row[:, first:first + hidden_t // 2]
    down_bias_o[...] = row[:, first + hidden_t // 2:first + hidden_t // 2 + upper]


def unpack(spans, patches, hidden_t, channels, ff, relative, tab, parts, after):
    sizes = [(1, channels), (1, channels), (patches // 2, hidden_t), (1, hidden_t // 2), (hidden_t // 2, patches), (1, patches // 2), (1, ff // 2), (1, channels // 2)]
    return launch(
        functools.partial(unpack_body, spans, patches, hidden_t, relative), [tab, parts], [IN_SMEM, IN_VMEM], after,
        out_shape=[jax.ShapeDtypeStruct(size, F32) for size in sizes],
        out_specs=[IN_VMEM] * len(sizes),
        scratch_shapes=[pltpu.VMEM((parts.shape[0] * parts.shape[1], parts.shape[2]), F32)],
        compiler_params=pltpu.CompilerParams(vmem_limit_bytes=VMEM_BYTES),
        cost_estimate=lasting(2),
        name="unpack",
    )


def both_body(first, second, out):
    out[0:first.shape[0]] = first[...]
    out[first.shape[0]:] = second[...]


def both(first, second, after):
    shape = (2 * first.shape[0],) + first.shape[1:]
    return launch(both_body, [first, second], [IN_VMEM] * 2, after, out_shape=jax.ShapeDtypeStruct(shape, first.dtype), out_specs=IN_VMEM,
                  compiler_params=pltpu.CompilerParams(vmem_limit_bytes=VMEM_BYTES), cost_estimate=lasting(2), name="both")


def split_body(both, first_o, second_o, sems):
    copies = [pltpu.make_async_copy(both.at[i], target, sems.at[i]) for i, target in enumerate((first_o, second_o))]
    for copy in copies:
        copy.start()
    for copy in copies:
        copy.wait()


def split(both, after):
    return launch(split_body, [both], [IN_ANY], after, out_shape=[jax.ShapeDtypeStruct(both.shape[1:], both.dtype)] * 2,
                  out_specs=[IN_VMEM] * 2, scratch_shapes=[pltpu.SemaphoreType.DMA((2,))],
                  compiler_params=pltpu.CompilerParams(vmem_limit_bytes=VMEM_BYTES), cost_estimate=lasting(0.1), name="split")


def place_body(tab, here, beside, across, corner, mixed_o, grad_o, mixed_v, grad_v, sems):
    layer = tab[PLACE, LAYER]
    half = tab[PLACE, HALF]
    sources = (here, beside, across, corner)
    places, width, patches = mixed_o.shape
    upper = mixed_v.shape[1]
    buffers = (mixed_v, grad_v)

    def copy(kind, place, source):
        return pltpu.make_async_copy(source.at[kind, place // 2], buffers[kind].at[tab[ORDER, place]], sems.at[kind, place])

    for place in range(places):
        for kind, row in enumerate((MIXED_FAR, GRAD_FAR)):
            which = jnp.where(tab[row, place] == layer, 0, 2) + jnp.where(half == place % 2, 0, 1)
            for i, source in enumerate(sources):
                @pl.when(which == i)
                def _():
                    copy(kind, place, source).start()

    for place in range(places):
        for kind in range(2):
            copy(kind, place, here).wait()

    @pl.loop(0, places)
    def _(i):
        for source, target in ((mixed_v, mixed_o), (grad_v, grad_o)):
            whole = jnp.concatenate([source[i, :, 0:width], source[i, :, width:2 * width]], 0)
            target[i] = whole.T[:, 0:patches]


def pack_call(spans, packed_rows, lanes, patches, channels, tab, da, db, vec, after):
    return launch(
        functools.partial(pack_body, dict(spans, channels=channels), patches), [tab, da, db, vec], [IN_SMEM] + [IN_ANY] * 3, after,
        out_shape=jax.ShapeDtypeStruct((2, packed_rows, lanes), BF16),
        out_specs=IN_VMEM,
        scratch_shapes=[pltpu.VMEM(da.shape, F32), pltpu.VMEM(db.shape, F32), pltpu.VMEM(vec.shape, F32),
                        pltpu.VMEM((2, packed_rows, lanes), F32), pltpu.SemaphoreType.DMA((3, SLOTS))],
        compiler_params=pltpu.CompilerParams(vmem_limit_bytes=VMEM_BYTES),
        cost_estimate=lasting(2.5),
        name="pack",
    )


def place_call(slot_count, patches, width, tab, slabs, after):
    out_shape = jax.ShapeDtypeStruct((slot_count, width, patches), BF16)
    buffer = pltpu.VMEM((slot_count,) + slabs[0].shape[2:], BF16)
    return launch(
        place_body, [tab] + list(slabs), [IN_SMEM] + [IN_ANY] * 4, after,
        out_shape=[out_shape, out_shape],
        out_specs=[IN_VMEM] * 2,
        scratch_shapes=[buffer, buffer, pltpu.SemaphoreType.DMA((2, slot_count))],
        compiler_params=pltpu.CompilerParams(vmem_limit_bytes=VMEM_BYTES),
        cost_estimate=lasting(4),
        name="place",
    )


def local(images, cotangent, valid_rows, skip_masks, norm_gain, norm_bias, token_up, token_up_bias, token_down,
          token_down_bias, chan_up, chan_up_bias, chan_down, chan_down_bias):
    count = lax.axis_size("dp")
    slot_count, patches, channels = images.shape
    rows = -(-patches // 16) * 16
    hidden_t = token_up.shape[1]
    ff = chan_up.shape[1]

    parcel_spans, height = parcel_rows(patches, hidden_t)
    own = parcel(parcel_spans, height, (token_up, token_down, token_up_bias, token_down_bias, chan_up_bias, chan_down_bias, norm_gain, norm_bias))
    got = flipped(own, "pipe", 1)
    got_up = flipped(chan_up, "pipe", 1)
    got_down = flipped(chan_down, "pipe", 1)

    tab, ticks = pl.pallas_call(
        table_body,
        out_shape=[jax.ShapeDtypeStruct((10, MOST), jnp.int32), jax.ShapeDtypeStruct((1,), jnp.int32)],
        in_specs=[IN_SMEM] * 4,
        out_specs=[IN_SMEM] * 2,
        cost_estimate=lasting(0.1),
        name="table",
    )(jnp.asarray(JOB_TABLE.reshape(-1, MOST)), jnp.asarray(TICK_TABLE[None, :]), valid_rows[None, :], skip_masks.T)

    weights = dict(prep(parcel_spans, patches, rows, hidden_t, ff, tab, own, got), own_up=chan_up, got_up=got_up, own_down=chan_down, got_down=got_down)
    blank = jnp.zeros((rows, channels), BF16)
    send, kept = tick_call(None, tab, images, cotangent, blank, weights, None)

    def one(tick, carried):
        send, recv, kept = carried
        arriving = flipped(send, "pipe", 2)
        send, kept = tick_call(tick, tab, images, cotangent, recv, weights, kept)
        return send, arriving, kept

    _, last, kept = lax.fori_loop(1, ticks[0], one, (send, blank, kept))
    kept = dict(zip(KEPT, kept))

    chunks = 2
    bits = tuple(range(count.bit_length() - 1))
    other_bits = (bits[1], bits[0]) + bits[2:]
    orders = (bits, other_bits, bits, other_bits)
    spans, packed_rows, lanes = packing(patches, hidden_t, channels, ff)

    made = []

    def step(function, *arrays):
        out = function(*arrays, after=tuple(made))
        made[:] = jax.tree.leaves(out)[:1]
        return out

    pieces = [None] * (2 * chunks)
    moving = [None] * (2 * chunks)

    def begin(which, pair):
        pieces[which] = pair[1]
        moving[which] = flipped(pair[0], "pipe", 1)

    def advance(which, stage):
        pieces[which], sent = step(halved, pieces[which], moving[which])
        moving[which] = flipped(sent, "dp", 1 << orders[which][stage])

    def finished(which, kind, first=None):
        size = channels // count if which < chunks else channels // 2 // chunks
        return step(summed, kind, pieces[which], moving[which], size, first)

    _, late_kept = step(tick_call, None, tab, images, cotangent, last, weights, tuple(kept[k] for k in KEPT))
    made[:] = late_kept[:1]
    kept = dict(zip(KEPT, late_kept))
    over = flipped(kept["slab23"], "pipe", 2)
    beside = flipped(kept["slab1"], "pipe", 1)
    rider = step(pack_call, spans, packed_rows, lanes, patches, channels, tab, kept["da"], kept["db"], kept["vec"])
    made.append(beside)
    for i, pair in enumerate(step(down_grad_call, chunks, count, orders[:chunks], tab, kept["f"], kept["z"], rider)):
        begin(i, pair)
    advance(0, 0)
    advance(1, 0)
    for i, pair in enumerate(step(up_grad_call, chunks, count, orders[chunks:], tab, kept["n2"], kept["dq"])):
        begin(chunks + i, pair)
    advance(0, 1)
    advance(1, 1)
    advance(2, 0)
    advance(3, 0)
    across, turned = step(split, over)
    corner = flipped(turned, "pipe", 1)
    for stage in range(2, len(bits)):
        advance(0, stage)
        advance(1, stage)
    advance(2, 1)
    width = channels // 4
    mixed, input_grad = step(place_call, slot_count, patches, width, tab, (kept["slab0"], beside, across, corner))
    advance(3, 1)
    down_first, *small = finished(0, "alone")
    parts = small[0][None] if small else None
    relative = [0]
    gathered = list(reversed(bits)) if small else []

    def gather():
        nonlocal parts, relative
        if gathered:
            bit = gathered.pop(0)
            parts = step(both, parts, flipped(parts, "dp", 1 << bit))
            relative += [i ^ (1 << bit) for i in relative]

    chan_down_grad, = finished(1, "beside", down_first)
    gather()
    for stage in range(2, len(bits)):
        advance(2, stage)
        advance(3, stage)
    while gathered:
        gather()
    if parts is None:
        total = rider[1].astype(F32) + flipped(rider[0], "pipe", 1).astype(F32)
        for bit in bits:
            sent = lax.optimization_barrier(total.astype(BF16))
            total = sent.astype(F32) + flipped(sent, "dp", 1 << bit).astype(F32)
        parts = total[None]
    gain, shift, token_up_grad, up_bias, token_down_grad, down_bias, chan_up_bias_grad, chan_down_bias_grad = step(
        unpack, spans, patches, hidden_t, channels, ff, relative, tab, parts)
    up_first, = finished(2, "alone")
    chan_up_grad, = finished(3, "above", up_first)

    return (
        jnp.swapaxes(mixed, 1, 2),
        jnp.swapaxes(input_grad, 1, 2),
        gain,
        shift,
        token_up_grad,
        up_bias[0],
        token_down_grad,
        down_bias[0],
        chan_up_grad,
        chan_up_bias_grad[0],
        chan_down_grad.T,
        chan_down_bias_grad[0],
    )


def solution(mesh):
    placed = (
        P("dp", None, None),
        P("dp", None, None),
        P("dp"),
        P("dp", None),
        P("pipe", None),
        P("pipe", None),
        P("pipe", None),
        P("pipe"),
        P("pipe", None),
        P("pipe"),
        P("pipe", None),
        P("pipe"),
        P("pipe", None),
        P("pipe"),
    )
    return jax.shard_map(
        local,
        mesh=mesh,
        in_specs=placed,
        out_specs=(
            P("dp", None, "pipe"),
            P("dp", None, "pipe"),
            P("pipe", None),
            P("pipe", None),
            P("pipe", None),
            P("pipe"),
            P("pipe", None),
            P("pipe"),
            P("pipe", "dp"),
            P("pipe"),
            P("pipe", "dp"),
            P("pipe"),
        ),
        check_vma=False,
    )
```

```python
import functools

import jax
import jax.numpy as jnp
import numpy as np
from jax import lax
from jax.experimental import pallas as pl
from jax.experimental.pallas import tpu as pltpu
from jax.sharding import PartitionSpec as P

F32 = jnp.float32
BF16 = jnp.bfloat16
NORM_EPS = 1e-06
GELU_SCALE = 0.7978845608
GELU_CUBE = 0.044715
STEPS = 2
SLOTS = 4
VMEM_BYTES = 40 << 20

IN_VMEM = pl.BlockSpec(memory_space=pltpu.VMEM)
IN_ANY = pl.BlockSpec(memory_space=pl.ANY)
IN_SMEM = pl.BlockSpec(memory_space=pltpu.SMEM)


def lasting(microseconds):
    return pl.CostEstimate(flops=int(microseconds * 10e9), bytes_accessed=1, transcendentals=0)


ON, VALID, CROSSING, IMAGE, PLACE, FORWARD, BACKWARD, ORDER, MIXED_FAR, GRAD_FAR = range(10)
LAYER, HALF, ME, LATE, HOPS = range(5)

JOBS = [
    [(-1, -1, -1, -1), (0, 0, 0, 0), (1, 1, 1, 1), (2, 2, 2, 2), (3, 3, 3, 3)],
    [(0, -1, -1, -1), (1, 1, 1, 1), (2, 0, 2, 0), (3, 2, 3, 2), (-1, 3, 0, 3)],
    [(0, -1, -1, -1), (1, 2, -1, 2), (2, 0, 2, 0), (3, 1, 3, 1), (-1, 3, 0, 3)],
    [(0, -1, -1, -1), (1, -1, -1, -1), (2, 0, -1, 0), (3, 1, 3, 1), (-1, 2, 0, 2), (-1, 3, 1, 3)],
    [(0, -1, -1, -1), (1, -1, -1, -1), (2, 0, -1, 0), (3, 1, -1, 1), (-1, 2, 0, 2), (-1, 3, 1, 3), (-1, -1, 2, -1)],
]
MOST = 8
JOB_TABLE = np.full((len(JOBS), 4, MOST), -1, np.int32)
for _hops, _rows in enumerate(JOBS):
    for _tick, _row in enumerate(_rows):
        JOB_TABLE[_hops, :, _tick] = _row
TICK_TABLE = np.array([len(_rows) for _rows in JOBS], np.int32)


def flipped(block, axis, distance):
    count = lax.axis_size(axis)
    route = [(i, i ^ distance) for i in range(count) if i ^ distance < count]
    return lax.ppermute(block, axis, route)


def mm(left, right):
    return lax.dot_general(left, right, (((1,), (0,)), ((), ())), preferred_element_type=F32)


def mm_nt(left, right):
    return lax.dot_general(left, right, (((1,), (1,)), ((), ())), preferred_element_type=F32)


def gelu_pair(pre):
    square = pre * pre
    gate = 0.5 + 0.5 * jnp.tanh(pre * (GELU_SCALE + (GELU_SCALE * GELU_CUBE) * square))
    value = pre * gate
    slope = gate + value * (1.0 - gate) * (2 * GELU_SCALE + (6 * GELU_SCALE * GELU_CUBE) * square)
    return value.astype(BF16), slope.astype(BF16)


def normalised(hidden):
    centred = hidden - jnp.mean(hidden, axis=-1, keepdims=True)
    scale = lax.rsqrt(jnp.mean(centred * centred, axis=-1, keepdims=True) + NORM_EPS)
    return centred * scale, scale


def launch(body, ins, specs, after, **options):
    first = len(ins)

    def trimmed(*refs):
        body(*refs[:first], *refs[first + len(after):])

    return pl.pallas_call(trimmed, in_specs=specs + [IN_ANY] * len(after), **options)(*ins, *after)


def table_body(jobs, ticks, valid, skip, tab, ticks_o):
    section = lax.axis_index("pipe")
    layer, half, me = section // 2, section % 2, lax.axis_index("dp")
    total = valid.shape[1]
    far = layer == 1
    firsts = [valid[0, i] * skip[0, i] for i in range(total)]
    seconds = [valid[0, i] * skip[1, i] for i in range(total)]
    kinds = [jnp.where(a * b == 1, 0, jnp.where(b == 1, 1, jnp.where(a == 1, 2, 3))) for a, b in zip(firsts, seconds)]
    crossing = sum(a * b for a, b in zip(firsts, seconds))
    hops = (crossing + 1) // 2
    for i in range(total):
        place = sum(((kinds[j] < kinds[i]) if j > i else (kinds[j] <= kinds[i])).astype(jnp.int32) for j in range(total) if j != i)
        tab[ORDER, place] = i
        tab[MIXED_FAR, place] = 1 - firsts[i] * (1 - seconds[i])
        tab[GRAD_FAR, place] = seconds[i] * (1 - firsts[i])

        @pl.when(place % 2 == half)
        def _():
            slot = place // 2
            tab[ON, slot] = jnp.where(far, seconds[i], firsts[i])
            tab[VALID, slot] = valid[0, i]
            tab[CROSSING, slot] = firsts[i] * seconds[i]
            tab[IMAGE, slot] = i

    tab[PLACE, LAYER] = layer
    tab[PLACE, HALF] = half
    tab[PLACE, ME] = me
    tab[PLACE, LATE] = jnp.where(far | (hops == 1), -1, hops - 1)
    tab[PLACE, HOPS] = hops
    ticks_o[0] = ticks[0, hops]
    for tick in range(MOST):
        tab[FORWARD, tick] = jobs[hops * 4 + layer, tick]
        tab[BACKWARD, tick] = jobs[hops * 4 + 2 + layer, tick]


KEPT = ("slab0", "slab1", "slab23", "z", "gz", "zt", "gt", "h0", "h1", "n2", "f", "dq", "da", "db", "vec")


def tick_body(phases, *refs):
    late_call = phases == "last"
    first_call = phases == "first"
    refs = list(refs)
    tick_ref = None if late_call or first_call else refs.pop(0)
    (tab, images, cots, recv, own_up, got_up, own_down, got_down,
     up_w, up_t, down_w, down_t, up_col, down_col, u_row, w_row, gains, shifts,
     send_o, slab0, slab1, slab23, z_o, gz_o, zt_o, gt_o, h0_o, h1_o, n2_o, f_o, dq_o, da_o, db_o, vec_o,
     up_v, down_v, raw_v, e_v, h0_v, h1_v, n2_v, z_v, gz_v, zt_v, gt_v, dq_v, acc_v, out_v, part_v, da_v, db_v, vec_v,
     w_sems, in_sems, load_sems, slab_sems, keep_sems, back_sems) = refs
    far = tab[PLACE, LAYER] == 1
    half = tab[PLACE, HALF]
    section = tab[PLACE, LAYER] * 2 + half
    slabs = (slab0, slab1, slab23.at[0], slab23.at[1])
    patches, channels = raw_v.shape[1:]
    rows = h0_v.shape[0]
    ff = up_v.shape[1]
    hidden_t = zt_v.shape[0]
    width = ff // STEPS
    part = channels // len(slabs)
    if late_call:
        f_job = jnp.int32(-1)
        b_job = tab[PLACE, LATE]
    elif first_call:
        f_job = tab[FORWARD, 0]
        b_job = jnp.int32(-1)
    else:
        f_job = tab[FORWARD, tick_ref[0]]
        b_job = tab[BACKWARD, tick_ref[0]]
    f_slot = jnp.maximum(f_job, 0)
    b_slot = jnp.maximum(b_job, 0)
    f_on = (f_job >= 0) & (tab[ON, f_slot] == 1)
    b_on = (b_job >= 0) & (tab[ON, b_slot] == 1)
    any_on = f_on | b_on

    def weight_copies(step):
        size = channels // 2
        cols = pl.ds(pl.multiple_of(step * width, width), width)
        own = pl.ds(pl.multiple_of(half * size, 16), size)
        rest = pl.ds(pl.multiple_of((1 - half) * size, 16), size)
        local = pl.ds(pl.multiple_of((step % (STEPS // 2)) * width, width), width)
        return (lambda: pltpu.make_async_copy(own_up.at[:, cols], up_v.at[own, cols], w_sems.at[0, step]),
                lambda: pltpu.make_async_copy(got_up.at[:, cols], up_v.at[rest, cols], w_sems.at[1, step]),
                lambda: pltpu.make_async_copy(own_down.at[local, :], down_v.at[cols, :], w_sems.at[2, step]),
                lambda: pltpu.make_async_copy(got_down.at[local, :], down_v.at[cols, :], w_sems.at[2, step]))

    def start_up(step):
        own, rest, _, _ = weight_copies(step)
        own().start()
        rest().start()

    def start_down(step):
        _, _, mine, theirs = weight_copies(step)

        @pl.when(step // (STEPS // 2) == half)
        def _():
            mine().start()

        @pl.when(step // (STEPS // 2) != half)
        def _():
            theirs().start()

    def await_up(step):
        own, rest, _, _ = weight_copies(step)
        own().wait()
        rest().wait()

    def await_down(step):
        weight_copies(step)[2]().wait()

    def fetch(kind, job, slot, crossed, source, target):
        @pl.when((job >= 0) & crossed)
        def _():
            pltpu.make_async_copy(recv, target, in_sems.at[kind]).start()

        @pl.when((job >= 0) & jnp.logical_not(crossed))
        def _():
            pltpu.make_async_copy(source.at[tab[IMAGE, slot]], raw_v.at[kind], in_sems.at[kind]).start()

    def fetched(kind, job, slot, crossed, source, target):
        @pl.when((job >= 0) & crossed)
        def _():
            pltpu.make_async_copy(recv, target, in_sems.at[kind]).wait()

        @pl.when((job >= 0) & jnp.logical_not(crossed))
        def _():
            pltpu.make_async_copy(source.at[tab[IMAGE, slot]], raw_v.at[kind], in_sems.at[kind]).wait()
            target[pl.ds(rows - 16, 16), :] = jnp.zeros((16, channels), BF16)
            target[pl.ds(0, patches), :] = raw_v[kind]

    forward_in = (0, f_job, f_slot, far & (tab[CROSSING, f_slot] == 1), images, h0_v)
    backward_in = (1, b_job, b_slot, jnp.logical_not(far) & (tab[CROSSING, b_slot] == 1), cots, e_v)
    loads = ((gz_o, gz_v), (h1_o, h1_v), (gt_o, gt_v), (h0_o, h0_v), (zt_o, zt_v))

    def load(i):
        return pltpu.make_async_copy(loads[i][0].at[b_slot], loads[i][1], load_sems.at[i])

    def reload(i):
        @pl.when(jnp.logical_not(f_on))
        def _():
            load(i).wait()

    if not late_call:
        fetch(*forward_in)

    @pl.when(f_on)
    def _():
        for step in range(STEPS):
            start_up(step)
        for step in range(STEPS):
            start_down(step)

    fetch(*backward_in)

    @pl.when(b_on & jnp.logical_not(f_on))
    def _():
        load(0).start()
        start_down(0)
        start_up(0)

    def slab_copy(kind, slot, flip):
        return pltpu.make_async_copy(part_v.at[kind, section ^ flip], slabs[flip].at[kind, slot], slab_sems.at[kind, flip])

    def send_copy(kind):
        return pltpu.make_async_copy(out_v.at[kind], send_o, slab_sems.at[kind, len(slabs)])

    def deliver(kind, slot, sends):
        @pl.when(sends)
        def _():
            send_copy(kind).start()

        @pl.when(jnp.logical_not(sends & (tab[CROSSING, slot] == 1)))
        def _():
            whole = out_v[kind]
            upper = part_v.shape[2]
            for d in range(len(slabs)):
                part_v[kind, d, :, 0:part] = whole[:upper, d * part:(d + 1) * part]
                part_v[kind, d, 0:rows - upper, part:2 * part] = whole[upper:, d * part:(d + 1) * part]
            for flip in range(len(slabs)):
                slab_copy(kind, slot, flip).start()

    def delivered(kind, slot, sends):
        @pl.when(jnp.logical_not(sends & (tab[CROSSING, slot] == 1)))
        def _():
            for flip in range(len(slabs)):
                slab_copy(kind, slot, flip).wait()

        @pl.when(sends)
        def _():
            send_copy(kind).wait()

    saves = ((gz_v, gz_o), (zt_v, zt_o), (gt_v, gt_o), (h0_v, h0_o), (h1_v, h1_o), (z_v, z_o), (n2_v, n2_o))

    def save(i):
        return pltpu.make_async_copy(saves[i][0], saves[i][1].at[f_slot], keep_sems.at[i])

    def run_forward():
        h0 = h0_v[...].astype(F32)
        centred, _ = normalised(h0)
        n1 = (centred * gains[0:1, :] + shifts[0:1, :]).astype(BF16)
        value, slope = gelu_pair(mm(up_t[...], n1) + up_col[...])
        zt_v[...] = value
        gt_v[...] = slope
        h1 = (h0 + (mm(down_t[...], value) + down_col[...])).astype(BF16)
        h1_v[...] = h1
        h1 = h1.astype(F32)
        centred, _ = normalised(h1)
        n2_v[...] = (centred * gains[1:2, :] + shifts[1:2, :]).astype(BF16)
        save(6).start()

        @pl.when(jnp.logical_not(b_on))
        def _():
            for i in range(1, 5):
                save(i).start()

        for step in range(STEPS):
            await_up(step)
        part_width = ff // 2

        @pl.loop(0, 2)
        def _(step):
            cols = pl.ds(pl.multiple_of(step * part_width, part_width), part_width)
            value, slope = gelu_pair(mm(n2_v[...], up_v[:, cols]) + u_row[:, cols])
            z_v[:, cols] = value
            gz_v[:, cols] = slope

        save(5).start()

        @pl.when(jnp.logical_not(b_on))
        def _():
            save(0).start()

        for step in range(STEPS):
            await_down(step)
        out_v[0] = (h1 + w_row[...] + mm(z_v[...], down_v[...])).astype(BF16)

    def norm_back(hidden, dn, grad, row):
        centred, scale = normalised(hidden)
        vec_v[2 + row:3 + row, 0:channels] = jnp.sum(dn * centred, axis=0, keepdims=True)
        vec_v[4 + row:5 + row, 0:channels] = jnp.sum(dn, axis=0, keepdims=True)
        scaled = dn * gains[row:row + 1, :]
        along = jnp.mean(scaled * centred, axis=-1, keepdims=True)
        flat = jnp.mean(scaled, axis=-1, keepdims=True)
        return centred, grad + scale * (scaled - flat - centred * along)

    backs = ((e_v, f_o), (dq_v, dq_o), (da_v, da_o), (db_v, db_o), (vec_v, vec_o))

    def back(i):
        return pltpu.make_async_copy(backs[i][0], backs[i][1].at[b_slot], back_sems.at[i])

    def run_backward():
        back(0).start()
        grad = e_v[...].astype(F32)
        vec_v[...] = jnp.zeros_like(vec_v)
        vec_v[1:2, 0:channels] = jnp.sum(grad, axis=0, keepdims=True)
        acc_v[...] = jnp.zeros_like(acc_v)
        reload(0)

        @pl.when(jnp.logical_not(f_on))
        def _():
            await_down(0)
            await_up(0)
            for step in range(1, STEPS):
                start_down(step)
                start_up(step)
            for i in range(1, len(loads)):
                load(i).start()

        @pl.loop(0, STEPS)
        def _(step):
            cols = pl.ds(pl.multiple_of(step * width, width), width)

            @pl.when(jnp.logical_not(f_on) & (step > 0))
            def _():
                await_down(step)
                await_up(step)

            dq = (mm_nt(e_v[...], down_v[cols, :]) * gz_v[:, cols].astype(F32)).astype(BF16)
            dq_v[:, cols] = dq
            vec_v[0:1, cols] = jnp.sum(dq.astype(F32), axis=0, keepdims=True)
            acc_v[...] += mm_nt(dq, up_v[:, cols])

        back(1).start()
        reload(1)
        _, grad = norm_back(h1_v[...].astype(F32), acc_v[...], grad, 1)
        f1 = grad.astype(BF16)
        reload(2)
        dq = (mm(down_w[...], f1) * gt_v[...].astype(F32)).astype(BF16)
        reload(3)
        centred, grad = norm_back(h0_v[...].astype(F32), mm(up_w[...], dq), f1.astype(F32), 0)
        out_v[1] = grad.astype(BF16)
        deliver(1, b_slot, far)
        n1 = (centred * gains[0:1, :] + shifts[0:1, :]).astype(BF16)
        reload(4)
        da_v[...] = mm_nt(n1, dq)
        back(2).start()
        db_v[...] = mm_nt(f1, zt_v[...])
        back(3).start()
        ones = jnp.ones((8, channels), BF16)
        vec_v[6:7, 0:hidden_t] = mm_nt(ones, dq)[0:1]
        vec_v[7:8, 0:rows] = mm_nt(ones, f1)[0:1]
        back(4).start()

    near = jnp.logical_not(far)

    if not late_call:
        fetched(*forward_in)

        @pl.when(f_on)
        def _():
            run_forward()

        @pl.when((f_job >= 0) & jnp.logical_not(f_on))
        def _():
            out_v[0] = h0_v[...] * tab[VALID, f_slot].astype(F32).astype(BF16)

        @pl.when(f_job >= 0)
        def _():
            deliver(0, f_slot, near)

    if not first_call:
        fetched(*backward_in)

        @pl.when(b_on)
        def _():
            run_backward()

        @pl.when((b_job >= 0) & jnp.logical_not(b_on))
        def _():
            out_v[1] = e_v[...] * tab[VALID, b_slot].astype(F32).astype(BF16)
            deliver(1, b_slot, far)

        @pl.when(b_job >= 0)
        def _():
            delivered(1, b_slot, far)

        @pl.when(b_on)
        def _():
            for i in range(5):
                back(i).wait()

    if not late_call:
        @pl.when(f_job >= 0)
        def _():
            delivered(0, f_slot, near)

        @pl.when(f_on)
        def _():
            save(5).wait()
            save(6).wait()

        @pl.when(f_on & jnp.logical_not(b_on))
        def _():
            for i in range(5):
                save(i).wait()


def parcel_rows(patches, hidden_t):
    spans = {}
    row = hidden_t // 2
    for name, height in (("up_bias", 1), ("down_bias", 1), ("w", 1), ("gain", 1), ("shift", 1), ("u", 2)):
        spans[name] = row
        row += height
    return spans, -(-row // 16) * 16


def parcel_body(spans, up, down, up_bias, down_bias, u, w, gain, shift, out, all_v):
    hidden_t = up.shape[1]
    lanes = all_v.shape[1]
    all_v[...] = jnp.zeros_like(all_v)
    all_v[0:up.shape[0], 0:hidden_t] = up[...].astype(F32)
    all_v[0:down.shape[0], hidden_t:hidden_t + down.shape[1]] = down[...].astype(F32)
    for name, part in (("up_bias", up_bias), ("down_bias", down_bias), ("w", w), ("gain", gain), ("shift", shift)):
        row = part[...].astype(F32).reshape(1, -1)
        all_v[spans[name]:spans[name] + 1, 0:row.shape[1]] = row
    row = u[...].astype(F32).reshape(1, -1)
    for step in range(row.shape[1] // lanes):
        all_v[spans["u"] + step:spans["u"] + step + 1, :] = row[:, step * lanes:(step + 1) * lanes]
    out[...] = all_v[...].astype(BF16)


def parcel(spans, height, parts):
    channels = parts[6].shape[1]
    return pl.pallas_call(
        functools.partial(parcel_body, spans),
        out_shape=jax.ShapeDtypeStruct((height, channels), BF16),
        in_specs=[IN_VMEM] * len(parts),
        out_specs=IN_VMEM,
        scratch_shapes=[pltpu.VMEM((height, channels), F32)],
        cost_estimate=lasting(0.1),
        name="parcel",
    )(*parts)


def prep_body(spans, patches, tab, own_i, got_i, up_w, up_t, down_w, down_t, up_col, down_col, u_row, w_row, gains, shifts, up_v, down_v):
    first = tab[PLACE, HALF] == 0
    own = own_i[...].astype(F32)
    got = got_i[...].astype(F32)
    halves = jnp.where(first, own, got), jnp.where(first, got, own)
    hidden_t = up_w.shape[1]
    lanes = own.shape[1]

    def column(row):
        return jnp.broadcast_to(row, (8, row.shape[1])).T[:, 0:1]

    up_v[...] = jnp.zeros_like(up_v)
    down_v[...] = jnp.zeros_like(down_v)
    down_col[...] = jnp.zeros_like(down_col)
    for side, half in enumerate(halves):
        size = patches // 2
        up_v[side * size:(side + 1) * size, :] = half[0:size, 0:hidden_t]
        down_col[side * size:(side + 1) * size, :] = column(half[spans["down_bias"]:spans["down_bias"] + 1, 0:size])
        size = hidden_t // 2
        down_v[side * size:(side + 1) * size, 0:patches] = half[0:size, hidden_t:hidden_t + patches]
        up_col[side * size:(side + 1) * size, :] = column(half[spans["up_bias"]:spans["up_bias"] + 1, 0:size])
        size = w_row.shape[1] // 2
        w_row[:, side * size:(side + 1) * size] = half[spans["w"]:spans["w"] + 1, 0:size]
        gains[side:side + 1, :] = half[spans["gain"]:spans["gain"] + 1, :]
        shifts[side:side + 1, :] = half[spans["shift"]:spans["shift"] + 1, :]
        steps = u_row.shape[1] // 2 // lanes
        for step in range(steps):
            at = (side * steps + step) * lanes
            u_row[:, at:at + lanes] = half[spans["u"] + step:spans["u"] + step + 1, :]
    up_w[...] = up_v[...].astype(BF16)
    up_t[...] = up_v[...].T.astype(BF16)
    down_w[...] = down_v[...].astype(BF16)
    down_t[...] = down_v[...].T.astype(BF16)


def prep(spans, patches, rows, hidden_t, ff, tab, own, got):
    channels = own.shape[1]
    names = ("up_w", "up_t", "down_w", "down_t", "up_col", "down_col", "u_row", "w_row", "gains", "shifts")
    sizes = [(rows, hidden_t), (hidden_t, rows), (hidden_t, rows), (rows, hidden_t), (hidden_t, 1), (rows, 1),
             (1, ff), (1, channels), (2, channels), (2, channels)]
    out = pl.pallas_call(
        functools.partial(prep_body, spans, patches),
        out_shape=[jax.ShapeDtypeStruct(size, BF16 if i < 4 else F32) for i, size in enumerate(sizes)],
        in_specs=[IN_SMEM] + [IN_VMEM] * 2,
        out_specs=[IN_VMEM] * len(sizes),
        scratch_shapes=[pltpu.VMEM((rows, hidden_t), F32), pltpu.VMEM((hidden_t, rows), F32)],
        compiler_params=pltpu.CompilerParams(vmem_limit_bytes=VMEM_BYTES),
        cost_estimate=lasting(0.1),
        name="prep",
    )(tab, own, got)
    return dict(zip(names, out))


def tick_call(tick, tab, images, cots, recv, w, kept, after=()):
    patches, channels = images.shape[1:]
    rows = recv.shape[0]
    ff = w["own_up"].shape[1]
    hidden_t = w["up_t"].shape[0]
    sections = 4
    shape = jax.ShapeDtypeStruct
    upper = -(-rows // 32) * 16
    slab = shape((2, SLOTS, upper, 2 * channels // sections), BF16)
    wide = shape((SLOTS, rows, ff), BF16)
    tall = shape((SLOTS, hidden_t, channels), BF16)
    plain = shape((SLOTS, rows, channels), BF16)
    shapes = [shape((rows, channels), BF16), slab, slab, shape((2,) + slab.shape, BF16)] + [wide, wide, tall, tall, plain, plain, plain, plain, wide,
              shape((SLOTS, rows, hidden_t), F32), shape((SLOTS, rows, hidden_t), F32), shape((SLOTS, 8, ff), F32)]
    names = ("own_up", "got_up", "own_down", "got_down", "up_w", "up_t", "down_w", "down_t", "up_col", "down_col", "u_row", "w_row", "gains", "shifts")
    ins = [tab, images, cots, recv] + [w[k] for k in names]
    specs = [IN_SMEM] + [IN_ANY] * 7 + [IN_VMEM] * 10
    if tick is not None:
        ins.insert(0, tick.reshape(1))
        specs.insert(0, IN_SMEM)
    ins += list(after)
    specs += [IN_ANY] * len(after)
    first = len(ins)
    passed = 0
    aliases = {}
    if kept is not None:
        passed = len(kept)
        aliases = {first + i: 1 + i for i in range(passed)}
        ins += list(kept)
        specs += [IN_ANY] * passed

    def trimmed(*refs):
        tick_body("both" if tick is not None else "first" if kept is None else "last", *refs[:first - len(after)], *refs[first + passed:])

    vmem = pltpu.VMEM
    line = vmem((rows, channels), BF16)
    broad = vmem((rows, ff), BF16)
    high = vmem((hidden_t, channels), BF16)
    dma = pltpu.SemaphoreType.DMA
    out = pl.pallas_call(
        trimmed,
        out_shape=shapes,
        in_specs=specs,
        out_specs=[IN_ANY] * len(shapes),
        input_output_aliases=aliases,
        scratch_shapes=[vmem((channels, ff), BF16), vmem((ff, channels), BF16), vmem((2, patches, channels), BF16), line, line, line, line,
                        broad, broad, high, high, broad, vmem((rows, channels), F32), vmem((2, rows, channels), BF16),
                        vmem((2, sections, upper, 2 * channels // sections), BF16),
                        vmem((rows, hidden_t), F32), vmem((rows, hidden_t), F32), vmem((8, ff), F32),
                        dma((3, STEPS)), dma((2,)), dma((5,)), dma((2, sections + 1)), dma((7,)), dma((5,))],
        compiler_params=pltpu.CompilerParams(vmem_limit_bytes=VMEM_BYTES),
        cost_estimate=lasting(8),
        name="tick" if tick is not None else "late_tick",
    )(*ins)
    return out[0], tuple(out[1:])


def position(relative, bits):
    place = 0
    for bit in bits:
        place = place * 2 + ((relative >> bit) & 1)
    return place


def down_grad_body(chunks, count, orders, aligned, tab, f_i, z_i, rider_i, *refs):
    outs, made, (f_v, ft_v, z_v, f_sems, z_sems, out_sems) = refs[:2 * chunks], refs[2 * chunks:4 * chunks], refs[4 * chunks:]
    half = tab[PLACE, HALF]
    me = tab[PLACE, ME]
    width = outs[0].shape[-1]
    channels = f_i.shape[2]
    rows = f_i.shape[1]
    size = z_i.shape[2] // 2
    tile = 256 if width % 256 == 0 else width
    piece = channels // count
    extra = rider_i.shape[1] // count if aligned else 0

    def z_copy(slot, which):
        first = pl.multiple_of(jnp.where(half == which % 2, 1, 0) * size + which // 2 * width, 128)
        return pltpu.make_async_copy(z_i.at[slot, :, pl.ds(first, width)], z_v.at[which, pl.ds(slot * rows, rows), :], z_sems.at[which, slot])

    def f_copy(slot):
        return pltpu.make_async_copy(f_i.at[slot], f_v.at[pl.ds(slot * rows, rows), :], f_sems.at[slot])

    for slot in range(SLOTS):
        @pl.when(tab[ON, slot] == 1)
        def _():
            f_copy(slot).start()

        @pl.when(tab[ON, slot] != 1)
        def _():
            f_v[pl.ds(slot * rows, rows), :] = jnp.zeros((rows, channels), BF16)

    for which in range(2 * chunks):
        for slot in range(SLOTS):
            @pl.when(tab[ON, slot] == 1)
            def _():
                z_copy(slot, which).start()

            @pl.when(tab[ON, slot] != 1)
            def _():
                z_v[which, pl.ds(slot * rows, rows), :] = jnp.zeros((rows, width), BF16)

    for slot in range(SLOTS):
        @pl.when(tab[ON, slot] == 1)
        def _():
            f_copy(slot).wait()

    ft_v[...] = f_v[...].T
    copies = [pltpu.make_async_copy(made[which], outs[which], out_sems.at[which]) for which in range(2 * chunks)]
    for which, out in enumerate(made):
        for slot in range(SLOTS):
            @pl.when(tab[ON, slot] == 1)
            def _():
                z_copy(slot, which).wait()

        each = piece + (extra if which < 2 else 0)
        first = [pl.multiple_of(position(d ^ me, orders[which // 2]) * each, 16) for d in range(count)]

        @pl.loop(0, width // tile)
        def _(step):
            cols = pl.ds(pl.multiple_of(step * tile, tile), tile)
            total = mm(ft_v[...], z_v[which, :, cols]).astype(BF16)
            if aligned:
                for d in range(count):
                    out[pl.ds(first[d], piece), cols] = total[d * piece:(d + 1) * piece]
            else:
                out[:, cols] = total

        if extra and which < 2:
            for d in range(count):
                out[pl.ds(first[d] + piece, extra), :] = rider_i[which, d * extra:(d + 1) * extra, :]

        copies[which].start()

    for copy in copies:
        copy.wait()


def up_grad_body(chunks, height, count, orders, aligned, tab, n_i, dq_i, *refs):
    outs, made, (n_v, nt_v, dq_v, n_sems, dq_sems, out_sems) = refs[:2 * chunks], refs[2 * chunks:4 * chunks], refs[4 * chunks:]
    half = tab[PLACE, HALF]
    me = tab[PLACE, ME]
    rows = n_i.shape[1]
    size = n_i.shape[2] // 2
    ff = dq_i.shape[2]

    def n_copy(slot):
        return pltpu.make_async_copy(n_i.at[slot], n_v.at[pl.ds(slot * rows, rows), :], n_sems.at[slot])

    def dq_copy(side, slot):
        cols = pl.ds(side * (ff // 2), ff // 2)
        return pltpu.make_async_copy(dq_i.at[slot, :, cols], dq_v.at[pl.ds(slot * rows, rows), cols], dq_sems.at[side, slot])

    for slot in range(SLOTS):
        @pl.when(tab[ON, slot] == 1)
        def _():
            n_copy(slot).start()

        @pl.when(tab[ON, slot] != 1)
        def _():
            n_v[pl.ds(slot * rows, rows), :] = jnp.zeros((rows, 2 * size), BF16)
            dq_v[pl.ds(slot * rows, rows), :] = jnp.zeros((rows, ff), BF16)

    for side in range(2):
        for slot in range(SLOTS):
            @pl.when(tab[ON, slot] == 1)
            def _():
                dq_copy(side, slot).start()

    for slot in range(SLOTS):
        @pl.when(tab[ON, slot] == 1)
        def _():
            n_copy(slot).wait()

    turned = n_v[...].T
    for fixed in range(2):
        side = jnp.where(half == fixed, 1, 0)
        for chunk in range(chunks):
            first = fixed * size + chunk * height
            nt_v[chunk, pl.ds(pl.multiple_of(side * height, 16), height), :] = turned[first:first + height]

    piece = ff // count if aligned else 384
    copies = [pltpu.make_async_copy(made[i], outs[i], out_sems.at[i]) for i in range(2 * chunks)]
    for chunk in range(chunks):
        theirs_v, mine_v = made[2 * chunk:2 * chunk + 2]
        for side in range(2):
            if chunk == 0:
                for slot in range(SLOTS):
                    @pl.when(tab[ON, slot] == 1)
                    def _():
                        dq_copy(side, slot).wait()

            @pl.loop(side * (ff // piece // 4), (side + 1) * (ff // piece // 4))
            def _(pair):
                cols = pl.ds(pl.multiple_of(pair * 2 * piece, 128), 2 * piece)
                total = mm(nt_v[chunk], dq_v[:, cols]).astype(BF16)
                if not aligned:
                    theirs_v[:, cols] = total[:height]
                    mine_v[:, cols] = total[height:]
                    return
                for i in range(2):
                    place = pl.ds(pl.multiple_of(position((2 * pair + i) ^ me, orders[chunk]) * height, 16), height)
                    theirs_v[place, :] = total[:height, i * piece:(i + 1) * piece]
                    mine_v[place, :] = total[height:, i * piece:(i + 1) * piece]

        copies[2 * chunk].start()
        copies[2 * chunk + 1].start()

    for copy in copies:
        copy.wait()


def arranged(pieces, bits):
    count = pieces.shape[0]
    order = [0] * count
    for relative in range(count):
        order[position(relative, bits)] = relative
    return jnp.take(pieces, jnp.array(order) ^ lax.axis_index("dp"), axis=0)


def down_grad_call(chunks, count, orders, tab, f, z, rider, after):
    slots, rows, channels = f.shape
    width = z.shape[2] // 2 // chunks
    piece = channels // count
    aligned = piece % 16 == 0
    extra = rider.shape[1] if aligned else 0
    shapes = [(channels + (extra if i == 0 else 0), width) for i in range(chunks)]
    out = launch(
        functools.partial(down_grad_body, chunks, count, orders, aligned), [tab, f, z, rider], [IN_SMEM, IN_ANY, IN_ANY, IN_VMEM], after,
        out_shape=[jax.ShapeDtypeStruct(shapes[i // 2], BF16) for i in range(2 * chunks)],
        out_specs=[IN_ANY] * (2 * chunks),
        scratch_shapes=[pltpu.VMEM(shapes[i // 2], BF16) for i in range(2 * chunks)]
                       + [pltpu.VMEM((slots * rows, channels), BF16), pltpu.VMEM((channels, slots * rows), BF16),
                          pltpu.VMEM((2 * chunks, slots * rows, width), BF16),
                          pltpu.SemaphoreType.DMA((slots,)), pltpu.SemaphoreType.DMA((2 * chunks, slots)), pltpu.SemaphoreType.DMA((2 * chunks,))],
        compiler_params=pltpu.CompilerParams(vmem_limit_bytes=VMEM_BYTES),
        cost_estimate=lasting(9),
        name="down_grad",
    )
    if not aligned:
        out = [arranged(part.reshape(count, piece, width), orders[i // 2]).reshape(part.shape) for i, part in enumerate(out)]
    return [out[2 * i:2 * i + 2] for i in range(chunks)]


def up_grad_call(chunks, count, orders, tab, n, dq, after):
    slots, rows, channels = n.shape
    ff = dq.shape[2]
    height = channels // 2 // chunks
    piece = ff // count
    aligned = piece % 128 == 0
    shape = (count * height, piece) if aligned else (height, ff)
    out = launch(
        functools.partial(up_grad_body, chunks, height, count, orders, aligned), [tab, n, dq], [IN_SMEM, IN_ANY, IN_ANY], after,
        out_shape=[jax.ShapeDtypeStruct(shape, BF16)] * (2 * chunks),
        out_specs=[IN_ANY] * (2 * chunks),
        scratch_shapes=[pltpu.VMEM(shape, BF16)] * (2 * chunks)
                       + [pltpu.VMEM((slots * rows, channels), BF16), pltpu.VMEM((chunks, 2 * height, slots * rows), BF16),
                          pltpu.VMEM((slots * rows, ff), BF16),
                          pltpu.SemaphoreType.DMA((slots,)), pltpu.SemaphoreType.DMA((2, slots)), pltpu.SemaphoreType.DMA((2 * chunks,))],
        compiler_params=pltpu.CompilerParams(vmem_limit_bytes=VMEM_BYTES),
        cost_estimate=lasting(9),
        name="up_grad",
    )
    if not aligned:
        out = [arranged(jnp.swapaxes(part.reshape(height, count, piece), 0, 1), orders[i // 2]).reshape(count * height, piece) for i, part in enumerate(out)]
    return [out[2 * i:2 * i + 2] for i in range(chunks)]


def halved_body(mine, got, kept, sent):
    middle = kept.shape[0]
    low, high = pl.ds(0, middle), pl.ds(middle, middle)
    sent[...] = (mine[high, :].astype(F32) + got[high, :].astype(F32)).astype(BF16)
    kept[...] = (mine[low, :].astype(F32) + got[low, :].astype(F32)).astype(BF16)


def halved(mine, got, after):
    size, width = mine.shape
    return launch(halved_body, [mine, got], [IN_VMEM] * 2, after,
                  out_shape=[jax.ShapeDtypeStruct((size // 2, width), BF16)] * 2, out_specs=[IN_VMEM] * 2,
                  compiler_params=pltpu.CompilerParams(vmem_limit_bytes=VMEM_BYTES), cost_estimate=lasting(2), name="halved")


def summed_body(kind, mine, got, *refs):
    total = mine[...].astype(F32) + got[...].astype(F32)
    if kind == "above":
        first, out = refs
        out[0:first.shape[0]] = first[...]
        out[first.shape[0]:] = total
    elif kind == "beside":
        first, out = refs
        out[:, 0:first.shape[1]] = first[...]
        out[:, first.shape[1]:] = total
    else:
        out, *rest = refs
        out[...] = total[:out.shape[0]]
        for rider in rest:
            rider[...] = total[out.shape[0]:].astype(BF16)


def summed(kind, mine, got, size, first, after):
    rows, width = mine.shape
    shape = jax.ShapeDtypeStruct
    ins = [mine, got]
    if kind == "above":
        shapes = [shape((first.shape[0] + rows, width), F32)]
    elif kind == "beside":
        shapes = [shape((rows, first.shape[1] + width), F32)]
    else:
        shapes = [shape((size, width), F32)] + [shape((rows - size, width), BF16)] * (rows > size)
    if first is not None:
        ins.append(first)
    return launch(functools.partial(summed_body, kind), ins, [IN_VMEM] * len(ins), after,
                  out_shape=shapes, out_specs=[IN_VMEM] * len(shapes),
                  compiler_params=pltpu.CompilerParams(vmem_limit_bytes=VMEM_BYTES), cost_estimate=lasting(0.1), name="summed")


def packing(patches, hidden_t, channels, ff):
    spans = {}
    row = 0
    for name, height in (("token", -(-patches // 2 // 8) * 8), ("chan_up_bias", ff // 2 // channels), ("biases", 1), ("gain", 1), ("shift", 1)):
        spans[name] = row
        row += height
    return spans, -(-row // 128) * 128, channels


def pack_body(spans, patches, tab, da_i, db_i, vec_i, out, da_v, db_v, vec_v, both_v, sems):
    half = tab[PLACE, HALF]
    lanes = both_v.shape[-1]
    hidden_t = db_v.shape[2]
    upper = patches // 2
    sources = ((da_i, da_v), (db_i, db_v), (vec_i, vec_v))

    def copy(kind, slot):
        return pltpu.make_async_copy(sources[kind][0].at[slot], sources[kind][1].at[slot], sems.at[kind, slot])

    for slot in range(SLOTS):
        @pl.when(tab[ON, slot] == 1)
        def _():
            for kind in range(3):
                copy(kind, slot).start()

        @pl.when(tab[ON, slot] != 1)
        def _():
            for _, buffer in sources:
                buffer[slot] = jnp.zeros(buffer.shape[1:], F32)

    for slot in range(SLOTS):
        @pl.when(tab[ON, slot] == 1)
        def _():
            for kind in range(3):
                copy(kind, slot).wait()

    da = (da_v[0] + da_v[1]) + (da_v[2] + da_v[3])
    db = (db_v[0] + db_v[1]) + (db_v[2] + db_v[3])
    vec = (vec_v[0] + vec_v[1]) + (vec_v[2] + vec_v[3])
    both_v[...] = jnp.zeros_like(both_v)
    ff = vec.shape[1]
    channels = spans["channels"]
    for side in range(2):
        at = spans["token"]
        both_v[side, at:at + upper, 0:hidden_t] = da[side * upper:(side + 1) * upper]
        block = db[:, side * (hidden_t // 2):(side + 1) * (hidden_t // 2)]
        both_v[side, at:at + upper, hidden_t:hidden_t + hidden_t // 2] = block[:upper]
        both_v[side, at:at + upper, hidden_t + hidden_t // 2:2 * hidden_t] = block[upper:patches]

        def line(name, row, first, length, left=0):
            at = spans[name]
            for step in range(-(-length // lanes)):
                size = min(lanes, length - step * lanes)
                both_v[side, at + step:at + step + 1, left:left + size] = vec[row:row + 1, first + step * lanes:first + step * lanes + size]

        line("chan_up_bias", 0, side * (ff // 2), ff // 2)
        line("biases", 1, side * (channels // 2), channels // 2)
        line("biases", 6, side * (hidden_t // 2), hidden_t // 2, channels // 2)
        line("biases", 7, side * upper, upper, channels // 2 + hidden_t // 2)
        line("gain", 2 + side, 0, channels)
        line("shift", 4 + side, 0, channels)
    out[0] = both_v[1 - half].astype(BF16)
    out[1] = both_v[half].astype(BF16)


def unpack_body(spans, patches, hidden_t, relative, tab, parts, gain_o, shift_o, up_o, up_bias_o, down_o, down_bias_o, chan_up_bias_o, chan_down_bias_o, all_v):
    size = parts.shape[1]
    for i, shift in enumerate(relative):
        first = pl.multiple_of((tab[PLACE, ME] ^ shift) * size, 8) if len(relative) > 1 else 0
        all_v[pl.ds(first, size), :] = parts[i].astype(F32)
    upper = patches // 2
    lanes = all_v.shape[1]
    at = spans["token"]
    up_o[...] = all_v[at:at + upper, 0:hidden_t]
    block = all_v[at:at + -(-upper // 8) * 8, hidden_t:2 * hidden_t]
    down_o[:, 0:upper] = block[:, :hidden_t // 2].T[:, :upper]
    down_o[:, upper:patches] = block[:, hidden_t // 2:].T[:, :upper]
    gain_o[...] = all_v[spans["gain"]:spans["gain"] + 1, :]
    shift_o[...] = all_v[spans["shift"]:spans["shift"] + 1, :]
    for step in range(chan_up_bias_o.shape[1] // lanes):
        at = spans["chan_up_bias"] + step
        chan_up_bias_o[:, step * lanes:(step + 1) * lanes] = all_v[at:at + 1, :]
    row = all_v[spans["biases"]:spans["biases"] + 1, :]
    first = chan_down_bias_o.shape[1]
    chan_down_bias_o[...] = row[:, :first]
    up_bias_o[...] = row[:, first:first + hidden_t // 2]
    down_bias_o[...] = row[:, first + hidden_t // 2:first + hidden_t // 2 + upper]


def unpack(spans, patches, hidden_t, channels, ff, relative, tab, parts, after):
    sizes = [(1, channels), (1, channels), (patches // 2, hidden_t), (1, hidden_t // 2), (hidden_t // 2, patches), (1, patches // 2), (1, ff // 2), (1, channels // 2)]
    return launch(
        functools.partial(unpack_body, spans, patches, hidden_t, relative), [tab, parts], [IN_SMEM, IN_VMEM], after,
        out_shape=[jax.ShapeDtypeStruct(size, F32) for size in sizes],
        out_specs=[IN_VMEM] * len(sizes),
        scratch_shapes=[pltpu.VMEM((parts.shape[0] * parts.shape[1], parts.shape[2]), F32)],
        compiler_params=pltpu.CompilerParams(vmem_limit_bytes=VMEM_BYTES),
        cost_estimate=lasting(2),
        name="unpack",
    )


def both_body(first, second, out):
    out[0:first.shape[0]] = first[...]
    out[first.shape[0]:] = second[...]


def both(first, second, after):
    shape = (2 * first.shape[0],) + first.shape[1:]
    return launch(both_body, [first, second], [IN_VMEM] * 2, after, out_shape=jax.ShapeDtypeStruct(shape, first.dtype), out_specs=IN_VMEM,
                  compiler_params=pltpu.CompilerParams(vmem_limit_bytes=VMEM_BYTES), cost_estimate=lasting(2), name="both")


def split_body(both, first_o, second_o, sems):
    copies = [pltpu.make_async_copy(both.at[i], target, sems.at[i]) for i, target in enumerate((first_o, second_o))]
    for copy in copies:
        copy.start()
    for copy in copies:
        copy.wait()


def split(both, after):
    return launch(split_body, [both], [IN_ANY], after, out_shape=[jax.ShapeDtypeStruct(both.shape[1:], both.dtype)] * 2,
                  out_specs=[IN_VMEM] * 2, scratch_shapes=[pltpu.SemaphoreType.DMA((2,))],
                  compiler_params=pltpu.CompilerParams(vmem_limit_bytes=VMEM_BYTES), cost_estimate=lasting(0.1), name="split")


def place_body(tab, here, beside, across, corner, mixed_o, grad_o, mixed_v, grad_v, sems):
    layer = tab[PLACE, LAYER]
    half = tab[PLACE, HALF]
    sources = (here, beside, across, corner)
    places, width, patches = mixed_o.shape
    upper = mixed_v.shape[1]
    buffers = (mixed_v, grad_v)

    def copy(kind, place, source):
        return pltpu.make_async_copy(source.at[kind, place // 2], buffers[kind].at[tab[ORDER, place]], sems.at[kind, place])

    for place in range(places):
        for kind, row in enumerate((MIXED_FAR, GRAD_FAR)):
            which = jnp.where(tab[row, place] == layer, 0, 2) + jnp.where(half == place % 2, 0, 1)
            for i, source in enumerate(sources):
                @pl.when(which == i)
                def _():
                    copy(kind, place, source).start()

    for place in range(places):
        for kind in range(2):
            copy(kind, place, here).wait()

    @pl.loop(0, places)
    def _(i):
        for source, target in ((mixed_v, mixed_o), (grad_v, grad_o)):
            whole = jnp.concatenate([source[i, :, 0:width], source[i, :, width:2 * width]], 0)
            target[i] = whole.T[:, 0:patches]


def pack_call(spans, packed_rows, lanes, patches, channels, tab, da, db, vec, after):
    return launch(
        functools.partial(pack_body, dict(spans, channels=channels), patches), [tab, da, db, vec], [IN_SMEM] + [IN_ANY] * 3, after,
        out_shape=jax.ShapeDtypeStruct((2, packed_rows, lanes), BF16),
        out_specs=IN_VMEM,
        scratch_shapes=[pltpu.VMEM(da.shape, F32), pltpu.VMEM(db.shape, F32), pltpu.VMEM(vec.shape, F32),
                        pltpu.VMEM((2, packed_rows, lanes), F32), pltpu.SemaphoreType.DMA((3, SLOTS))],
        compiler_params=pltpu.CompilerParams(vmem_limit_bytes=VMEM_BYTES),
        cost_estimate=lasting(2.5),
        name="pack",
    )


def place_call(slot_count, patches, width, tab, slabs, after):
    out_shape = jax.ShapeDtypeStruct((slot_count, width, patches), BF16)
    buffer = pltpu.VMEM((slot_count,) + slabs[0].shape[2:], BF16)
    return launch(
        place_body, [tab] + list(slabs), [IN_SMEM] + [IN_ANY] * 4, after,
        out_shape=[out_shape, out_shape],
        out_specs=[IN_VMEM] * 2,
        scratch_shapes=[buffer, buffer, pltpu.SemaphoreType.DMA((2, slot_count))],
        compiler_params=pltpu.CompilerParams(vmem_limit_bytes=VMEM_BYTES),
        cost_estimate=lasting(4),
        name="place",
    )


def local(images, cotangent, valid_rows, skip_masks, norm_gain, norm_bias, token_up, token_up_bias, token_down,
          token_down_bias, chan_up, chan_up_bias, chan_down, chan_down_bias):
    count = lax.axis_size("dp")
    slot_count, patches, channels = images.shape
    rows = -(-patches // 16) * 16
    hidden_t = token_up.shape[1]
    ff = chan_up.shape[1]

    parcel_spans, height = parcel_rows(patches, hidden_t)
    own = parcel(parcel_spans, height, (token_up, token_down, token_up_bias, token_down_bias, chan_up_bias, chan_down_bias, norm_gain, norm_bias))
    got = flipped(own, "pipe", 1)
    got_up = flipped(chan_up, "pipe", 1)
    got_down = flipped(chan_down, "pipe", 1)

    tab, ticks = pl.pallas_call(
        table_body,
        out_shape=[jax.ShapeDtypeStruct((10, MOST), jnp.int32), jax.ShapeDtypeStruct((1,), jnp.int32)],
        in_specs=[IN_SMEM] * 4,
        out_specs=[IN_SMEM] * 2,
        cost_estimate=lasting(0.1),
        name="table",
    )(jnp.asarray(JOB_TABLE.reshape(-1, MOST)), jnp.asarray(TICK_TABLE[None, :]), valid_rows[None, :], skip_masks.T)

    weights = dict(prep(parcel_spans, patches, rows, hidden_t, ff, tab, own, got), own_up=chan_up, got_up=got_up, own_down=chan_down, got_down=got_down)
    blank = jnp.zeros((rows, channels), BF16)
    send, kept = tick_call(None, tab, images, cotangent, blank, weights, None)

    def one(tick, carried):
        send, recv, kept = carried
        arriving = flipped(send, "pipe", 2)
        send, kept = tick_call(tick, tab, images, cotangent, recv, weights, kept)
        return send, arriving, kept

    _, last, kept = lax.fori_loop(1, ticks[0], one, (send, blank, kept))
    kept = dict(zip(KEPT, kept))

    chunks = 2
    bits = tuple(range(count.bit_length() - 1))
    other_bits = (bits[1], bits[0]) + bits[2:]
    orders = (bits, other_bits, bits, other_bits)
    spans, packed_rows, lanes = packing(patches, hidden_t, channels, ff)

    made = []

    def step(function, *arrays):
        out = function(*arrays, after=tuple(made))
        made[:] = jax.tree.leaves(out)[:1]
        return out

    pieces = [None] * (2 * chunks)
    moving = [None] * (2 * chunks)

    def begin(which, pair):
        pieces[which] = pair[1]
        moving[which] = flipped(pair[0], "pipe", 1)

    def advance(which, stage):
        pieces[which], sent = step(halved, pieces[which], moving[which])
        moving[which] = flipped(sent, "dp", 1 << orders[which][stage])

    def finished(which, kind, first=None):
        size = channels // count if which < chunks else channels // 2 // chunks
        return step(summed, kind, pieces[which], moving[which], size, first)

    _, late_kept = step(tick_call, None, tab, images, cotangent, last, weights, tuple(kept[k] for k in KEPT))
    made[:] = late_kept[:1]
    kept = dict(zip(KEPT, late_kept))
    over = flipped(kept["slab23"], "pipe", 2)
    beside = flipped(kept["slab1"], "pipe", 1)
    rider = step(pack_call, spans, packed_rows, lanes, patches, channels, tab, kept["da"], kept["db"], kept["vec"])
    made.append(beside)
    for i, pair in enumerate(step(down_grad_call, chunks, count, orders[:chunks], tab, kept["f"], kept["z"], rider)):
        begin(i, pair)
    advance(0, 0)
    advance(1, 0)
    for i, pair in enumerate(step(up_grad_call, chunks, count, orders[chunks:], tab, kept["n2"], kept["dq"])):
        begin(chunks + i, pair)
    advance(0, 1)
    advance(1, 1)
    advance(2, 0)
    advance(3, 0)
    across, turned = step(split, over)
    corner = flipped(turned, "pipe", 1)
    for stage in range(2, len(bits)):
        advance(0, stage)
        advance(1, stage)
    advance(2, 1)
    width = channels // 4
    mixed, input_grad = step(place_call, slot_count, patches, width, tab, (kept["slab0"], beside, across, corner))
    advance(3, 1)
    down_first, *small = finished(0, "alone")
    parts = small[0][None] if small else None
    relative = [0]
    gathered = list(reversed(bits)) if small else []

    def gather():
        nonlocal parts, relative
        if gathered:
            bit = gathered.pop(0)
            parts = step(both, parts, flipped(parts, "dp", 1 << bit))
            relative += [i ^ (1 << bit) for i in relative]

    chan_down_grad, = finished(1, "beside", down_first)
    gather()
    for stage in range(2, len(bits)):
        advance(2, stage)
        advance(3, stage)
    while gathered:
        gather()
    if parts is None:
        total = rider[1].astype(F32) + flipped(rider[0], "pipe", 1).astype(F32)
        for bit in bits:
            sent = lax.optimization_barrier(total.astype(BF16))
            total = sent.astype(F32) + flipped(sent, "dp", 1 << bit).astype(F32)
        parts = total[None]
    gain, shift, token_up_grad, up_bias, token_down_grad, down_bias, chan_up_bias_grad, chan_down_bias_grad = step(
        unpack, spans, patches, hidden_t, channels, ff, relative, tab, parts)
    up_first, = finished(2, "alone")
    chan_up_grad, = finished(3, "above", up_first)

    return (
        jnp.swapaxes(mixed, 1, 2),
        jnp.swapaxes(input_grad, 1, 2),
        gain,
        shift,
        token_up_grad,
        up_bias[0],
        token_down_grad,
        down_bias[0],
        chan_up_grad,
        chan_up_bias_grad[0],
        chan_down_grad.T,
        chan_down_bias_grad[0],
    )


def solution(mesh):
    placed = (
        P("dp", None, None),
        P("dp", None, None),
        P("dp"),
        P("dp", None),
        P("pipe", None),
        P("pipe", None),
        P("pipe", None),
        P("pipe"),
        P("pipe", None),
        P("pipe"),
        P("pipe", None),
        P("pipe"),
        P("pipe", None),
        P("pipe"),
    )
    return jax.shard_map(
        local,
        mesh=mesh,
        in_specs=placed,
        out_specs=(
            P("dp", None, "pipe"),
            P("dp", None, "pipe"),
            P("pipe", None),
            P("pipe", None),
            P("pipe", None),
            P("pipe"),
            P("pipe", None),
            P("pipe"),
            P("pipe", "dp"),
            P("pipe"),
            P("pipe", "dp"),
            P("pipe"),
        ),
        check_vma=False,
    )
```

```python
import functools

import jax
import jax.numpy as jnp
import numpy as np
from jax import lax
from jax.experimental import pallas as pl
from jax.experimental.pallas import tpu as pltpu
from jax.sharding import PartitionSpec as P

F32 = jnp.float32
BF16 = jnp.bfloat16
NORM_EPS = 1e-06
GELU_SCALE = 0.7978845608
GELU_CUBE = 0.044715
STEPS = 2
SLOTS = 4
VMEM_BYTES = 40 << 20

IN_VMEM = pl.BlockSpec(memory_space=pltpu.VMEM)
IN_ANY = pl.BlockSpec(memory_space=pl.ANY)
IN_SMEM = pl.BlockSpec(memory_space=pltpu.SMEM)


def lasting(microseconds):
    return pl.CostEstimate(flops=int(microseconds * 10e9), bytes_accessed=1, transcendentals=0)


ON, VALID, CROSSING, IMAGE, PLACE, FORWARD, BACKWARD, ORDER, MIXED_FAR, GRAD_FAR = range(10)
LAYER, HALF, ME, LATE, HOPS = range(5)

JOBS = [
    [(-1, -1, -1, -1), (0, 0, 0, 0), (1, 1, 1, 1), (2, 2, 2, 2), (3, 3, 3, 3)],
    [(0, -1, -1, -1), (1, 1, 1, 1), (2, 0, 2, 0), (3, 2, 3, 2), (-1, 3, 0, 3)],
    [(0, -1, -1, -1), (1, 2, -1, 2), (2, 0, 2, 0), (3, 1, 3, 1), (-1, 3, 0, 3)],
    [(0, -1, -1, -1), (1, -1, -1, -1), (2, 0, -1, 0), (3, 1, 3, 1), (-1, 2, 0, 2), (-1, 3, 1, 3)],
    [(0, -1, -1, -1), (1, -1, -1, -1), (2, 0, -1, 0), (3, 1, -1, 1), (-1, 2, 0, 2), (-1, 3, 1, 3), (-1, -1, 2, -1)],
]
MOST = 8
JOB_TABLE = np.full((len(JOBS), 4, MOST), -1, np.int32)
for _hops, _rows in enumerate(JOBS):
    for _tick, _row in enumerate(_rows):
        JOB_TABLE[_hops, :, _tick] = _row
TICK_TABLE = np.array([len(_rows) for _rows in JOBS], np.int32)


def flipped(block, axis, distance):
    count = lax.axis_size(axis)
    route = [(i, i ^ distance) for i in range(count) if i ^ distance < count]
    return lax.ppermute(block, axis, route)


def mm(left, right):
    return lax.dot_general(left, right, (((1,), (0,)), ((), ())), preferred_element_type=F32)


def mm_nt(left, right):
    return lax.dot_general(left, right, (((1,), (1,)), ((), ())), preferred_element_type=F32)


def gelu_pair(pre):
    square = pre * pre
    gate = 0.5 + 0.5 * jnp.tanh(pre * (GELU_SCALE + (GELU_SCALE * GELU_CUBE) * square))
    value = pre * gate
    slope = gate + value * (1.0 - gate) * (2 * GELU_SCALE + (6 * GELU_SCALE * GELU_CUBE) * square)
    return value.astype(BF16), slope.astype(BF16)


def normalised(hidden):
    centred = hidden - jnp.mean(hidden, axis=-1, keepdims=True)
    scale = lax.rsqrt(jnp.mean(centred * centred, axis=-1, keepdims=True) + NORM_EPS)
    return centred * scale, scale


def launch(body, ins, specs, after, **options):
    first = len(ins)

    def trimmed(*refs):
        body(*refs[:first], *refs[first + len(after):])

    return pl.pallas_call(trimmed, in_specs=specs + [IN_ANY] * len(after), **options)(*ins, *after)


def table_body(jobs, ticks, valid, skip, tab, ticks_o):
    section = lax.axis_index("pipe")
    layer, half, me = section // 2, section % 2, lax.axis_index("dp")
    total = valid.shape[1]
    far = layer == 1
    firsts = [valid[0, i] * skip[0, i] for i in range(total)]
    seconds = [valid[0, i] * skip[1, i] for i in range(total)]
    kinds = [jnp.where(a * b == 1, 0, jnp.where(b == 1, 1, jnp.where(a == 1, 2, 3))) for a, b in zip(firsts, seconds)]
    crossing = sum(a * b for a, b in zip(firsts, seconds))
    hops = (crossing + 1) // 2
    for i in range(total):
        place = sum(((kinds[j] < kinds[i]) if j > i else (kinds[j] <= kinds[i])).astype(jnp.int32) for j in range(total) if j != i)
        tab[ORDER, place] = i
        tab[MIXED_FAR, place] = 1 - firsts[i] * (1 - seconds[i])
        tab[GRAD_FAR, place] = seconds[i] * (1 - firsts[i])

        @pl.when(place % 2 == half)
        def _():
            slot = place // 2
            tab[ON, slot] = jnp.where(far, seconds[i], firsts[i])
            tab[VALID, slot] = valid[0, i]
            tab[CROSSING, slot] = firsts[i] * seconds[i]
            tab[IMAGE, slot] = i

    tab[PLACE, LAYER] = layer
    tab[PLACE, HALF] = half
    tab[PLACE, ME] = me
    tab[PLACE, LATE] = jnp.where(far | (hops == 1), -1, hops - 1)
    tab[PLACE, HOPS] = hops
    ticks_o[0] = ticks[0, hops]
    for tick in range(MOST):
        tab[FORWARD, tick] = jobs[hops * 4 + layer, tick]
        tab[BACKWARD, tick] = jobs[hops * 4 + 2 + layer, tick]


KEPT = ("slab0", "slab1", "slab23", "z", "gz", "zt", "gt", "h0", "h1", "n2", "f", "dq", "da", "db", "vec")


def tick_body(phases, *refs):
    late_call = phases == "last"
    first_call = phases == "first"
    refs = list(refs)
    tick_ref = None if late_call or first_call else refs.pop(0)
    (tab, images, cots, recv, own_up, got_up, own_down, got_down,
     up_w, up_t, down_w, down_t, up_col, down_col, u_row, w_row, gains, shifts,
     send_o, slab0, slab1, slab23, z_o, gz_o, zt_o, gt_o, h0_o, h1_o, n2_o, f_o, dq_o, da_o, db_o, vec_o,
     up_v, down_v, raw_v, e_v, h0_v, h1_v, n2_v, z_v, gz_v, zt_v, gt_v, dq_v, acc_v, out_v, part_v, da_v, db_v, vec_v,
     w_sems, in_sems, load_sems, slab_sems, keep_sems, back_sems) = refs
    far = tab[PLACE, LAYER] == 1
    half = tab[PLACE, HALF]
    section = tab[PLACE, LAYER] * 2 + half
    slabs = (slab0, slab1, slab23.at[0], slab23.at[1])
    patches, channels = raw_v.shape[1:]
    rows = h0_v.shape[0]
    ff = up_v.shape[1]
    hidden_t = zt_v.shape[0]
    width = ff // STEPS
    part = channels // len(slabs)
    if late_call:
        f_job = jnp.int32(-1)
        b_job = tab[PLACE, LATE]
    elif first_call:
        f_job = tab[FORWARD, 0]
        b_job = jnp.int32(-1)
    else:
        f_job = tab[FORWARD, tick_ref[0]]
        b_job = tab[BACKWARD, tick_ref[0]]
    f_slot = jnp.maximum(f_job, 0)
    b_slot = jnp.maximum(b_job, 0)
    f_on = (f_job >= 0) & (tab[ON, f_slot] == 1)
    b_on = (b_job >= 0) & (tab[ON, b_slot] == 1)
    any_on = f_on | b_on

    def weight_copies(step):
        size = channels // 2
        cols = pl.ds(pl.multiple_of(step * width, width), width)
        own = pl.ds(pl.multiple_of(half * size, 16), size)
        rest = pl.ds(pl.multiple_of((1 - half) * size, 16), size)
        local = pl.ds(pl.multiple_of((step % (STEPS // 2)) * width, width), width)
        return (lambda: pltpu.make_async_copy(own_up.at[:, cols], up_v.at[own, cols], w_sems.at[0, step]),
                lambda: pltpu.make_async_copy(got_up.at[:, cols], up_v.at[rest, cols], w_sems.at[1, step]),
                lambda: pltpu.make_async_copy(own_down.at[local, :], down_v.at[cols, :], w_sems.at[2, step]),
                lambda: pltpu.make_async_copy(got_down.at[local, :], down_v.at[cols, :], w_sems.at[2, step]))

    def start_up(step):
        own, rest, _, _ = weight_copies(step)
        own().start()
        rest().start()

    def start_down(step):
        _, _, mine, theirs = weight_copies(step)

        @pl.when(step // (STEPS // 2) == half)
        def _():
            mine().start()

        @pl.when(step // (STEPS // 2) != half)
        def _():
            theirs().start()

    def await_up(step):
        own, rest, _, _ = weight_copies(step)
        own().wait()
        rest().wait()

    def await_down(step):
        weight_copies(step)[2]().wait()

    def fetch(kind, job, slot, crossed, source, target):
        @pl.when((job >= 0) & crossed)
        def _():
            pltpu.make_async_copy(recv, target, in_sems.at[kind]).start()

        @pl.when((job >= 0) & jnp.logical_not(crossed))
        def _():
            pltpu.make_async_copy(source.at[tab[IMAGE, slot]], raw_v.at[kind], in_sems.at[kind]).start()

    def fetched(kind, job, slot, crossed, source, target):
        @pl.when((job >= 0) & crossed)
        def _():
            pltpu.make_async_copy(recv, target, in_sems.at[kind]).wait()

        @pl.when((job >= 0) & jnp.logical_not(crossed))
        def _():
            pltpu.make_async_copy(source.at[tab[IMAGE, slot]], raw_v.at[kind], in_sems.at[kind]).wait()
            target[pl.ds(rows - 16, 16), :] = jnp.zeros((16, channels), BF16)
            target[pl.ds(0, patches), :] = raw_v[kind]

    forward_in = (0, f_job, f_slot, far & (tab[CROSSING, f_slot] == 1), images, h0_v)
    backward_in = (1, b_job, b_slot, jnp.logical_not(far) & (tab[CROSSING, b_slot] == 1), cots, e_v)
    loads = ((gz_o, gz_v), (h1_o, h1_v), (gt_o, gt_v), (h0_o, h0_v), (zt_o, zt_v))

    def load(i):
        return pltpu.make_async_copy(loads[i][0].at[b_slot], loads[i][1], load_sems.at[i])

    def reload(i):
        @pl.when(jnp.logical_not(f_on))
        def _():
            load(i).wait()

    if not late_call:
        fetch(*forward_in)

    @pl.when(f_on)
    def _():
        for step in range(STEPS):
            start_up(step)
        for step in range(STEPS):
            start_down(step)

    fetch(*backward_in)

    @pl.when(b_on & jnp.logical_not(f_on))
    def _():
        load(0).start()
        start_down(0)
        start_up(0)

    def slab_copy(kind, slot, flip):
        return pltpu.make_async_copy(part_v.at[kind, section ^ flip], slabs[flip].at[kind, slot], slab_sems.at[kind, flip])

    def send_copy(kind):
        return pltpu.make_async_copy(out_v.at[kind], send_o, slab_sems.at[kind, len(slabs)])

    def deliver(kind, slot, sends):
        @pl.when(sends)
        def _():
            send_copy(kind).start()

        @pl.when(jnp.logical_not(sends & (tab[CROSSING, slot] == 1)))
        def _():
            whole = out_v[kind]
            upper = part_v.shape[2]
            for d in range(len(slabs)):
                part_v[kind, d, :, 0:part] = whole[:upper, d * part:(d + 1) * part]
                part_v[kind, d, 0:rows - upper, part:2 * part] = whole[upper:, d * part:(d + 1) * part]
            for flip in range(len(slabs)):
                slab_copy(kind, slot, flip).start()

    def delivered(kind, slot, sends):
        @pl.when(jnp.logical_not(sends & (tab[CROSSING, slot] == 1)))
        def _():
            for flip in range(len(slabs)):
                slab_copy(kind, slot, flip).wait()

        @pl.when(sends)
        def _():
            send_copy(kind).wait()

    saves = ((gz_v, gz_o), (zt_v, zt_o), (gt_v, gt_o), (h0_v, h0_o), (h1_v, h1_o), (z_v, z_o), (n2_v, n2_o))

    def save(i):
        return pltpu.make_async_copy(saves[i][0], saves[i][1].at[f_slot], keep_sems.at[i])

    def run_forward():
        h0 = h0_v[...].astype(F32)
        centred, _ = normalised(h0)
        n1 = (centred * gains[0:1, :] + shifts[0:1, :]).astype(BF16)
        value, slope = gelu_pair(mm(up_t[...], n1) + up_col[...])
        zt_v[...] = value
        gt_v[...] = slope
        h1 = (h0 + (mm(down_t[...], value) + down_col[...])).astype(BF16)
        h1_v[...] = h1
        h1 = h1.astype(F32)
        centred, _ = normalised(h1)
        n2_v[...] = (centred * gains[1:2, :] + shifts[1:2, :]).astype(BF16)
        save(6).start()

        @pl.when(jnp.logical_not(b_on))
        def _():
            for i in range(1, 5):
                save(i).start()

        for step in range(STEPS):
            await_up(step)
        value, slope = gelu_pair(mm(n2_v[...], up_v[...]) + u_row[...])
        z_v[...] = value
        gz_v[...] = slope
        save(5).start()

        @pl.when(jnp.logical_not(b_on))
        def _():
            save(0).start()

        for step in range(STEPS):
            await_down(step)
        out_v[0] = (h1 + w_row[...] + mm(z_v[...], down_v[...])).astype(BF16)

    def norm_back(hidden, dn, grad, row):
        centred, scale = normalised(hidden)
        vec_v[2 + row:3 + row, 0:channels] = jnp.sum(dn * centred, axis=0, keepdims=True)
        vec_v[4 + row:5 + row, 0:channels] = jnp.sum(dn, axis=0, keepdims=True)
        scaled = dn * gains[row:row + 1, :]
        along = jnp.mean(scaled * centred, axis=-1, keepdims=True)
        flat = jnp.mean(scaled, axis=-1, keepdims=True)
        return centred, grad + scale * (scaled - flat - centred * along)

    backs = ((e_v, f_o), (dq_v, dq_o), (da_v, da_o), (db_v, db_o), (vec_v, vec_o))

    def back(i):
        return pltpu.make_async_copy(backs[i][0], backs[i][1].at[b_slot], back_sems.at[i])

    def run_backward():
        back(0).start()
        grad = e_v[...].astype(F32)
        vec_v[...] = jnp.zeros_like(vec_v)
        vec_v[1:2, 0:channels] = jnp.sum(grad, axis=0, keepdims=True)
        acc_v[...] = jnp.zeros_like(acc_v)
        reload(0)

        @pl.when(jnp.logical_not(f_on))
        def _():
            await_down(0)
            await_up(0)
            for step in range(1, STEPS):
                start_down(step)
                start_up(step)
            for i in range(1, len(loads)):
                load(i).start()

        @pl.loop(0, STEPS)
        def _(step):
            cols = pl.ds(pl.multiple_of(step * width, width), width)

            @pl.when(jnp.logical_not(f_on) & (step > 0))
            def _():
                await_down(step)
                await_up(step)

            dq = (mm_nt(e_v[...], down_v[cols, :]) * gz_v[:, cols].astype(F32)).astype(BF16)
            dq_v[:, cols] = dq
            vec_v[0:1, cols] = jnp.sum(dq.astype(F32), axis=0, keepdims=True)
            acc_v[...] += mm_nt(dq, up_v[:, cols])

        back(1).start()
        reload(1)
        _, grad = norm_back(h1_v[...].astype(F32), acc_v[...], grad, 1)
        f1 = grad.astype(BF16)
        reload(2)
        dq = (mm(down_w[...], f1) * gt_v[...].astype(F32)).astype(BF16)
        reload(3)
        centred, grad = norm_back(h0_v[...].astype(F32), mm(up_w[...], dq), f1.astype(F32), 0)
        out_v[1] = grad.astype(BF16)
        deliver(1, b_slot, far)
        n1 = (centred * gains[0:1, :] + shifts[0:1, :]).astype(BF16)
        reload(4)
        da_v[...] = mm_nt(n1, dq)
        db_v[...] = mm_nt(f1, zt_v[...])
        ones = jnp.ones((8, channels), BF16)
        vec_v[6:7, 0:hidden_t] = mm_nt(ones, dq)[0:1]
        vec_v[7:8, 0:rows] = mm_nt(ones, f1)[0:1]
        for i in range(2, 5):
            back(i).start()

    near = jnp.logical_not(far)

    if not late_call:
        fetched(*forward_in)

        @pl.when(f_on)
        def _():
            run_forward()

        @pl.when((f_job >= 0) & jnp.logical_not(f_on))
        def _():
            out_v[0] = h0_v[...] * tab[VALID, f_slot].astype(F32).astype(BF16)

        @pl.when(f_job >= 0)
        def _():
            deliver(0, f_slot, near)

    if not first_call:
        fetched(*backward_in)

        @pl.when(b_on)
        def _():
            run_backward()

        @pl.when((b_job >= 0) & jnp.logical_not(b_on))
        def _():
            out_v[1] = e_v[...] * tab[VALID, b_slot].astype(F32).astype(BF16)
            deliver(1, b_slot, far)

        @pl.when(b_job >= 0)
        def _():
            delivered(1, b_slot, far)

        @pl.when(b_on)
        def _():
            for i in range(5):
                back(i).wait()

    if not late_call:
        @pl.when(f_job >= 0)
        def _():
            delivered(0, f_slot, near)

        @pl.when(f_on)
        def _():
            save(5).wait()
            save(6).wait()

        @pl.when(f_on & jnp.logical_not(b_on))
        def _():
            for i in range(5):
                save(i).wait()


def parcel_rows(patches, hidden_t):
    spans = {}
    row = hidden_t // 2
    for name, height in (("up_bias", 1), ("down_bias", 1), ("w", 1), ("gain", 1), ("shift", 1), ("u", 2)):
        spans[name] = row
        row += height
    return spans, -(-row // 16) * 16


def parcel_body(spans, up, down, up_bias, down_bias, u, w, gain, shift, out, all_v):
    hidden_t = up.shape[1]
    lanes = all_v.shape[1]
    all_v[...] = jnp.zeros_like(all_v)
    all_v[0:up.shape[0], 0:hidden_t] = up[...].astype(F32)
    all_v[0:down.shape[0], hidden_t:hidden_t + down.shape[1]] = down[...].astype(F32)
    for name, part in (("up_bias", up_bias), ("down_bias", down_bias), ("w", w), ("gain", gain), ("shift", shift)):
        row = part[...].astype(F32).reshape(1, -1)
        all_v[spans[name]:spans[name] + 1, 0:row.shape[1]] = row
    row = u[...].astype(F32).reshape(1, -1)
    for step in range(row.shape[1] // lanes):
        all_v[spans["u"] + step:spans["u"] + step + 1, :] = row[:, step * lanes:(step + 1) * lanes]
    out[...] = all_v[...].astype(BF16)


def parcel(spans, height, parts):
    channels = parts[6].shape[1]
    return pl.pallas_call(
        functools.partial(parcel_body, spans),
        out_shape=jax.ShapeDtypeStruct((height, channels), BF16),
        in_specs=[IN_VMEM] * len(parts),
        out_specs=IN_VMEM,
        scratch_shapes=[pltpu.VMEM((height, channels), F32)],
        cost_estimate=lasting(0.1),
        name="parcel",
    )(*parts)


def prep_body(spans, patches, tab, own_i, got_i, up_w, up_t, down_w, down_t, up_col, down_col, u_row, w_row, gains, shifts, up_v, down_v):
    first = tab[PLACE, HALF] == 0
    own = own_i[...].astype(F32)
    got = got_i[...].astype(F32)
    halves = jnp.where(first, own, got), jnp.where(first, got, own)
    hidden_t = up_w.shape[1]
    lanes = own.shape[1]

    def column(row):
        return jnp.broadcast_to(row, (8, row.shape[1])).T[:, 0:1]

    up_v[...] = jnp.zeros_like(up_v)
    down_v[...] = jnp.zeros_like(down_v)
    down_col[...] = jnp.zeros_like(down_col)
    for side, half in enumerate(halves):
        size = patches // 2
        up_v[side * size:(side + 1) * size, :] = half[0:size, 0:hidden_t]
        down_col[side * size:(side + 1) * size, :] = column(half[spans["down_bias"]:spans["down_bias"] + 1, 0:size])
        size = hidden_t // 2
        down_v[side * size:(side + 1) * size, 0:patches] = half[0:size, hidden_t:hidden_t + patches]
        up_col[side * size:(side + 1) * size, :] = column(half[spans["up_bias"]:spans["up_bias"] + 1, 0:size])
        size = w_row.shape[1] // 2
        w_row[:, side * size:(side + 1) * size] = half[spans["w"]:spans["w"] + 1, 0:size]
        gains[side:side + 1, :] = half[spans["gain"]:spans["gain"] + 1, :]
        shifts[side:side + 1, :] = half[spans["shift"]:spans["shift"] + 1, :]
        steps = u_row.shape[1] // 2 // lanes
        for step in range(steps):
            at = (side * steps + step) * lanes
            u_row[:, at:at + lanes] = half[spans["u"] + step:spans["u"] + step + 1, :]
    up_w[...] = up_v[...].astype(BF16)
    up_t[...] = up_v[...].T.astype(BF16)
    down_w[...] = down_v[...].astype(BF16)
    down_t[...] = down_v[...].T.astype(BF16)


def prep(spans, patches, rows, hidden_t, ff, tab, own, got):
    channels = own.shape[1]
    names = ("up_w", "up_t", "down_w", "down_t", "up_col", "down_col", "u_row", "w_row", "gains", "shifts")
    sizes = [(rows, hidden_t), (hidden_t, rows), (hidden_t, rows), (rows, hidden_t), (hidden_t, 1), (rows, 1),
             (1, ff), (1, channels), (2, channels), (2, channels)]
    out = pl.pallas_call(
        functools.partial(prep_body, spans, patches),
        out_shape=[jax.ShapeDtypeStruct(size, BF16 if i < 4 else F32) for i, size in enumerate(sizes)],
        in_specs=[IN_SMEM] + [IN_VMEM] * 2,
        out_specs=[IN_VMEM] * len(sizes),
        scratch_shapes=[pltpu.VMEM((rows, hidden_t), F32), pltpu.VMEM((hidden_t, rows), F32)],
        compiler_params=pltpu.CompilerParams(vmem_limit_bytes=VMEM_BYTES),
        cost_estimate=lasting(0.1),
        name="prep",
    )(tab, own, got)
    return dict(zip(names, out))


def tick_call(tick, tab, images, cots, recv, w, kept, after=()):
    patches, channels = images.shape[1:]
    rows = recv.shape[0]
    ff = w["own_up"].shape[1]
    hidden_t = w["up_t"].shape[0]
    sections = 4
    shape = jax.ShapeDtypeStruct
    upper = -(-rows // 32) * 16
    slab = shape((2, SLOTS, upper, 2 * channels // sections), BF16)
    wide = shape((SLOTS, rows, ff), BF16)
    tall = shape((SLOTS, hidden_t, channels), BF16)
    plain = shape((SLOTS, rows, channels), BF16)
    shapes = [shape((rows, channels), BF16), slab, slab, shape((2,) + slab.shape, BF16)] + [wide, wide, tall, tall, plain, plain, plain, plain, wide,
              shape((SLOTS, rows, hidden_t), F32), shape((SLOTS, rows, hidden_t), F32), shape((SLOTS, 8, ff), F32)]
    names = ("own_up", "got_up", "own_down", "got_down", "up_w", "up_t", "down_w", "down_t", "up_col", "down_col", "u_row", "w_row", "gains", "shifts")
    ins = [tab, images, cots, recv] + [w[k] for k in names]
    specs = [IN_SMEM] + [IN_ANY] * 7 + [IN_VMEM] * 10
    if tick is not None:
        ins.insert(0, tick.reshape(1))
        specs.insert(0, IN_SMEM)
    ins += list(after)
    specs += [IN_ANY] * len(after)
    first = len(ins)
    passed = 0
    aliases = {}
    if kept is not None:
        passed = len(kept)
        aliases = {first + i: 1 + i for i in range(passed)}
        ins += list(kept)
        specs += [IN_ANY] * passed

    def trimmed(*refs):
        tick_body("both" if tick is not None else "first" if kept is None else "last", *refs[:first - len(after)], *refs[first + passed:])

    vmem = pltpu.VMEM
    line = vmem((rows, channels), BF16)
    broad = vmem((rows, ff), BF16)
    high = vmem((hidden_t, channels), BF16)
    dma = pltpu.SemaphoreType.DMA
    out = pl.pallas_call(
        trimmed,
        out_shape=shapes,
        in_specs=specs,
        out_specs=[IN_ANY] * len(shapes),
        input_output_aliases=aliases,
        scratch_shapes=[vmem((channels, ff), BF16), vmem((ff, channels), BF16), vmem((2, patches, channels), BF16), line, line, line, line,
                        broad, broad, high, high, broad, vmem((rows, channels), F32), vmem((2, rows, channels), BF16),
                        vmem((2, sections, upper, 2 * channels // sections), BF16),
                        vmem((rows, hidden_t), F32), vmem((rows, hidden_t), F32), vmem((8, ff), F32),
                        dma((3, STEPS)), dma((2,)), dma((5,)), dma((2, sections + 1)), dma((7,)), dma((5,))],
        compiler_params=pltpu.CompilerParams(vmem_limit_bytes=VMEM_BYTES),
        cost_estimate=lasting(8),
        name="tick" if tick is not None else "late_tick",
    )(*ins)
    return out[0], tuple(out[1:])


def position(relative, bits):
    place = 0
    for bit in bits:
        place = place * 2 + ((relative >> bit) & 1)
    return place


def down_grad_body(chunks, count, orders, aligned, tab, f_i, z_i, rider_i, *refs):
    outs, made, (f_v, ft_v, z_v, f_sems, z_sems, out_sems) = refs[:2 * chunks], refs[2 * chunks:4 * chunks], refs[4 * chunks:]
    half = tab[PLACE, HALF]
    me = tab[PLACE, ME]
    width = outs[0].shape[-1]
    channels = f_i.shape[2]
    rows = f_i.shape[1]
    size = z_i.shape[2] // 2
    tile = 256 if width % 256 == 0 else width
    piece = channels // count
    extra = rider_i.shape[1] // count if aligned else 0

    def z_copy(slot, which):
        first = pl.multiple_of(jnp.where(half == which % 2, 1, 0) * size + which // 2 * width, 128)
        return pltpu.make_async_copy(z_i.at[slot, :, pl.ds(first, width)], z_v.at[which, pl.ds(slot * rows, rows), :], z_sems.at[which, slot])

    def f_copy(slot):
        return pltpu.make_async_copy(f_i.at[slot], f_v.at[pl.ds(slot * rows, rows), :], f_sems.at[slot])

    for slot in range(SLOTS):
        @pl.when(tab[ON, slot] == 1)
        def _():
            f_copy(slot).start()

        @pl.when(tab[ON, slot] != 1)
        def _():
            f_v[pl.ds(slot * rows, rows), :] = jnp.zeros((rows, channels), BF16)

    for which in range(2 * chunks):
        for slot in range(SLOTS):
            @pl.when(tab[ON, slot] == 1)
            def _():
                z_copy(slot, which).start()

            @pl.when(tab[ON, slot] != 1)
            def _():
                z_v[which, pl.ds(slot * rows, rows), :] = jnp.zeros((rows, width), BF16)

    for slot in range(SLOTS):
        @pl.when(tab[ON, slot] == 1)
        def _():
            f_copy(slot).wait()

    ft_v[...] = f_v[...].T
    copies = [pltpu.make_async_copy(made[which], outs[which], out_sems.at[which]) for which in range(2 * chunks)]
    for which, out in enumerate(made):
        for slot in range(SLOTS):
            @pl.when(tab[ON, slot] == 1)
            def _():
                z_copy(slot, which).wait()

        each = piece + (extra if which < 2 else 0)
        first = [pl.multiple_of(position(d ^ me, orders[which // 2]) * each, 16) for d in range(count)]

        @pl.loop(0, width // tile)
        def _(step):
            cols = pl.ds(pl.multiple_of(step * tile, tile), tile)
            total = mm(ft_v[...], z_v[which, :, cols]).astype(BF16)
            if aligned:
                for d in range(count):
                    out[pl.ds(first[d], piece), cols] = total[d * piece:(d + 1) * piece]
            else:
                out[:, cols] = total

        if extra and which < 2:
            for d in range(count):
                out[pl.ds(first[d] + piece, extra), :] = rider_i[which, d * extra:(d + 1) * extra, :]

        copies[which].start()

    for copy in copies:
        copy.wait()


def up_grad_body(chunks, height, count, orders, aligned, tab, n_i, dq_i, *refs):
    outs, made, (n_v, nt_v, dq_v, n_sems, dq_sems, out_sems) = refs[:2 * chunks], refs[2 * chunks:4 * chunks], refs[4 * chunks:]
    half = tab[PLACE, HALF]
    me = tab[PLACE, ME]
    rows = n_i.shape[1]
    size = n_i.shape[2] // 2
    ff = dq_i.shape[2]

    def n_copy(slot):
        return pltpu.make_async_copy(n_i.at[slot], n_v.at[pl.ds(slot * rows, rows), :], n_sems.at[slot])

    def dq_copy(side, slot):
        cols = pl.ds(side * (ff // 2), ff // 2)
        return pltpu.make_async_copy(dq_i.at[slot, :, cols], dq_v.at[pl.ds(slot * rows, rows), cols], dq_sems.at[side, slot])

    for slot in range(SLOTS):
        @pl.when(tab[ON, slot] == 1)
        def _():
            n_copy(slot).start()

        @pl.when(tab[ON, slot] != 1)
        def _():
            n_v[pl.ds(slot * rows, rows), :] = jnp.zeros((rows, 2 * size), BF16)
            dq_v[pl.ds(slot * rows, rows), :] = jnp.zeros((rows, ff), BF16)

    for side in range(2):
        for slot in range(SLOTS):
            @pl.when(tab[ON, slot] == 1)
            def _():
                dq_copy(side, slot).start()

    for slot in range(SLOTS):
        @pl.when(tab[ON, slot] == 1)
        def _():
            n_copy(slot).wait()

    turned = n_v[...].T
    for fixed in range(2):
        side = jnp.where(half == fixed, 1, 0)
        for chunk in range(chunks):
            first = fixed * size + chunk * height
            nt_v[chunk, pl.ds(pl.multiple_of(side * height, 16), height), :] = turned[first:first + height]

    piece = ff // count if aligned else 384
    copies = [pltpu.make_async_copy(made[i], outs[i], out_sems.at[i]) for i in range(2 * chunks)]
    for chunk in range(chunks):
        theirs_v, mine_v = made[2 * chunk:2 * chunk + 2]
        for side in range(2):
            if chunk == 0:
                for slot in range(SLOTS):
                    @pl.when(tab[ON, slot] == 1)
                    def _():
                        dq_copy(side, slot).wait()

            @pl.loop(side * (ff // piece // 4), (side + 1) * (ff // piece // 4))
            def _(pair):
                cols = pl.ds(pl.multiple_of(pair * 2 * piece, 128), 2 * piece)
                total = mm(nt_v[chunk], dq_v[:, cols]).astype(BF16)
                if not aligned:
                    theirs_v[:, cols] = total[:height]
                    mine_v[:, cols] = total[height:]
                    return
                for i in range(2):
                    place = pl.ds(pl.multiple_of(position((2 * pair + i) ^ me, orders[chunk]) * height, 16), height)
                    theirs_v[place, :] = total[:height, i * piece:(i + 1) * piece]
                    mine_v[place, :] = total[height:, i * piece:(i + 1) * piece]

        copies[2 * chunk].start()
        copies[2 * chunk + 1].start()

    for copy in copies:
        copy.wait()


def arranged(pieces, bits):
    count = pieces.shape[0]
    order = [0] * count
    for relative in range(count):
        order[position(relative, bits)] = relative
    return jnp.take(pieces, jnp.array(order) ^ lax.axis_index("dp"), axis=0)


def down_grad_call(chunks, count, orders, tab, f, z, rider, after):
    slots, rows, channels = f.shape
    width = z.shape[2] // 2 // chunks
    piece = channels // count
    aligned = piece % 16 == 0
    extra = rider.shape[1] if aligned else 0
    shapes = [(channels + (extra if i == 0 else 0), width) for i in range(chunks)]
    out = launch(
        functools.partial(down_grad_body, chunks, count, orders, aligned), [tab, f, z, rider], [IN_SMEM, IN_ANY, IN_ANY, IN_VMEM], after,
        out_shape=[jax.ShapeDtypeStruct(shapes[i // 2], BF16) for i in range(2 * chunks)],
        out_specs=[IN_ANY] * (2 * chunks),
        scratch_shapes=[pltpu.VMEM(shapes[i // 2], BF16) for i in range(2 * chunks)]
                       + [pltpu.VMEM((slots * rows, channels), BF16), pltpu.VMEM((channels, slots * rows), BF16),
                          pltpu.VMEM((2 * chunks, slots * rows, width), BF16),
                          pltpu.SemaphoreType.DMA((slots,)), pltpu.SemaphoreType.DMA((2 * chunks, slots)), pltpu.SemaphoreType.DMA((2 * chunks,))],
        compiler_params=pltpu.CompilerParams(vmem_limit_bytes=VMEM_BYTES),
        cost_estimate=lasting(9),
        name="down_grad",
    )
    if not aligned:
        out = [arranged(part.reshape(count, piece, width), orders[i // 2]).reshape(part.shape) for i, part in enumerate(out)]
    return [out[2 * i:2 * i + 2] for i in range(chunks)]


def up_grad_call(chunks, count, orders, tab, n, dq, after):
    slots, rows, channels = n.shape
    ff = dq.shape[2]
    height = channels // 2 // chunks
    piece = ff // count
    aligned = piece % 128 == 0
    shape = (count * height, piece) if aligned else (height, ff)
    out = launch(
        functools.partial(up_grad_body, chunks, height, count, orders, aligned), [tab, n, dq], [IN_SMEM, IN_ANY, IN_ANY], after,
        out_shape=[jax.ShapeDtypeStruct(shape, BF16)] * (2 * chunks),
        out_specs=[IN_ANY] * (2 * chunks),
        scratch_shapes=[pltpu.VMEM(shape, BF16)] * (2 * chunks)
                       + [pltpu.VMEM((slots * rows, channels), BF16), pltpu.VMEM((chunks, 2 * height, slots * rows), BF16),
                          pltpu.VMEM((slots * rows, ff), BF16),
                          pltpu.SemaphoreType.DMA((slots,)), pltpu.SemaphoreType.DMA((2, slots)), pltpu.SemaphoreType.DMA((2 * chunks,))],
        compiler_params=pltpu.CompilerParams(vmem_limit_bytes=VMEM_BYTES),
        cost_estimate=lasting(9),
        name="up_grad",
    )
    if not aligned:
        out = [arranged(jnp.swapaxes(part.reshape(height, count, piece), 0, 1), orders[i // 2]).reshape(count * height, piece) for i, part in enumerate(out)]
    return [out[2 * i:2 * i + 2] for i in range(chunks)]


def halved_body(mine, got, kept, sent):
    middle = kept.shape[0]
    low, high = pl.ds(0, middle), pl.ds(middle, middle)
    sent[...] = (mine[high, :].astype(F32) + got[high, :].astype(F32)).astype(BF16)
    kept[...] = (mine[low, :].astype(F32) + got[low, :].astype(F32)).astype(BF16)


def halved(mine, got, after):
    size, width = mine.shape
    return launch(halved_body, [mine, got], [IN_VMEM] * 2, after,
                  out_shape=[jax.ShapeDtypeStruct((size // 2, width), BF16)] * 2, out_specs=[IN_VMEM] * 2,
                  compiler_params=pltpu.CompilerParams(vmem_limit_bytes=VMEM_BYTES), cost_estimate=lasting(2), name="halved")


def summed_body(kind, mine, got, *refs):
    total = mine[...].astype(F32) + got[...].astype(F32)
    if kind == "above":
        first, out = refs
        out[0:first.shape[0]] = first[...]
        out[first.shape[0]:] = total
    elif kind == "beside":
        first, out = refs
        out[:, 0:first.shape[1]] = first[...]
        out[:, first.shape[1]:] = total
    else:
        out, *rest = refs
        out[...] = total[:out.shape[0]]
        for rider in rest:
            rider[...] = total[out.shape[0]:].astype(BF16)


def summed(kind, mine, got, size, first, after):
    rows, width = mine.shape
    shape = jax.ShapeDtypeStruct
    ins = [mine, got]
    if kind == "above":
        shapes = [shape((first.shape[0] + rows, width), F32)]
    elif kind == "beside":
        shapes = [shape((rows, first.shape[1] + width), F32)]
    else:
        shapes = [shape((size, width), F32)] + [shape((rows - size, width), BF16)] * (rows > size)
    if first is not None:
        ins.append(first)
    return launch(functools.partial(summed_body, kind), ins, [IN_VMEM] * len(ins), after,
                  out_shape=shapes, out_specs=[IN_VMEM] * len(shapes),
                  compiler_params=pltpu.CompilerParams(vmem_limit_bytes=VMEM_BYTES), cost_estimate=lasting(0.1), name="summed")


def packing(patches, hidden_t, channels, ff):
    spans = {}
    row = 0
    for name, height in (("token", -(-patches // 2 // 8) * 8), ("chan_up_bias", ff // 2 // channels), ("biases", 1), ("gain", 1), ("shift", 1)):
        spans[name] = row
        row += height
    return spans, -(-row // 128) * 128, channels


def pack_body(spans, patches, tab, da_i, db_i, vec_i, out, da_v, db_v, vec_v, both_v, sems):
    half = tab[PLACE, HALF]
    lanes = both_v.shape[-1]
    hidden_t = db_v.shape[2]
    upper = patches // 2
    sources = ((da_i, da_v), (db_i, db_v), (vec_i, vec_v))

    def copy(kind, slot):
        return pltpu.make_async_copy(sources[kind][0].at[slot], sources[kind][1].at[slot], sems.at[kind, slot])

    for slot in range(SLOTS):
        @pl.when(tab[ON, slot] == 1)
        def _():
            for kind in range(3):
                copy(kind, slot).start()

        @pl.when(tab[ON, slot] != 1)
        def _():
            for _, buffer in sources:
                buffer[slot] = jnp.zeros(buffer.shape[1:], F32)

    for slot in range(SLOTS):
        @pl.when(tab[ON, slot] == 1)
        def _():
            for kind in range(3):
                copy(kind, slot).wait()

    da = (da_v[0] + da_v[1]) + (da_v[2] + da_v[3])
    db = (db_v[0] + db_v[1]) + (db_v[2] + db_v[3])
    vec = (vec_v[0] + vec_v[1]) + (vec_v[2] + vec_v[3])
    both_v[...] = jnp.zeros_like(both_v)
    ff = vec.shape[1]
    channels = spans["channels"]
    for side in range(2):
        at = spans["token"]
        both_v[side, at:at + upper, 0:hidden_t] = da[side * upper:(side + 1) * upper]
        block = db[:, side * (hidden_t // 2):(side + 1) * (hidden_t // 2)]
        both_v[side, at:at + upper, hidden_t:hidden_t + hidden_t // 2] = block[:upper]
        both_v[side, at:at + upper, hidden_t + hidden_t // 2:2 * hidden_t] = block[upper:patches]

        def line(name, row, first, length, left=0):
            at = spans[name]
            for step in range(-(-length // lanes)):
                size = min(lanes, length - step * lanes)
                both_v[side, at + step:at + step + 1, left:left + size] = vec[row:row + 1, first + step * lanes:first + step * lanes + size]

        line("chan_up_bias", 0, side * (ff // 2), ff // 2)
        line("biases", 1, side * (channels // 2), channels // 2)
        line("biases", 6, side * (hidden_t // 2), hidden_t // 2, channels // 2)
        line("biases", 7, side * upper, upper, channels // 2 + hidden_t // 2)
        line("gain", 2 + side, 0, channels)
        line("shift", 4 + side, 0, channels)
    out[0] = both_v[1 - half].astype(BF16)
    out[1] = both_v[half].astype(BF16)


def unpack_body(spans, patches, hidden_t, relative, tab, parts, gain_o, shift_o, up_o, up_bias_o, down_o, down_bias_o, chan_up_bias_o, chan_down_bias_o, all_v):
    size = parts.shape[1]
    for i, shift in enumerate(relative):
        first = pl.multiple_of((tab[PLACE, ME] ^ shift) * size, 8) if len(relative) > 1 else 0
        all_v[pl.ds(first, size), :] = parts[i].astype(F32)
    upper = patches // 2
    lanes = all_v.shape[1]
    at = spans["token"]
    up_o[...] = all_v[at:at + upper, 0:hidden_t]
    block = all_v[at:at + -(-upper // 8) * 8, hidden_t:2 * hidden_t]
    down_o[:, 0:upper] = block[:, :hidden_t // 2].T[:, :upper]
    down_o[:, upper:patches] = block[:, hidden_t // 2:].T[:, :upper]
    gain_o[...] = all_v[spans["gain"]:spans["gain"] + 1, :]
    shift_o[...] = all_v[spans["shift"]:spans["shift"] + 1, :]
    for step in range(chan_up_bias_o.shape[1] // lanes):
        at = spans["chan_up_bias"] + step
        chan_up_bias_o[:, step * lanes:(step + 1) * lanes] = all_v[at:at + 1, :]
    row = all_v[spans["biases"]:spans["biases"] + 1, :]
    first = chan_down_bias_o.shape[1]
    chan_down_bias_o[...] = row[:, :first]
    up_bias_o[...] = row[:, first:first + hidden_t // 2]
    down_bias_o[...] = row[:, first + hidden_t // 2:first + hidden_t // 2 + upper]


def unpack(spans, patches, hidden_t, channels, ff, relative, tab, parts, after):
    sizes = [(1, channels), (1, channels), (patches // 2, hidden_t), (1, hidden_t // 2), (hidden_t // 2, patches), (1, patches // 2), (1, ff // 2), (1, channels // 2)]
    return launch(
        functools.partial(unpack_body, spans, patches, hidden_t, relative), [tab, parts], [IN_SMEM, IN_VMEM], after,
        out_shape=[jax.ShapeDtypeStruct(size, F32) for size in sizes],
        out_specs=[IN_VMEM] * len(sizes),
        scratch_shapes=[pltpu.VMEM((parts.shape[0] * parts.shape[1], parts.shape[2]), F32)],
        compiler_params=pltpu.CompilerParams(vmem_limit_bytes=VMEM_BYTES),
        cost_estimate=lasting(2),
        name="unpack",
    )


def both_body(first, second, out):
    out[0:first.shape[0]] = first[...]
    out[first.shape[0]:] = second[...]


def both(first, second, after):
    shape = (2 * first.shape[0],) + first.shape[1:]
    return launch(both_body, [first, second], [IN_VMEM] * 2, after, out_shape=jax.ShapeDtypeStruct(shape, first.dtype), out_specs=IN_VMEM,
                  compiler_params=pltpu.CompilerParams(vmem_limit_bytes=VMEM_BYTES), cost_estimate=lasting(2), name="both")


def split_body(both, first_o, second_o, sems):
    copies = [pltpu.make_async_copy(both.at[i], target, sems.at[i]) for i, target in enumerate((first_o, second_o))]
    for copy in copies:
        copy.start()
    for copy in copies:
        copy.wait()


def split(both, after):
    return launch(split_body, [both], [IN_ANY], after, out_shape=[jax.ShapeDtypeStruct(both.shape[1:], both.dtype)] * 2,
                  out_specs=[IN_VMEM] * 2, scratch_shapes=[pltpu.SemaphoreType.DMA((2,))],
                  compiler_params=pltpu.CompilerParams(vmem_limit_bytes=VMEM_BYTES), cost_estimate=lasting(0.1), name="split")


def place_body(tab, here, beside, across, corner, mixed_o, grad_o, mixed_v, grad_v, sems):
    layer = tab[PLACE, LAYER]
    half = tab[PLACE, HALF]
    sources = (here, beside, across, corner)
    places, width, patches = mixed_o.shape
    upper = mixed_v.shape[1]
    buffers = (mixed_v, grad_v)

    def copy(kind, place, source):
        return pltpu.make_async_copy(source.at[kind, place // 2], buffers[kind].at[tab[ORDER, place]], sems.at[kind, place])

    for place in range(places):
        for kind, row in enumerate((MIXED_FAR, GRAD_FAR)):
            which = jnp.where(tab[row, place] == layer, 0, 2) + jnp.where(half == place % 2, 0, 1)
            for i, source in enumerate(sources):
                @pl.when(which == i)
                def _():
                    copy(kind, place, source).start()

    for place in range(places):
        for kind in range(2):
            copy(kind, place, here).wait()

    @pl.loop(0, places)
    def _(i):
        for source, target in ((mixed_v, mixed_o), (grad_v, grad_o)):
            whole = jnp.concatenate([source[i, :, 0:width], source[i, :, width:2 * width]], 0)
            target[i] = whole.T[:, 0:patches]


def pack_call(spans, packed_rows, lanes, patches, channels, tab, da, db, vec, after):
    return launch(
        functools.partial(pack_body, dict(spans, channels=channels), patches), [tab, da, db, vec], [IN_SMEM] + [IN_ANY] * 3, after,
        out_shape=jax.ShapeDtypeStruct((2, packed_rows, lanes), BF16),
        out_specs=IN_VMEM,
        scratch_shapes=[pltpu.VMEM(da.shape, F32), pltpu.VMEM(db.shape, F32), pltpu.VMEM(vec.shape, F32),
                        pltpu.VMEM((2, packed_rows, lanes), F32), pltpu.SemaphoreType.DMA((3, SLOTS))],
        compiler_params=pltpu.CompilerParams(vmem_limit_bytes=VMEM_BYTES),
        cost_estimate=lasting(2.5),
        name="pack",
    )


def place_call(slot_count, patches, width, tab, slabs, after):
    out_shape = jax.ShapeDtypeStruct((slot_count, width, patches), BF16)
    buffer = pltpu.VMEM((slot_count,) + slabs[0].shape[2:], BF16)
    return launch(
        place_body, [tab] + list(slabs), [IN_SMEM] + [IN_ANY] * 4, after,
        out_shape=[out_shape, out_shape],
        out_specs=[IN_VMEM] * 2,
        scratch_shapes=[buffer, buffer, pltpu.SemaphoreType.DMA((2, slot_count))],
        compiler_params=pltpu.CompilerParams(vmem_limit_bytes=VMEM_BYTES),
        cost_estimate=lasting(4),
        name="place",
    )


def local(images, cotangent, valid_rows, skip_masks, norm_gain, norm_bias, token_up, token_up_bias, token_down,
          token_down_bias, chan_up, chan_up_bias, chan_down, chan_down_bias):
    count = lax.axis_size("dp")
    slot_count, patches, channels = images.shape
    rows = -(-patches // 16) * 16
    hidden_t = token_up.shape[1]
    ff = chan_up.shape[1]

    parcel_spans, height = parcel_rows(patches, hidden_t)
    own = parcel(parcel_spans, height, (token_up, token_down, token_up_bias, token_down_bias, chan_up_bias, chan_down_bias, norm_gain, norm_bias))
    got = flipped(own, "pipe", 1)
    got_up = flipped(chan_up, "pipe", 1)
    got_down = flipped(chan_down, "pipe", 1)

    tab, ticks = pl.pallas_call(
        table_body,
        out_shape=[jax.ShapeDtypeStruct((10, MOST), jnp.int32), jax.ShapeDtypeStruct((1,), jnp.int32)],
        in_specs=[IN_SMEM] * 4,
        out_specs=[IN_SMEM] * 2,
        cost_estimate=lasting(0.1),
        name="table",
    )(jnp.asarray(JOB_TABLE.reshape(-1, MOST)), jnp.asarray(TICK_TABLE[None, :]), valid_rows[None, :], skip_masks.T)

    weights = dict(prep(parcel_spans, patches, rows, hidden_t, ff, tab, own, got), own_up=chan_up, got_up=got_up, own_down=chan_down, got_down=got_down)
    blank = jnp.zeros((rows, channels), BF16)
    send, kept = tick_call(None, tab, images, cotangent, blank, weights, None)

    def one(tick, carried):
        send, recv, kept = carried
        arriving = flipped(send, "pipe", 2)
        send, kept = tick_call(tick, tab, images, cotangent, recv, weights, kept)
        return send, arriving, kept

    _, last, kept = lax.fori_loop(1, ticks[0], one, (send, blank, kept))
    kept = dict(zip(KEPT, kept))

    chunks = 2
    bits = tuple(range(count.bit_length() - 1))
    other_bits = (bits[1], bits[0]) + bits[2:]
    orders = (bits, other_bits, bits, other_bits)
    spans, packed_rows, lanes = packing(patches, hidden_t, channels, ff)

    made = []

    def step(function, *arrays):
        out = function(*arrays, after=tuple(made))
        made[:] = jax.tree.leaves(out)[:1]
        return out

    pieces = [None] * (2 * chunks)
    moving = [None] * (2 * chunks)

    def begin(which, pair):
        pieces[which] = pair[1]
        moving[which] = flipped(pair[0], "pipe", 1)

    def advance(which, stage):
        pieces[which], sent = step(halved, pieces[which], moving[which])
        moving[which] = flipped(sent, "dp", 1 << orders[which][stage])

    def finished(which, kind, first=None):
        size = channels // count if which < chunks else channels // 2 // chunks
        return step(summed, kind, pieces[which], moving[which], size, first)

    _, late_kept = step(tick_call, None, tab, images, cotangent, last, weights, tuple(kept[k] for k in KEPT))
    made[:] = late_kept[:1]
    kept = dict(zip(KEPT, late_kept))
    over = flipped(kept["slab23"], "pipe", 2)
    beside = flipped(kept["slab1"], "pipe", 1)
    rider = step(pack_call, spans, packed_rows, lanes, patches, channels, tab, kept["da"], kept["db"], kept["vec"])
    made.append(beside)
    for i, pair in enumerate(step(down_grad_call, chunks, count, orders[:chunks], tab, kept["f"], kept["z"], rider)):
        begin(i, pair)
    advance(0, 0)
    advance(1, 0)
    for i, pair in enumerate(step(up_grad_call, chunks, count, orders[chunks:], tab, kept["n2"], kept["dq"])):
        begin(chunks + i, pair)
    advance(0, 1)
    advance(1, 1)
    advance(2, 0)
    advance(3, 0)
    across, turned = step(split, over)
    corner = flipped(turned, "pipe", 1)
    for stage in range(2, len(bits)):
        advance(0, stage)
        advance(1, stage)
    advance(2, 1)
    width = channels // 4
    mixed, input_grad = step(place_call, slot_count, patches, width, tab, (kept["slab0"], beside, across, corner))
    advance(3, 1)
    down_first, *small = finished(0, "alone")
    parts = small[0][None] if small else None
    relative = [0]
    gathered = list(reversed(bits)) if small else []

    def gather():
        nonlocal parts, relative
        if gathered:
            bit = gathered.pop(0)
            parts = step(both, parts, flipped(parts, "dp", 1 << bit))
            relative += [i ^ (1 << bit) for i in relative]

    chan_down_grad, = finished(1, "beside", down_first)
    gather()
    for stage in range(2, len(bits)):
        advance(2, stage)
        advance(3, stage)
    while gathered:
        gather()
    if parts is None:
        total = rider[1].astype(F32) + flipped(rider[0], "pipe", 1).astype(F32)
        for bit in bits:
            sent = lax.optimization_barrier(total.astype(BF16))
            total = sent.astype(F32) + flipped(sent, "dp", 1 << bit).astype(F32)
        parts = total[None]
    gain, shift, token_up_grad, up_bias, token_down_grad, down_bias, chan_up_bias_grad, chan_down_bias_grad = step(
        unpack, spans, patches, hidden_t, channels, ff, relative, tab, parts)
    up_first, = finished(2, "alone")
    chan_up_grad, = finished(3, "above", up_first)

    return (
        jnp.swapaxes(mixed, 1, 2),
        jnp.swapaxes(input_grad, 1, 2),
        gain,
        shift,
        token_up_grad,
        up_bias[0],
        token_down_grad,
        down_bias[0],
        chan_up_grad,
        chan_up_bias_grad[0],
        chan_down_grad.T,
        chan_down_bias_grad[0],
    )


def solution(mesh):
    placed = (
        P("dp", None, None),
        P("dp", None, None),
        P("dp"),
        P("dp", None),
        P("pipe", None),
        P("pipe", None),
        P("pipe", None),
        P("pipe"),
        P("pipe", None),
        P("pipe"),
        P("pipe", None),
        P("pipe"),
        P("pipe", None),
        P("pipe"),
    )
    return jax.shard_map(
        local,
        mesh=mesh,
        in_specs=placed,
        out_specs=(
            P("dp", None, "pipe"),
            P("dp", None, "pipe"),
            P("pipe", None),
            P("pipe", None),
            P("pipe", None),
            P("pipe"),
            P("pipe", None),
            P("pipe"),
            P("pipe", "dp"),
            P("pipe"),
            P("pipe", "dp"),
            P("pipe"),
        ),
        check_vma=False,
    )
```
